32 devices in a mesh: dp: 8 (over z, core), tensor: 4 (over y, x).
Axes of the slice: x: 2, y: 2, z: 4, core: 2. Of those that a mesh axis runs over, the one named last changes fastest.
Arguments:
- tokens: bfloat16 [16, 128, 8, 512], P('dp', 'tensor'), may hold values from -6 to 6
- cotangent: bfloat16 [16, 128, 8, 512], P('dp', 'tensor'), may hold values from -6 to 6
- block_task: int32 [16], P('dp'), may hold values from 0 to 1, as said below
- sample_len: int32 [16], P('dp'), may hold values from 1 to 128, as said below
- feature_len: int32 [16], P('dp'), may hold values from 1 to 8, as said below
- norm_gain: float32 [2, 3, 512], replicated, may hold values from 0.5 to 1.5
- norm_shift: float32 [2, 3, 512], replicated, may hold values from -2 to 2
- sample_qkv: bfloat16 [2, 512, 3, 512], P(None, None, None, 'tensor'), may hold values from -0.25 to 0.25
- sample_out: bfloat16 [2, 512, 512], P(None, 'tensor'), may hold values from -0.75 to 0.75
- feature_qkv: bfloat16 [2, 512, 3, 512], P(None, None, None, 'tensor'), may hold values from -0.25 to 0.25
- feature_out: bfloat16 [2, 512, 512], P(None, 'tensor'), may hold values from -0.5 to 0.5
- out_bias: float32 [2, 3, 512], replicated, may hold values from -2 to 2
- up_weight: bfloat16 [2, 512, 2048], P(None, None, 'tensor'), may hold values from -0.25 to 0.25
- up_bias: float32 [2, 2048], replicated, may hold values from -2 to 2
- down_weight: bfloat16 [2, 2048, 512], P(None, 'tensor'), may hold values from -0.125 to 0.125
Outputs:
- output: bfloat16 [16, 128, 8, 512], P('dp', 'tensor')
- tokens_grad: float32 [16, 128, 8, 512], P('dp', 'tensor')
- norm_gain_grad: float32 [2, 3, 512], replicated
- norm_shift_grad: float32 [2, 3, 512], replicated
- sample_qkv_grad: float32 [2, 512, 3, 512], P(None, 'dp', None, 'tensor')
- sample_out_grad: float32 [2, 512, 512], P(None, 'tensor', 'dp')
- feature_qkv_grad: float32 [2, 512, 3, 512], P(None, 'dp', None, 'tensor')
- feature_out_grad: float32 [2, 512, 512], P(None, 'tensor', 'dp')
- out_bias_grad: float32 [2, 3, 512], replicated
- up_weight_grad: float32 [2, 512, 2048], P(None, 'dp', 'tensor')
- up_bias_grad: float32 [2, 2048], replicated
- down_weight_grad: float32 [2, 2048, 512], P(None, 'tensor', 'dp')
The draws below stay inside these ranges and needn't reach their ends.
Inputs may be any that keep to these rules, and one draw needn't show every extreme that they name: `block_task`: each data group is 2 consecutive blocks; within it tables are numbered from 0 in block order without gaps, and a table never leaves its group. `sample_len`: only a table's last block may be short, and a group's first block is always full. `feature_len`: equal for all blocks of one table.
All inputs are finite; a program needn't handle non-finite values.
Results may differ from the reference program's by a relative error of at most 0.029.
Values may be sent and summed in bfloat16 or wider, within the bound.
No kernel may reach another device: no remote copies, remote signals or barrier semaphores. Data moves between devices by JAX's collectives and lax.ppermute only.
A program may use at most 192 MiB of HBM per device.

```python
from functools import partial
import jax
import jax.numpy as jnp
from jax import lax

D = 512
H = 8
HD = 64
FF = 2048
L = 2
SB = 128
FEAT = 8
NBG = 2
BLOCKS = 16


def table_layout(key):
    group_count = BLOCKS // NBG
    column = jnp.broadcast_to(jnp.arange(NBG, dtype=jnp.int32)[None, :], (group_count, NBG))
    group_row = jnp.broadcast_to(jnp.arange(group_count, dtype=jnp.int32)[:, None], (group_count, NBG))
    flips = jax.random.randint(jax.random.fold_in(key, 11), (group_count, NBG), 0, 3)
    starts = jnp.where((column == 0) | (group_row == 0), 1, jnp.where(flips == 0, 1, 0)).astype(jnp.int32)
    tasks = jnp.cumsum(starts, axis=1) - 1
    following = jnp.concatenate([starts[:, 1:], jnp.ones((group_count, 1), jnp.int32)], axis=1)
    short_len = jax.random.randint(jax.random.fold_in(key, 12), (group_count, NBG), 1, SB + 1)
    samples = jnp.where((following == 1) & (column > 0), short_len, SB)
    width_draw = jax.random.randint(jax.random.fold_in(key, 13), (group_count, NBG), 1, FEAT + 1)
    width_draw = width_draw.at[0, 0].set(FEAT)
    first_block = lax.cummax(jnp.where(starts == 1, column, 0), axis=1)
    widths = jnp.take_along_axis(width_draw, first_block, axis=1)
    return (tasks.reshape(BLOCKS).astype(jnp.int32), samples.reshape(BLOCKS).astype(jnp.int32), widths.reshape(BLOCKS).astype(jnp.int32))


def draw_block_task(key, part):
    return table_layout(key)[0]


def draw_sample_len(key, part):
    return table_layout(key)[1]


def draw_feature_len(key, part):
    return table_layout(key)[2]


def level_of(key, shape, split, least, largest):
    factor_of = 1.0
    for dim, parts in split:
        draws = jax.random.uniform(jax.random.fold_in(jax.random.fold_in(key, 6), dim), (parts,), jnp.float32, least / len(split), largest / len(split))
        factor_of = factor_of * jnp.repeat(jnp.exp(draws), shape[dim] // parts).reshape((-1,) + (1,) * (len(shape) - 1 - dim))
    return factor_of


def bell_draw(own_key, extent, deviation, bound, pieces=(), kind=jnp.bfloat16):
    entries = jax.random.normal(own_key, extent, jnp.float32) * deviation
    if len(pieces) > 0:
        entries = level_of(own_key, extent, pieces, -0.22, 0.18) * entries
    return jnp.clip(entries, min=-bound, max=bound).astype(kind)


def setup_inputs(seed: int = 0) -> dict:
    key_list = jax.random.split(jax.random.key(seed), 16)
    return {
        "tokens": bell_draw(key_list[0], (BLOCKS, SB, FEAT, D), 1.0, 6.0, ((0, 8), (1, 4))),
        "cotangent": bell_draw(key_list[1], (BLOCKS, SB, FEAT, D), 1.0, 6.0, ((0, 8), (1, 4))),
        "block_task": draw_block_task(jax.random.fold_in(key_list[15], 71), 0),
        "sample_len": draw_sample_len(jax.random.fold_in(key_list[15], 71), 0),
        "feature_len": draw_feature_len(jax.random.fold_in(key_list[15], 71), 0),
        "norm_gain": jnp.clip(1.0 + 0.1 * jax.random.normal(key_list[5], (L, 3, D), jnp.float32), 0.5, 1.5),
        "norm_shift": bell_draw(key_list[6], (L, 3, D), 0.3, 2.0, (), jnp.float32),
        "sample_qkv": bell_draw(key_list[7], (L, D, 3, H * HD), D ** -0.5, 0.25, ((3, 4),)),
        "sample_out": bell_draw(key_list[8], (L, H * HD, D), HD ** -0.5, 0.75, ((1, 4),)),
        "feature_qkv": bell_draw(key_list[9], (L, D, 3, H * HD), D ** -0.5, 0.25, ((3, 4),)),
        "feature_out": bell_draw(key_list[10], (L, H * HD, D), (H * HD // 4) ** -0.5, 0.5, ((1, 4),)),
        "out_bias": bell_draw(key_list[11], (L, 3, D), 0.3, 2.0, (), jnp.float32),
        "up_weight": bell_draw(key_list[12], (L, D, FF), D ** -0.5, 0.25, ((2, 4),)),
        "up_bias": bell_draw(key_list[13], (L, FF), 0.3, 2.0, (), jnp.float32),
        "down_weight": bell_draw(key_list[14], (L, FF, D), FF ** -0.5, 0.125, ((1, 4),)),
    }


epsilon = 1e-05
masked_score = -1e+30
highest = lax.Precision.HIGHEST

@jax.custom_vjp
def low(v):
    return lax.optimization_barrier(v.astype(jnp.bfloat16)).astype(jnp.float32)

@jax.custom_vjp
def low_back(v):
    return v

def low_keep(v):
    return (low(v), None)

def low_pass(kept, grad):
    return (grad,)

def back_keep(v):
    return (v, None)

def back_low(kept, grad):
    return (low(grad),)
low.defvjp(low_keep, low_pass)
low_back.defvjp(back_keep, back_low)

def layer_norm(hidden_in, gain_row, shift_row):
    centre = hidden_in - lax.optimization_barrier(jnp.mean(hidden_in, axis=-1, keepdims=True))
    spread = lax.optimization_barrier(jnp.mean(centre * centre, axis=-1, keepdims=True))
    return centre * lax.rsqrt(spread + epsilon) * gain_row + shift_row

def softmax_masked(scores, key_mask):
    scores = jnp.where(key_mask, scores, masked_score)
    row_top = lax.optimization_barrier(jnp.max(scores, axis=-1, keepdims=True))
    totals = row_top + jnp.log(lax.optimization_barrier(jnp.sum(jnp.exp(scores - row_top), axis=-1, keepdims=True)))
    return jnp.exp(scores - totals)

def project_all(normed, weight, row_count):
    projected = jnp.einsum('bsfd,dcx->cbsfx', normed, weight, precision=highest)
    return low_back(low(projected)).reshape(3, row_count, FEAT, H, HD)

def sample_group(item, weight, out_weight, out_shift):
    normed, tasks, lengths = item
    row_count = normed.shape[0] * SB
    projected = project_all(normed, weight, row_count)
    query_all, key_all, value_all = (projected[0], projected[1], projected[2])
    scores = low_back(jnp.einsum('qfhe,kfhe->fhqk', query_all, key_all, precision=highest) * HD ** (-0.5))
    row_task = jnp.repeat(tasks, SB)
    row_live = (jnp.arange(SB)[None, :] < lengths[:, None]).reshape(row_count)
    key_mask = (row_task[:, None] == row_task[None, :]) & row_live[None, :]
    weights = low(softmax_masked(scores, key_mask))
    mixed = jnp.einsum('fhqk,kfhe->qfhe', weights, value_all, precision=highest)
    mixed = low_back(low(mixed.reshape(row_count, FEAT, H * HD)))
    branch = jnp.einsum('qfx,xd->qfd', mixed, out_weight, precision=highest) + out_shift
    return low_back(branch).reshape(normed.shape)

def feature_group(item, weight, out_weight, out_shift):
    normed, widths = item
    row_count = normed.shape[0] * SB
    projected = project_all(normed, weight, row_count)
    query_all, key_all, value_all = (projected[0], projected[1], projected[2])
    scores = low_back(jnp.einsum('qfhe,qghe->qhfg', query_all, key_all, precision=highest) * HD ** (-0.5))
    live = jnp.arange(FEAT)[None, :] < widths[:, None]
    key_mask = jnp.repeat(live, SB, axis=0)[:, None, None, :]
    weights = low(softmax_masked(scores, key_mask))
    mixed = jnp.einsum('qhfg,qghe->qfhe', weights, value_all, precision=highest)
    mixed = low_back(low(mixed.reshape(row_count, FEAT, H * HD)))
    branch = jnp.einsum('qfx,xd->qfd', mixed, out_weight, precision=highest) + out_shift
    return low_back(branch).reshape(normed.shape)

def feed_forward(normed, up_w, up_b, down_w, down_b):
    up_value = low_back(jnp.einsum('bsfd,dk->bsfk', normed, up_w, precision=highest) + up_b)
    hidden = low(jax.nn.gelu(up_value))
    return low_back(jnp.einsum('bsfk,kd->bsfd', hidden, down_w, precision=highest) + down_b)

def forward(tokens, norm_gain, norm_shift, sample_qkv, sample_out, feature_qkv, feature_out, out_bias, up_weight, up_bias, down_weight, block_task, sample_len, feature_len):
    groups = tokens.shape[0] // NBG
    grouped = (groups, NBG) + tokens.shape[1:]
    tasks = block_task.reshape(groups, NBG)
    lengths = sample_len.reshape(groups, NBG)
    widths = feature_len.reshape(groups, NBG)
    state = tokens
    for layer_at in range(L):
        normed = low(layer_norm(state, norm_gain[layer_at, 0], norm_shift[layer_at, 0])).reshape(grouped)
        sample_fn = jax.checkpoint(partial(sample_group, weight=sample_qkv[layer_at], out_weight=sample_out[layer_at], out_shift=out_bias[layer_at, 0]))
        state = state + lax.map(sample_fn, (normed, tasks, lengths)).reshape(tokens.shape)
        normed = low(layer_norm(state, norm_gain[layer_at, 1], norm_shift[layer_at, 1])).reshape(grouped)
        feature_fn = jax.checkpoint(partial(feature_group, weight=feature_qkv[layer_at], out_weight=feature_out[layer_at], out_shift=out_bias[layer_at, 1]))
        state = state + lax.map(feature_fn, (normed, widths)).reshape(tokens.shape)
        normed = low(layer_norm(state, norm_gain[layer_at, 2], norm_shift[layer_at, 2]))
        state = state + feed_forward(normed, up_weight[layer_at], up_bias[layer_at], down_weight[layer_at], out_bias[layer_at, 2])
    return state

def reference(tokens, cotangent, block_task, sample_len, feature_len, norm_gain, norm_shift, sample_qkv, sample_out, feature_qkv, feature_out, out_bias, up_weight, up_bias, down_weight):
    wide = jnp.float32

    def run(tokens_in, gain_in, shift_in, sq_in, so_in, fq_in, fo_in, bias_in, uw_in, ub_in, dw_in):
        return forward(tokens_in, gain_in, shift_in, sq_in, so_in, fq_in, fo_in, bias_in, uw_in, ub_in, dw_in, block_task, sample_len, feature_len)
    output, pull = jax.vjp(run, tokens.astype(wide), norm_gain.astype(wide), norm_shift.astype(wide), sample_qkv.astype(wide), sample_out.astype(wide), feature_qkv.astype(wide), feature_out.astype(wide), out_bias.astype(wide), up_weight.astype(wide), up_bias.astype(wide), down_weight.astype(wide))
    sample_live = jnp.arange(SB)[None, :] < sample_len[:, None]
    feature_live = jnp.arange(FEAT)[None, :] < feature_len[:, None]
    live = (sample_live[:, :, None] & feature_live[:, None, :]).astype(wide)
    grads = pull(cotangent.astype(wide) * live[..., None])
    return (output.astype(jnp.bfloat16), grads[0], grads[1], grads[2], grads[3], grads[4], grads[5], grads[6], grads[7], grads[8], grads[9], grads[10])
```

```python
import functools

import jax
import jax.numpy as jnp
from jax import lax
from jax.experimental import pallas as pl
from jax.experimental.pallas import tpu as pltpu
from jax.sharding import PartitionSpec as P

HD = 64
L = 2
PIECES = 4
PAIR = 2 * HD
QKV = 3 * PAIR
TILE = 128

epsilon = 1e-05
masked_score = -1e30
SCALE = HD ** (-0.5)
F32 = jnp.float32
BF = jnp.bfloat16
NT = (((1,), (1,)), ((), ()))
TN = (((0,), (0,)), ((), ()))
TANH_A = 0.7978845608028654
TANH_B = 0.044715
VMEM = pl.BlockSpec(memory_space=pltpu.VMEM)
SMEM = pl.BlockSpec(memory_space=pltpu.SMEM)
ANY = pl.BlockSpec(memory_space=pl.ANY)


class Sizes:
    def __init__(self, shape, tensor, dp):
        self.blocks, self.samples, self.feats, self.width = shape
        self.tensor, self.dp = tensor, dp
        self.rows = self.blocks * self.samples * self.feats
        self.own_feats = self.feats // tensor
        self.run = self.blocks * self.samples
        self.chunk = self.own_feats * self.run
        self.group = tensor * self.run
        self.block_rows = self.samples * self.feats
        self.fast = tensor == 4 and dp == 8


def places(z):
    tensor_at = lax.axis_index("tensor")
    dp_at = lax.axis_index("dp")
    return tensor_at, lax.rem(dp_at, 2), lax.div(dp_at, 2)


def dot(a, b):
    return jnp.dot(a, b, preferred_element_type=F32)


def dot_nt(a, b):
    return lax.dot_general(a, b, NT, preferred_element_type=F32)


def dot_tn(a, b):
    return lax.dot_general(a, b, TN, preferred_element_type=F32)


def normal_rows(x):
    centre = x - jnp.mean(x, axis=-1, keepdims=True)
    spread = jnp.mean(centre * centre, axis=-1, keepdims=True)
    rate = lax.rsqrt(spread + epsilon)
    return centre * rate, rate


def over_rows(rows, fn, carry=0, step=64):
    def one(at, kept):
        return fn(pl.ds(pl.multiple_of(at * step, step), step), kept)

    return lax.fori_loop(0, rows // step, one, carry)


def fold(x):
    return jnp.sum(x.reshape(-1, 8, x.shape[-1]), axis=0)


def total(x):
    return jnp.sum(x, axis=0, keepdims=True)


def put_strips(strips, rows, value):
    for lane in range(value.shape[1] // TILE):
        strips[lane, rows, :] = value[:, lane * TILE : (lane + 1) * TILE]


def get_strips(strips, rows):
    return jnp.concatenate([strips[lane, rows, :] for lane in range(strips.shape[0])], axis=1)


def feature_slot(sz, tensor_at, at, slot):
    return (tensor_at ^ at) * sz.own_feats + slot


def spread_out(sz, tensor_at, wide, chunks):
    for at in range(sz.tensor):
        for slot in range(sz.own_feats):
            first = feature_slot(sz, tensor_at, at, slot)
            for lane in range(sz.width // TILE):
                rows = wide[lane, pl.ds(first, sz.run, stride=sz.feats), :]
                chunks[at][
                    slot * sz.run : (slot + 1) * sz.run, lane * TILE : (lane + 1) * TILE
                ] = rows.astype(BF)


def bring_back(sz, tensor_at, chunks, wide):
    for at in range(sz.tensor):
        for slot in range(sz.own_feats):
            first = feature_slot(sz, tensor_at, at, slot)
            for lane in range(sz.width // TILE):
                rows = chunks[at][
                    slot * sz.run : (slot + 1) * sz.run, lane * TILE : (lane + 1) * TILE
                ]
                wide[lane, pl.ds(first, sz.run, stride=sz.feats), :] = rows.astype(F32)


def by_feature(sz, chunks, x):
    for at in range(sz.tensor):
        for slot in range(sz.own_feats):
            first = slot * sz.group + at * sz.run
            x[first : first + sz.run, :] = chunks[at][slot * sz.run : (slot + 1) * sz.run, :]


def to_chunks(sz, value, chunks):
    for at in range(sz.tensor):
        for slot in range(sz.own_feats):
            first = slot * sz.group + at * sz.run
            chunks[at][slot * sz.run : (slot + 1) * sz.run, :] = value[
                first : first + sz.run
            ].astype(BF)


def where_halves(core):
    other = 1 - core
    return (
        (1 + core, core),
        (2 - core, core),
        (3, core),
        (1 + other, other),
        (2 - other, other),
        (3, other),
    )


def load_unit(sz, parts, w, sems, core):
    copies = []
    if not sz.fast:
        copies.append(pltpu.make_async_copy(parts[0], w, sems.at[0]))
    else:
        copies.append(pltpu.make_async_copy(parts[0], w.at[0], sems.at[0]))
        half_rows = sz.width // 2
        for at, (piece, half) in enumerate(where_halves(core)):
            rows = pl.ds(pl.multiple_of(half * half_rows, half_rows), half_rows)
            copies.append(
                pltpu.make_async_copy(parts[at + 1], w.at[piece, rows, :], sems.at[at + 1])
            )
    for copy in copies:
        copy.start()
    return copies


def load_mlp(sz, layer_at, parts, up, down, sems, core):
    copies = []
    if not sz.fast:
        copies.append(pltpu.make_async_copy(parts[0], up, sems.at[0]))
        copies.append(pltpu.make_async_copy(parts[1], down, sems.at[1]))
    else:
        copies.append(pltpu.make_async_copy(parts[0].at[layer_at], up.at[0], sems.at[0]))
        copies.append(pltpu.make_async_copy(parts[1].at[layer_at], down.at[0], sems.at[1]))
        half_rows = sz.width // 2
        for at, (piece, half) in enumerate(where_halves(core)):
            rows = pl.ds(pl.multiple_of(half * half_rows, half_rows), half_rows)
            for member, w in enumerate((up, down)):
                copies.append(
                    pltpu.make_async_copy(
                        parts[at + 2].at[member],
                        w.at[piece, rows, :],
                        sems.at[2 + 2 * at + member],
                    )
                )
    for copy in copies:
        copy.start()
    return copies


def out_matrix(w, w_out):
    for piece in range(PIECES):
        for at in range(PIECES):
            w_out[piece * PAIR : (piece + 1) * PAIR, at * TILE : (at + 1) * TILE] = w[
                piece, at * TILE : (at + 1) * TILE, QKV:
            ]


def put_grad(sz, grads, outs, piece, member, core, z):
    if not sz.fast:
        outs[0][piece, member] = grads[...]
        return
    mine, theirs = outs
    if piece in (0, 3):
        at_mine = at_theirs = piece
    elif piece == 1:
        at_mine, at_theirs = 1 + core, 2 - core
    else:
        at_mine, at_theirs = 2 - core, 1 + core
    for near in range(4):
        first = (z ^ near) * 128
        rows_mine = pl.ds(pl.multiple_of(first + core * 64, 64), 64)
        rows_theirs = pl.ds(pl.multiple_of(first + (1 - core) * 64, 64), 64)
        mine[at_mine, near, member] = grads[rows_mine, :]
        theirs[at_theirs, near, member] = grads[rows_theirs, :]


def head_masks():
    lane = lax.broadcasted_iota(jnp.int32, (1, PAIR), 1)
    return lane < HD, lane >= HD


def sample_bias(sz, tensor_at, tasks, lengths, bias):
    def of(index):
        run_at = index // sz.run
        block = (index // sz.samples) % sz.blocks
        sample = (run_at ^ tensor_at) * sz.samples + index % sz.samples
        task = jnp.zeros_like(index)
        length = jnp.zeros_like(index)
        for at in range(sz.blocks):
            task = jnp.where(block == at, tasks[at], task)
            length = jnp.where(block == at, lengths[at], length)
        return task, sample < length

    row_task, unused = of(lax.broadcasted_iota(jnp.int32, (sz.group, 1), 0))
    key_task, key_live = of(lax.broadcasted_iota(jnp.int32, (1, sz.group), 1))
    key_task = jnp.where(key_live, key_task, -1)
    bias[...] = jnp.where(row_task == key_task, 0.0, masked_score)


def feature_bias(sz, length):
    row = lax.broadcasted_iota(jnp.int32, (TILE, TILE), 0)
    key = lax.broadcasted_iota(jnp.int32, (TILE, TILE), 1)
    same = (row // sz.feats) == (key // sz.feats)
    return jnp.where(same & (key % sz.feats < length), 0.0, masked_score)


def attend(proj, piece, rows, bias, probs, probs_at):
    first_head, second_head = head_masks()
    query = proj[piece, rows, :PAIR]
    key = proj[piece, rows, PAIR : 2 * PAIR]
    value = proj[piece, rows, 2 * PAIR :]
    mixed = []
    for head, mask in enumerate((first_head, second_head)):
        scores = dot_nt(jnp.where(mask, query, 0) * SCALE, key) + bias
        top = jnp.max(scores, axis=-1, keepdims=True)
        weights = jnp.exp(scores - top)
        weights = weights * (1.0 / jnp.sum(weights, axis=-1, keepdims=True))
        weights = weights.astype(BF)
        probs[probs_at + (head,)] = weights
        mixed.append(dot(weights, value))
    return jnp.where(first_head, mixed[0], mixed[1]).astype(BF)


def attend_back(proj, piece, rows, probs, probs_at, mixed_grad, proj_grad):
    first_head, second_head = head_masks()
    query = proj[piece, rows, :PAIR]
    key = proj[piece, rows, PAIR : 2 * PAIR]
    value = proj[piece, rows, 2 * PAIR :]
    query_grad, key_grad, value_grad = [], [], []
    for head, mask in enumerate((first_head, second_head)):
        weights = probs[probs_at + (head,)]
        head_grad = jnp.where(mask, mixed_grad, 0)
        weight_grad = dot_nt(head_grad, value)
        wide = weights.astype(F32)
        product = wide * weight_grad
        score_grad = product - wide * jnp.sum(product, axis=-1, keepdims=True)
        score_low = score_grad.astype(BF)
        value_grad.append(dot_tn(weights, head_grad))
        query_grad.append(dot(score_low, key))
        key_grad.append(dot_tn(score_low, jnp.where(mask, query, 0)))
    queries = jnp.where(first_head, query_grad[0], query_grad[1]) * SCALE
    proj_grad[piece, rows, :PAIR] = queries.astype(BF)
    proj_grad[piece, rows, PAIR : 2 * PAIR] = ((key_grad[0] + key_grad[1]) * SCALE).astype(BF)
    proj_grad[piece, rows, 2 * PAIR :] = (value_grad[0] + value_grad[1]).astype(BF)


def norm_back_rows(state, incoming, gain):
    xhat, rate = normal_rows(state)
    inner = incoming * gain
    back = rate * (
        inner
        - jnp.mean(inner, axis=-1, keepdims=True)
        - xhat * jnp.mean(inner * xhat, axis=-1, keepdims=True)
    )
    return xhat, back


def first_norm_kernel(sz, tokens, gains, shifts, *rest):
    chunks, (wide,) = rest[: sz.tensor], rest[sz.tensor :]
    tensor_at, core, z = places(sz)

    def rows_of(rows, kept):
        xhat, unused = normal_rows(tokens[rows, :].astype(F32))
        put_strips(wide, rows, xhat * gains[0, 0:1, :] + shifts[0, 0:1, :])
        return kept

    over_rows(sz.rows, rows_of)
    spread_out(sz, tensor_at, wide, chunks)


def pack_kernel(sz, units, with_mlp, *rest):
    sems = rest[-1]
    at = 2 * len(units)
    outs = rest[at + (2 if with_mlp else 0) : -1]
    tensor_at, core, z = places(sz)
    half = sz.width // 2
    started = []

    def go(source, target):
        copy = pltpu.make_async_copy(source, target, sems.at[len(started)])
        copy.start()
        started.append(copy)

    half_rows = pl.ds(pl.multiple_of(core * half, half), half)
    for unit, layer_at in enumerate(units):
        qkv, out = rest[2 * unit], rest[2 * unit + 1]
        own, sent = outs[2 * unit], outs[2 * unit + 1]
        for member in range(3):
            lanes = pl.ds(member * PAIR, PAIR)
            go(qkv.at[layer_at, member], own.at[:, lanes])
            go(qkv.at[layer_at, member, half_rows, :], sent.at[:, lanes])
        for block in range(PIECES):
            go(
                out.at[layer_at, :, pl.ds(block * TILE, TILE)],
                own.at[pl.ds(block * TILE, TILE), pl.ds(QKV, PAIR)],
            )
        for block in range(PIECES // 2):
            lanes = pl.ds(pl.multiple_of(core * half + block * TILE, TILE), TILE)
            go(
                out.at[layer_at, :, lanes],
                sent.at[pl.ds(block * TILE, TILE), pl.ds(QKV, PAIR)],
            )
    if with_mlp:
        up, down = rest[at], rest[at + 1]
        for layer_at in range(L):
            for member, w in enumerate((up, down)):
                go(w.at[layer_at, half_rows, :], outs[2 * len(units) + layer_at].at[member])
    for copy in started:
        copy.wait()


def sample_kernel(sz, tasks, lengths, *rest):
    n = sz.tensor
    parts = 7 if sz.fast else 1
    chunks, weights = rest[:n], rest[n : n + parts]
    outs = rest[n + parts :]
    back, proj, mixed, probs = outs[:n], outs[n], outs[n + 1], outs[n + 2]
    x, w, w_out, bias, sems = outs[n + 3 :]
    tensor_at, core, z = places(sz)
    copies = load_unit(sz, weights, w, sems, core)
    by_feature(sz, chunks, x)
    sample_bias(sz, tensor_at, tasks, lengths, bias)
    for copy in copies:
        copy.wait()
    out_matrix(w, w_out)
    for piece in range(PIECES):
        proj[piece] = dot(x[...], w[piece, :, :QKV]).astype(BF)
        for slot in range(sz.own_feats):
            rows = slice(slot * sz.group, (slot + 1) * sz.group)
            mixed[rows, piece * PAIR : (piece + 1) * PAIR] = attend(
                proj, piece, rows, bias[...], probs, (piece, slot)
            )
    to_chunks(sz, dot(mixed[...], w_out[...]), back)


def feature_kernel(sz, layer_at, lengths, state, gains, shifts, out_bias, *rest):
    n = sz.tensor
    parts = 7 if sz.fast else 1
    chunks, weights = rest[:n], rest[n : n + parts]
    state_1, state_2, normed_m, proj, mixed, probs = rest[n + parts : n + parts + 6]
    strips, wide, normed, w, w_out, sems = rest[n + parts + 6 :]
    tensor_at, core, z = places(sz)
    copies = load_unit(sz, weights, w, sems, core)
    bring_back(sz, tensor_at, chunks, strips)
    at = slice(layer_at, layer_at + 1)

    def before(rows, kept):
        value = state[rows, :].astype(F32) + get_strips(strips, rows) + out_bias[0, at, :]
        state_1[rows, :] = value
        xhat, unused = normal_rows(value)
        normed[rows, :] = (xhat * gains[1, at, :] + shifts[1, at, :]).astype(BF)
        return kept

    over_rows(sz.rows, before)
    biases = [feature_bias(sz, lengths[block]) for block in range(sz.blocks)]
    for copy in copies:
        copy.wait()
    out_matrix(w, w_out)
    for piece in range(PIECES):
        proj[piece] = dot(normed[...], w[piece, :, :QKV]).astype(BF)
        for tile in range(sz.rows // TILE):
            rows = slice(tile * TILE, (tile + 1) * TILE)
            mixed[rows, piece * PAIR : (piece + 1) * PAIR] = attend(
                proj, piece, rows, biases[tile * TILE // sz.block_rows], probs, (piece, tile)
            )
    wide[...] = dot(mixed[...], w_out[...])

    def after(rows, kept):
        value = state_1[rows, :] + wide[rows, :] + out_bias[1, at, :]
        state_2[rows, :] = value
        xhat, unused = normal_rows(value)
        normed_m[rows, :] = (xhat * gains[2, at, :] + shifts[2, at, :]).astype(BF)
        return kept

    over_rows(sz.rows, after)


def up_bias_rows(sz, tensor_at, piece):
    return (tensor_at ^ piece) if sz.fast else piece


def mlp_kernel(sz, layer_at, state_2, normed_m, up_bias, gains, shifts, out_bias, *rest):
    n = sz.tensor
    parts = 8 if sz.fast else 2
    weights, (state_3, *chunks) = rest[:parts], rest[parts : parts + 1 + n]
    strips, wide, up, down, sems = rest[parts + 1 + n :]
    tensor_at, core, z = places(sz)
    for copy in load_mlp(sz, layer_at, weights, up, down, sems, core):
        copy.wait()
    for piece in range(PIECES):
        shift = up_bias[layer_at, pl.ds(up_bias_rows(sz, tensor_at, piece), 1), :]
        value = dot(normed_m[...], up[piece]) + shift
        hidden = 0.5 * value * (1.0 + jnp.tanh(TANH_A * (value + TANH_B * value * value * value)))
        term = dot(hidden.astype(BF), down[piece])
        wide[...] = term if piece == 0 else wide[...] + term
    at = slice(layer_at, layer_at + 1)
    later = slice(layer_at + 1, layer_at + 2)

    def after(rows, kept):
        value = state_2[rows, :] + wide[rows, :] + out_bias[2, at, :]
        state_3[rows, :] = value
        xhat, unused = normal_rows(value)
        put_strips(strips, rows, xhat * gains[0, later, :] + shifts[0, later, :])
        return kept

    over_rows(sz.rows, after)
    spread_out(sz, tensor_at, strips, chunks)


def mlp_back(
    sz, layer_at, grad, state_2, normed_m, up_bias, gains, up, down, low, wide, wide_out, grads,
    grad_out, outs, small,
):
    tensor_at, core, z = places(sz)
    at = slice(layer_at, layer_at + 1)

    def lower(rows, kept):
        part = grad[rows, :].astype(BF)
        low[rows, :] = part
        return kept + fold(part.astype(F32))

    small[...] = jnp.zeros_like(small)
    small[2:3, :] = total(over_rows(sz.rows, lower, jnp.zeros((8, sz.width), F32)))
    for piece in range(PIECES):
        name = up_bias_rows(sz, tensor_at, piece)
        value = dot(normed_m[...], up[piece]) + up_bias[layer_at, pl.ds(name, 1), :]
        square = value * value
        bend = jnp.tanh(TANH_A * (value + TANH_B * square * value))
        hidden = (0.5 * value * (1.0 + bend)).astype(BF)
        slope = 0.5 * (1.0 + bend) + 0.5 * value * (1.0 - bend * bend) * (
            TANH_A * (1.0 + 3.0 * TANH_B * square)
        )
        if wide_out is not None:
            term = dot(hidden, down[piece])
            wide_out[...] = term if piece == 0 else wide_out[...] + term
        up_grad = (dot_nt(low[...], down[piece]) * slope).astype(BF)
        small[pl.ds(3 + name, 1), :] = total(fold(up_grad.astype(F32)))
        term = dot_nt(up_grad, up[piece])
        wide[...] = term if piece == 0 else wide[...] + term
        grads[...] = dot_tn(normed_m[...], up_grad).astype(BF)
        put_grad(sz, grads, outs, piece, 0, core, z)
        grads[...] = dot_tn(low[...], hidden).astype(BF)
        put_grad(sz, grads, outs, piece, 1, core, z)

    def back(rows, kept):
        incoming = wide[rows, :]
        xhat, change = norm_back_rows(state_2[rows, :], incoming, gains[2, at, :])
        grad_out[rows, :] = grad[rows, :] + change
        return kept[0] + fold(incoming * xhat), kept[1] + fold(incoming)

    nothing = jnp.zeros((8, sz.width), F32)
    gain_sum, shift_sum = over_rows(sz.rows, back, (nothing, nothing))
    small[0:1, :] = total(gain_sum)
    small[1:2, :] = total(shift_sum)


def last_mlp_kernel(
    sz, layer_at, sample_lens, feature_lens, cotangent, state_2, normed_m, up_bias, gains, out_bias,
    *rest,
):
    parts = 8 if sz.fast else 2
    halves = 2 if sz.fast else 1
    weights, rest = rest[:parts], rest[parts:]
    output, grad_out, small = rest[:3]
    outs = rest[3 : 3 + halves]
    grad, wide, wide_out, low, grads, up, down, sems = rest[3 + halves :]
    tensor_at, core, z = places(sz)
    copies = load_mlp(sz, layer_at, weights, up, down, sems, core)
    step = 64

    def live_rows(rows, kept):
        index = kept + lax.broadcasted_iota(jnp.int32, (step, 1), 0)
        block = index // sz.block_rows
        sample = tensor_at * sz.samples + (index // sz.feats) % sz.samples
        sample_len = jnp.zeros_like(index)
        feature_len = jnp.zeros_like(index)
        for at in range(sz.blocks):
            sample_len = jnp.where(block == at, sample_lens[at], sample_len)
            feature_len = jnp.where(block == at, feature_lens[at], feature_len)
        live = (sample < sample_len) & (index % sz.feats < feature_len)
        grad[rows, :] = jnp.where(live, cotangent[rows, :].astype(F32), 0.0)
        return kept + step

    over_rows(sz.rows, live_rows, 0, step)
    for copy in copies:
        copy.wait()
    mlp_back(
        sz, layer_at, grad, state_2, normed_m, up_bias, gains, up, down, low, wide, wide_out,
        grads, grad_out, outs, small,
    )
    at = slice(layer_at, layer_at + 1)

    def after(rows, kept):
        value = state_2[rows, :] + wide_out[rows, :] + out_bias[2, at, :]
        output[rows, :] = value.astype(BF)
        return kept

    over_rows(sz.rows, after)


def mlp_back_kernel(
    sz, layer_at, grad_in, state_3, state_2, normed_m, up_bias, gains, *rest
):
    n = sz.tensor
    parts = 8 if sz.fast else 2
    halves = 2 if sz.fast else 1
    chunks, weights, rest = rest[:n], rest[n : n + parts], rest[n + parts :]
    grad_out, small, small_s = rest[:3]
    outs = rest[3 : 3 + halves]
    grad, strips, wide, low, grads, up, down, sems = rest[3 + halves :]
    tensor_at, core, z = places(sz)
    copies = load_mlp(sz, layer_at, weights, up, down, sems, core)
    sample_norm_back(
        sz, layer_at + 1, tensor_at, grad_in, state_3, chunks, gains, strips, grad, small_s
    )
    for copy in copies:
        copy.wait()
    mlp_back(
        sz, layer_at, grad, state_2, normed_m, up_bias, gains, up, down, low, wide, None,
        grads, grad_out, outs, small,
    )


def sample_norm_back(sz, layer_at, tensor_at, grad_in, state, chunks, gains, strips, grad, small):
    bring_back(sz, tensor_at, chunks, strips)
    at = slice(layer_at, layer_at + 1)

    def back(rows, kept):
        incoming = get_strips(strips, rows)
        xhat, change = norm_back_rows(state[rows, :].astype(F32), incoming, gains[0, at, :])
        grad[rows, :] = grad_in[rows, :] + change
        return kept[0] + fold(incoming * xhat), kept[1] + fold(incoming)

    nothing = jnp.zeros((8, sz.width), F32)
    gain_sum, shift_sum = over_rows(sz.rows, back, (nothing, nothing))
    small[...] = jnp.zeros_like(small)
    small[0:1, :] = total(gain_sum)
    small[1:2, :] = total(shift_sum)


def last_norm_kernel(sz, grad_in, state, gains, *rest):
    chunks, (grad, small, strips) = rest[: sz.tensor], rest[sz.tensor :]
    tensor_at, core, z = places(sz)
    sample_norm_back(sz, 0, tensor_at, grad_in, state, chunks, gains, strips, grad, small)


def feature_back_kernel(sz, layer_at, grad, state_1, proj, probs, gains, shifts, *rest):
    n = sz.tensor
    parts = 7 if sz.fast else 1
    weights, rest = rest[:parts], rest[parts:]
    grad_out, low, proj_grad, normed, small = rest[:5]
    chunks = rest[5 : 5 + n]
    mixed_grad, strips, wide, w, w_out, sems = rest[5 + n :]
    tensor_at, core, z = places(sz)
    copies = load_unit(sz, weights, w, sems, core)
    at = slice(layer_at, layer_at + 1)
    nothing = jnp.zeros((8, sz.width), F32)

    def lower(rows, kept):
        part = grad[rows, :].astype(BF)
        low[rows, :] = part
        return kept + fold(part.astype(F32))

    small[...] = jnp.zeros_like(small)
    small[2:3, :] = total(over_rows(sz.rows, lower, nothing))
    for copy in copies:
        copy.wait()
    out_matrix(w, w_out)
    mixed_grad[...] = dot_nt(low[...], w_out[...]).astype(BF)
    for piece in range(PIECES):
        for tile in range(sz.rows // TILE):
            rows = slice(tile * TILE, (tile + 1) * TILE)
            part = mixed_grad[rows, piece * PAIR : (piece + 1) * PAIR]
            attend_back(proj, piece, rows, probs, (piece, tile), part, proj_grad)
        term = dot_nt(proj_grad[piece], w[piece, :, :QKV])
        wide[...] = term if piece == 0 else wide[...] + term

    def back(rows, kept):
        incoming = wide[rows, :]
        gain = gains[1, at, :]
        xhat, change = norm_back_rows(state_1[rows, :], incoming, gain)
        value = grad[rows, :] + change
        grad_out[rows, :] = value
        put_strips(strips, rows, value)
        normed[rows, :] = (xhat * gain + shifts[1, at, :]).astype(BF)
        rounded = value.astype(BF).astype(F32)
        return (
            kept[0] + fold(incoming * xhat),
            kept[1] + fold(incoming),
            kept[2] + fold(rounded),
        )

    sums = over_rows(sz.rows, back, (nothing, nothing, nothing))
    small[0:1, :] = total(sums[0])
    small[1:2, :] = total(sums[1])
    small[3:4, :] = total(sums[2])
    spread_out(sz, tensor_at, strips, chunks)


def sample_back_kernel(sz, proj, probs, *rest):
    n = sz.tensor
    parts = 7 if sz.fast else 1
    chunks, weights, rest = rest[:n], rest[n : n + parts], rest[n + parts :]
    back, low, proj_grad = rest[:n], rest[n], rest[n + 1]
    mixed_grad, wide, w, w_out, sems = rest[n + 2 :]
    tensor_at, core, z = places(sz)
    copies = load_unit(sz, weights, w, sems, core)
    by_feature(sz, chunks, low)
    for copy in copies:
        copy.wait()
    out_matrix(w, w_out)
    mixed_grad[...] = dot_nt(low[...], w_out[...]).astype(BF)
    for piece in range(PIECES):
        for slot in range(sz.own_feats):
            rows = slice(slot * sz.group, (slot + 1) * sz.group)
            part = mixed_grad[rows, piece * PAIR : (piece + 1) * PAIR]
            attend_back(proj, piece, rows, probs, (piece, slot), part, proj_grad)
        term = dot_nt(proj_grad[piece], w[piece, :, :QKV])
        wide[...] = term if piece == 0 else wide[...] + term
    to_chunks(sz, wide[...], back)


def matrix_grad_kernel(sz, count, proj_grad, low, mixed, *rest):
    halves = 2 if sz.fast else 1
    rows, outs, rest = rest[:count], rest[count : count + halves], rest[count + halves :]
    tensor_at, core, z = places(sz)
    if count == 1:
        (grads,) = rest
        (normed,) = rows
    else:
        grads, normed = rest
        by_feature(sz, rows, normed)
    for piece in range(PIECES):
        grads[:, :QKV] = dot_tn(normed[...], proj_grad[piece]).astype(BF)
        grads[:, QKV:] = dot_tn(low[...], mixed[:, piece * PAIR : (piece + 1) * PAIR]).astype(BF)
        put_grad(sz, grads, outs, piece, 0, core, z)


def shaped(shape, dtype):
    return jax.ShapeDtypeStruct(shape, dtype)


def launch(kernel, name, operands, specs, outs, scratch, mflops, out_spec=VMEM):
    return pl.pallas_call(
        kernel,
        out_shape=outs,
        in_specs=specs,
        out_specs=[out_spec] * len(outs),
        scratch_shapes=scratch,
        name=name,
        cost_estimate=pl.CostEstimate(
            flops=int(mflops * 1e6), bytes_accessed=8_000_000, transcendentals=0
        ),
        compiler_params=pltpu.CompilerParams(vmem_limit_bytes=52 * 2**20),
    )(*operands)


def unit_scratch(sz):
    return [
        pltpu.VMEM((PIECES, sz.width, sz.width), BF),
        pltpu.VMEM((sz.width, sz.width), BF),
    ]


def grad_shapes(sz, members):
    if sz.fast:
        return [shaped((PIECES, 4, members, 64, sz.width), BF)] * 2
    return [shaped((PIECES, members, sz.width, sz.width), BF)]


def swap_cores(sz, v):
    return lax.ppermute(v, "dp", [(at, at ^ 1) for at in range(sz.dp)])


def swap_near(sz, v, distance):
    return lax.ppermute(v, "tensor", [(at, at ^ distance) for at in range(sz.tensor)])


def swap_far(sz, v, distance):
    return lax.ppermute(v, "dp", [(at, at ^ (2 * distance)) for at in range(sz.dp)])


def swap_turn(sz, v, turn):
    pairs = []
    for dp_at in range(sz.dp):
        distance = 1 + ((dp_at + turn) % 2)
        for at in range(sz.tensor):
            base = dp_at * sz.tensor
            pairs.append((base + at, base + (at ^ distance)))
    return lax.ppermute(v, ("dp", "tensor"), pairs)


def exchange(sz, chunks):
    return [chunks[0]] + [swap_near(sz, chunks[at], at) for at in range(1, sz.tensor)]


def gather_unit(sz, half):
    first = swap_turn(sz, half, 0)
    second = swap_turn(sz, half, 1)
    third = swap_turn(sz, first, 1)
    got = [first, second, third]
    return got + [swap_cores(sz, v) for v in got]


def reduce_near(sz, mine, theirs):
    other = swap_cores(sz, theirs)

    def add(*terms):
        out = terms[0].astype(F32)
        for term in terms[1:]:
            out = out + term.astype(F32)
        return out

    second = swap_turn(sz, add(mine[2:], other[2:]).astype(BF), 1)
    first = swap_turn(sz, add(mine[1], other[1], second[1]).astype(BF), 0)
    return add(mine[0], other[0], second[0], first)


def reduce_far(sz, sums):
    got = swap_far(sz, sums[2:].astype(BF), 2)
    sums = sums[:2] + got.astype(F32)
    got = swap_far(sz, sums[1].astype(BF), 1)
    return sums[0] + got.astype(F32)


def reduce_whole(sz, full):
    members, width = full.shape[1], full.shape[2]
    full = full.transpose(1, 2, 0, 3)
    part = lax.psum_scatter(full, "dp", scatter_dimension=1, tiled=True)
    return lax.psum(part, "tensor").astype(F32)


def small_sum(sz, small):
    if not sz.fast:
        return lax.psum(small, ("dp", "tensor"))
    small = small + swap_cores(sz, small)
    small = small + swap_near(sz, small, 1)
    small = small + swap_near(sz, small, 2)
    small = small + swap_far(sz, small, 1)
    return small + swap_far(sz, small, 2)


def gathered_unit(qkv, out):
    qkv = lax.all_gather(qkv, "tensor", axis=2, tiled=True)
    out = lax.all_gather(out, "tensor", axis=0, tiled=True)
    width = qkv.shape[1]
    left = qkv.reshape(3, width, PIECES, PAIR).transpose(2, 1, 0, 3).reshape(PIECES, width, QKV)
    right = out.reshape(PIECES, PAIR, PIECES, TILE).transpose(0, 2, 1, 3)
    return jnp.concatenate([left, right.reshape(PIECES, width, PAIR)], axis=2)


def body(
    tokens,
    cotangent,
    block_task,
    sample_len,
    feature_len,
    norm_gain,
    norm_shift,
    sample_qkv,
    sample_out,
    feature_qkv,
    feature_out,
    out_bias,
    up_weight,
    up_bias,
    down_weight,
):
    shape = tokens.shape
    sz = Sizes(shape, lax.axis_size("tensor"), lax.axis_size("dp"))
    rows, width, n = sz.rows, sz.width, sz.tensor
    tokens = tokens.reshape(rows, width)
    cotangent = cotangent.reshape(rows, width)
    gains, shifts, biases = (
        jnp.transpose(v, (1, 0, 2)) for v in (norm_gain, norm_shift, out_bias)
    )
    up_rows = up_bias.reshape(L, PIECES, -1)
    qkvs = [jnp.transpose(v, (0, 2, 1, 3)) for v in (sample_qkv, feature_qkv)]
    outs = [sample_out, feature_out]
    part = functools.partial
    wide = pltpu.VMEM((rows, width), F32)
    strips = pltpu.VMEM((width // TILE, rows, TILE), F32)
    slim = pltpu.VMEM((rows, width), BF)
    dma = pltpu.SemaphoreType.DMA
    row_f32 = shaped((rows, width), F32)
    row_bf = shaped((rows, width), BF)
    chunk_shapes = [shaped((sz.chunk, width), BF)] * n
    proj_shape = shaped((PIECES, rows, QKV), BF)
    small_shape = shaped((8, width), F32)

    chunks = launch(
        part(first_norm_kernel, sz), "first_norm", (tokens, gains, shifts), [VMEM] * 3,
        chunk_shapes, [strips], 1,
    )

    units = [[None, None] for _ in range(L)]
    mlps = [None] * L
    if sz.fast:
        pair = [shaped((width, width), BF), shaped((width // 2, width), BF)]
        half_mlp = shaped((2, width // 2, width), BF)
        own, sent = launch(
            part(pack_kernel, sz, (0,), False), "pack_first", (qkvs[0], outs[0]), [ANY] * 2,
            pair, [dma((12,))], 1, ANY,
        )
        units[0][0] = [own] + gather_unit(sz, sent)
        rest = [(0, 1)] + [(layer_at, kind) for layer_at in range(1, L) for kind in range(2)]
        operands = []
        for layer_at, kind in rest:
            operands += [qkvs[kind], outs[kind]]
        packed = launch(
            part(pack_kernel, sz, tuple(layer_at for layer_at, _ in rest), True), "pack_rest",
            (*operands, up_weight, down_weight), [ANY] * (len(operands) + 2),
            pair * len(rest) + [half_mlp] * L, [dma((12 * len(rest) + 2 * L,))], 1, ANY,
        )
        by_unit = {key: packed[2 * at : 2 * at + 2] for at, key in enumerate(rest)}
        for layer_at in range(L):
            for kind in range(2):
                if units[layer_at][kind] is None:
                    own, sent = by_unit[layer_at, kind]
                    units[layer_at][kind] = [own] + gather_unit(sz, sent)
            halves = gather_unit(sz, packed[2 * len(rest) + layer_at])
            mlps[layer_at] = [up_weight, down_weight] + halves
    else:
        for layer_at in range(L):
            for kind in range(2):
                units[layer_at][kind] = [
                    gathered_unit(qkvs[kind][layer_at], outs[kind][layer_at])
                ]
            up = lax.all_gather(up_weight[layer_at], "tensor", axis=1, tiled=True)
            down = lax.all_gather(down_weight[layer_at], "tensor", axis=0, tiled=True)
            up = up.reshape(width, PIECES, width).transpose(1, 0, 2)
            mlps[layer_at] = [up, down.reshape(PIECES, width, width)]
    unit_specs = [ANY] * len(units[0][0])
    mlp_specs = [ANY] * len(mlps[0])
    unit_sems, mlp_sems = dma((len(unit_specs),)), dma((2 * len(mlp_specs) - 2,))
    mlp_scratch = [pltpu.VMEM((PIECES, width, width), BF)] * 2

    state = tokens
    kept = []
    for layer_at in range(L):
        entry = state
        got = exchange(sz, chunks)
        slots = sz.own_feats
        *back, proj_s, mixed_s, probs_s = launch(
            part(sample_kernel, sz), f"sample_{layer_at}",
            (block_task, sample_len, *got, *units[layer_at][0]),
            [SMEM] * 2 + [VMEM] * n + unit_specs,
            chunk_shapes
            + [proj_shape, row_bf, shaped((PIECES, slots, 2, sz.group, sz.group), BF)],
            [slim, *unit_scratch(sz), pltpu.VMEM((sz.group, sz.group), F32), unit_sems],
            3000,
        )
        back = exchange(sz, back)
        tiles = rows // TILE
        state_1, state_2, normed_m, proj_f, mixed_f, probs_f = launch(
            part(feature_kernel, sz, layer_at), f"feature_{layer_at}",
            (feature_len, state, gains, shifts, biases, *back, *units[layer_at][1]),
            [SMEM] + [VMEM] * (4 + n) + unit_specs,
            [row_f32, row_f32, row_bf, proj_shape, row_bf,
             shaped((PIECES, tiles, 2, TILE, TILE), BF)],
            [strips, wide, slim, *unit_scratch(sz), unit_sems],
            3000,
        )
        if layer_at < L - 1:
            state, *chunks = launch(
                part(mlp_kernel, sz, layer_at), f"mlp_{layer_at}",
                (state_2, normed_m, up_rows, gains, shifts, biases, *mlps[layer_at]),
                [VMEM] * 6 + mlp_specs,
                [row_f32] + chunk_shapes,
                [strips, wide, *mlp_scratch, mlp_sems],
                3000,
            )
        kept.append((entry, got, proj_s, mixed_s, probs_s, state_1, state_2, normed_m,
                     proj_f, mixed_f, probs_f))

    pending = []
    smalls = [None] * L
    matrix_grads = {}
    for layer_at in reversed(range(L)):
        (entry, got, proj_s, mixed_s, probs_s, state_1, state_2, normed_m,
         proj_f, mixed_f, probs_f) = kept[layer_at]
        if layer_at == L - 1:
            output, grad, small_m, *parts = launch(
                part(last_mlp_kernel, sz, layer_at), f"last_mlp_{layer_at}",
                (sample_len, feature_len, cotangent, state_2, normed_m, up_rows, gains, biases,
                 *mlps[layer_at]),
                [SMEM] * 2 + [VMEM] * 6 + mlp_specs,
                [row_bf, row_f32, small_shape] + grad_shapes(sz, 2),
                [wide, wide, wide, slim, pltpu.VMEM((width, width), BF), *mlp_scratch, mlp_sems],
                7000,
            )
        else:
            grad, small_m, small_s, *parts = launch(
                part(mlp_back_kernel, sz, layer_at), f"mlp_back_{layer_at}",
                (grad, kept[layer_at + 1][0], state_2, normed_m, up_rows, gains, *back,
                 *mlps[layer_at]),
                [VMEM] * (6 + n) + mlp_specs,
                [row_f32, small_shape, small_shape] + grad_shapes(sz, 2),
                [wide, strips, wide, slim, pltpu.VMEM((width, width), BF), *mlp_scratch,
                 mlp_sems],
                7000,
            )
            smalls[layer_at + 1].append(small_s)
        matrix_grads[layer_at, 2] = parts
        grad, low, proj_grad, normed, small_f, *chunks = launch(
            part(feature_back_kernel, sz, layer_at), f"feature_back_{layer_at}",
            (grad, state_1, proj_f, probs_f, gains, shifts, *units[layer_at][1]),
            [VMEM] * 6 + unit_specs,
            [row_f32, row_bf, proj_shape, row_bf, small_shape] + chunk_shapes,
            [slim, strips, wide, *unit_scratch(sz), unit_sems],
            4000,
        )
        smalls[layer_at] = [small_m, small_f]
        chunks = exchange(sz, chunks)
        matrix_grads[layer_at, 1] = launch(
            part(matrix_grad_kernel, sz, 1), f"feature_matrix_{layer_at}",
            (proj_grad, low, mixed_f, normed), [VMEM] * 4, grad_shapes(sz, 1),
            [pltpu.VMEM((width, width), BF)], 2000,
        )
        *back, low, proj_grad = launch(
            part(sample_back_kernel, sz), f"sample_back_{layer_at}",
            (proj_s, probs_s, *chunks, *units[layer_at][0]),
            [VMEM] * (2 + n) + unit_specs,
            chunk_shapes + [row_bf, proj_shape],
            [slim, wide, *unit_scratch(sz), unit_sems],
            4000,
        )
        back = exchange(sz, back)
        matrix_grads[layer_at, 0] = launch(
            part(matrix_grad_kernel, sz, n), f"sample_matrix_{layer_at}",
            (proj_grad, low, mixed_s, *got), [VMEM] * (3 + n), grad_shapes(sz, 1),
            [pltpu.VMEM((width, width), BF), slim], 2000,
        )
    tokens_grad, small_s = launch(
        part(last_norm_kernel, sz), "last_norm", (grad, tokens, gains, *back), [VMEM] * (3 + n),
        [row_f32, small_shape], [strips], 1,
    )

    early = []
    for layer_at in range(L):
        early += smalls[layer_at]
    early = small_sum(sz, jnp.concatenate(early, axis=0)).reshape(-1, 8, width)
    late = small_sum(sz, small_s)
    by_layer = []
    at = 0
    for layer_at in range(L):
        count = len(smalls[layer_at])
        sums = [early[at + member] for member in range(count)]
        at += count
        by_layer.append(sums if count == 3 else sums + [late])
    gain_total, shift_total = (
        jnp.stack([jnp.stack([s[row], f[row], m[row]]) for m, f, s in by_layer])
        for row in range(2)
    )
    bias_total = jnp.stack([jnp.stack([f[3], f[2], m[2]]) for m, f, s in by_layer])
    up_bias_total = jnp.stack([m[3 : 3 + PIECES].reshape(-1) for m, f, s in by_layer])

    done = {}
    if sz.fast:
        for layer_at in reversed(range(L)):
            groups = [[2], [1], [0]]
            for group in groups:
                for kind in group:
                    done[layer_at, kind] = reduce_far(
                        sz, reduce_near(sz, *matrix_grads[layer_at, kind])
                    )
    else:
        for key, (full,) in matrix_grads.items():
            done[key] = reduce_whole(sz, full)

    def attention_grads(kind):
        qkv, out = [], []
        for layer_at in range(L):
            if sz.fast:
                value = done[layer_at, kind][0]
                qkv.append(value[:, :QKV].reshape(-1, 3, PAIR))
                out.append(value[:, QKV:].T)
            else:
                value = done[layer_at, kind][0]
                columns = width // n
                start = lax.axis_index("tensor") * columns
                whole = value[:, :, :QKV].reshape(-1, PIECES, 3, PAIR).transpose(0, 2, 1, 3)
                whole = whole.reshape(-1, 3, width)
                qkv.append(lax.dynamic_slice_in_dim(whole, start, columns, 2))
                whole = value[:, :, QKV:].reshape(-1, width)
                out.append(lax.dynamic_slice_in_dim(whole, start, columns, 1).T)
        return jnp.stack(qkv), jnp.stack(out)

    sample_qkv_grad, sample_out_grad = attention_grads(0)
    feature_qkv_grad, feature_out_grad = attention_grads(1)
    ups, downs = [], []
    for layer_at in range(L):
        value = done[layer_at, 2]
        if not sz.fast:
            columns = PIECES * width // n
            start = lax.axis_index("tensor") * columns
            value = value.reshape(2, -1, PIECES * width)
            value = lax.dynamic_slice_in_dim(value, start, columns, 2)
        ups.append(value[0])
        downs.append(value[1].T)
    return (
        output.reshape(shape),
        tokens_grad.reshape(shape),
        gain_total,
        shift_total,
        sample_qkv_grad,
        sample_out_grad,
        feature_qkv_grad,
        feature_out_grad,
        bias_total,
        jnp.stack(ups),
        up_bias_total,
        jnp.stack(downs),
    )


def solution(mesh):
    placed = (
        P("dp", "tensor", None, None),
        P("dp", "tensor", None, None),
        P("dp"),
        P("dp"),
        P("dp"),
        P(),
        P(),
        P(None, None, None, "tensor"),
        P(None, "tensor", None),
        P(None, None, None, "tensor"),
        P(None, "tensor", None),
        P(),
        P(None, None, "tensor"),
        P(),
        P(None, "tensor", None),
    )
    return jax.shard_map(
        body,
        mesh=mesh,
        in_specs=placed,
        out_specs=(
            P("dp", "tensor", None, None),
            P("dp", "tensor", None, None),
            P(),
            P(),
            P(None, "dp", None, "tensor"),
            P(None, "tensor", "dp"),
            P(None, "dp", None, "tensor"),
            P(None, "tensor", "dp"),
            P(),
            P(None, "dp", "tensor"),
            P(),
            P(None, "tensor", "dp"),
        ),
        check_vma=False,
    )
```

```python
import functools

import jax
import jax.numpy as jnp
from jax import lax
from jax.experimental import pallas as pl
from jax.experimental.pallas import tpu as pltpu
from jax.sharding import PartitionSpec as P

HD = 64
L = 2
PIECES = 4
PAIR = 2 * HD
QKV = 3 * PAIR
TILE = 128

epsilon = 1e-05
masked_score = -1e30
SCALE = HD ** (-0.5)
F32 = jnp.float32
BF = jnp.bfloat16
NT = (((1,), (1,)), ((), ()))
TN = (((0,), (0,)), ((), ()))
TANH_A = 0.7978845608028654
TANH_B = 0.044715
VMEM_GRANT = 62 * 2**20
VMEM = pl.BlockSpec(memory_space=pltpu.VMEM)
SMEM = pl.BlockSpec(memory_space=pltpu.SMEM)
ANY = pl.BlockSpec(memory_space=pl.ANY)


class Sizes:
    def __init__(self, shape, tensor, dp):
        self.blocks, self.samples, self.feats, self.width = shape
        self.tensor, self.dp = tensor, dp
        self.rows = self.blocks * self.samples * self.feats
        self.own_feats = self.feats // tensor
        self.run = self.blocks * self.samples
        self.chunk = self.own_feats * self.run
        self.group = tensor * self.run
        self.block_rows = self.samples * self.feats
        self.fast = tensor == 4 and dp == 8


def places(z):
    tensor_at = lax.axis_index("tensor")
    dp_at = lax.axis_index("dp")
    return tensor_at, lax.rem(dp_at, 2), lax.div(dp_at, 2)


def dot(a, b):
    return jnp.dot(a, b, preferred_element_type=F32)


def dot_nt(a, b):
    return lax.dot_general(a, b, NT, preferred_element_type=F32)


def dot_tn(a, b):
    return lax.dot_general(a, b, TN, preferred_element_type=F32)


def normal_rows(x):
    centre = x - jnp.mean(x, axis=-1, keepdims=True)
    spread = jnp.mean(centre * centre, axis=-1, keepdims=True)
    rate = lax.rsqrt(spread + epsilon)
    return centre * rate, rate


def over_rows(rows, fn, carry=0, step=64):
    for at in range(rows // step):
        carry = fn(slice(at * step, (at + 1) * step), carry)
    return carry


def fold(x):
    return jnp.sum(x.reshape(-1, 8, x.shape[-1]), axis=0)


def total(x):
    return jnp.sum(x, axis=0, keepdims=True)


def put_strips(strips, rows, value):
    for lane in range(value.shape[1] // TILE):
        strips[lane, rows, :] = value[:, lane * TILE : (lane + 1) * TILE]


def get_strips(strips, rows):
    return jnp.concatenate([strips[lane, rows, :] for lane in range(strips.shape[0])], axis=1)


def feature_slot(sz, tensor_at, at, slot):
    return (tensor_at ^ at) * sz.own_feats + slot


def spread_out(sz, tensor_at, wide, chunks):
    for at in range(sz.tensor):
        for slot in range(sz.own_feats):
            first = feature_slot(sz, tensor_at, at, slot)
            for lane in range(sz.width // TILE):
                rows = wide[lane, pl.ds(first, sz.run, stride=sz.feats), :]
                chunks[at][
                    slot * sz.run : (slot + 1) * sz.run, lane * TILE : (lane + 1) * TILE
                ] = rows.astype(BF)


def bring_back(sz, tensor_at, chunks, wide):
    for at in range(sz.tensor):
        for slot in range(sz.own_feats):
            first = feature_slot(sz, tensor_at, at, slot)
            for lane in range(sz.width // TILE):
                rows = chunks[at][
                    slot * sz.run : (slot + 1) * sz.run, lane * TILE : (lane + 1) * TILE
                ]
                wide[lane, pl.ds(first, sz.run, stride=sz.feats), :] = rows.astype(F32)


def by_feature(sz, chunks, x):
    for at in range(sz.tensor):
        for slot in range(sz.own_feats):
            first = slot * sz.group + at * sz.run
            x[first : first + sz.run, :] = chunks[at][slot * sz.run : (slot + 1) * sz.run, :]


def to_chunks(sz, value, chunks):
    for at in range(sz.tensor):
        for slot in range(sz.own_feats):
            first = slot * sz.group + at * sz.run
            chunks[at][slot * sz.run : (slot + 1) * sz.run, :] = value[
                first : first + sz.run
            ].astype(BF)


def where_halves(core):
    other = 1 - core
    return (
        (1 + core, core),
        (2 - core, core),
        (3, core),
        (1 + other, other),
        (2 - other, other),
        (3, other),
    )


def load_unit(sz, layer_at, member, parts, w, w_out, sems, core):
    pairs = []
    if not sz.fast:
        pairs += [(parts[0], w), (parts[1], w_out)]
    else:
        qkv, out = parts[:2]
        for at in range(3):
            pairs.append((qkv.at[layer_at, at], w.at[:, pl.ds(at * PAIR, PAIR)]))
        pairs.append((out.at[layer_at], w_out.at[pl.ds(0, PAIR), :]))
        half_rows = sz.width // 2
        for source, (piece, half) in zip(parts[2:], where_halves(core)):
            if member is not None:
                source = source.at[member]
            start = pl.multiple_of(half * half_rows, half_rows)
            first = pl.multiple_of(piece * QKV, TILE)
            pairs.append(
                (source.at[:, pl.ds(0, QKV)], w.at[pl.ds(start, half_rows), pl.ds(first, QKV)])
            )
            first = pl.multiple_of(piece * PAIR, TILE)
            for block in range(half_rows // TILE):
                lanes = pl.ds(pl.multiple_of(start + block * TILE, TILE), TILE)
                pairs.append(
                    (
                        source.at[pl.ds(block * TILE, TILE), pl.ds(QKV, PAIR)],
                        w_out.at[pl.ds(first, PAIR), lanes],
                    )
                )
    return begin(pairs, sems)


def begin(pairs, sems):
    copies = []
    for source, target in pairs:
        copies.append(pltpu.make_async_copy(source, target, sems.at[len(copies)]))
        copies[-1].start()
    return copies


def finish(copies):
    for copy in copies:
        copy.wait()


def load_mlp(sz, layer_at, parts, up, down, sems, core):
    pairs = []
    if not sz.fast:
        pairs += [(parts[0], up), (parts[1], down)]
    else:
        width = sz.width
        pairs.append((parts[0].at[layer_at], up.at[:, pl.ds(0, width)]))
        pairs.append((parts[1].at[layer_at], down.at[pl.ds(0, width), :]))
        half_rows = width // 2
        for source, (piece, half) in zip(parts[2:], where_halves(core)):
            start = pl.multiple_of(half * half_rows, half_rows)
            first = pl.multiple_of(piece * width, width)
            pairs.append(
                (source.at[0], up.at[pl.ds(start, half_rows), pl.ds(first, width)])
            )
            rows = pl.ds(pl.multiple_of(first + start, half_rows), half_rows)
            pairs.append((source.at[1], down.at[rows, :]))
    return begin(pairs, sems)


def put_grad(sz, grads, outs, piece, member, core, z, direct=False):
    if not sz.fast:
        outs[0][piece, member] = grads[...]
        return
    if len(outs) == 1:
        name = lax.axis_index("tensor") ^ piece
        for far in range(4):
            for half in range(2):
                first = far * 128 + half * 64
                outs[0][half, name, far, member] = grads[first : first + 64, :]
        return
    mine, theirs = outs
    if direct or piece in (0, 3):
        at_mine = at_theirs = piece
    elif piece == 1:
        at_mine, at_theirs = 1 + core, 2 - core
    else:
        at_mine, at_theirs = 2 - core, 1 + core
    for place, near in enumerate((0, 1, 2, 3) if direct else (0, 2, 1, 3)):
        first = (z ^ near) * 128
        rows_mine = pl.ds(pl.multiple_of(first + core * 64, 64), 64)
        rows_theirs = pl.ds(pl.multiple_of(first + (1 - core) * 64, 64), 64)
        mine[at_mine, place, member] = grads[rows_mine, :]
        theirs[at_theirs, place, member] = grads[rows_theirs, :]


def head_masks():
    lane = lax.broadcasted_iota(jnp.int32, (1, PAIR), 1)
    return lane < HD, lane >= HD


def sample_bias(sz, tensor_at, tasks, lengths, bias):
    def of(index):
        run_at = index // sz.run
        block = (index // sz.samples) % sz.blocks
        sample = (run_at ^ tensor_at) * sz.samples + index % sz.samples
        task = jnp.zeros_like(index)
        length = jnp.zeros_like(index)
        for at in range(sz.blocks):
            task = jnp.where(block == at, tasks[at], task)
            length = jnp.where(block == at, lengths[at], length)
        return task, sample < length

    row_task, unused = of(lax.broadcasted_iota(jnp.int32, (sz.group, 1), 0))
    key_task, key_live = of(lax.broadcasted_iota(jnp.int32, (1, sz.group), 1))
    key_task = jnp.where(key_live, key_task, -1)
    bias[...] = jnp.where(row_task == key_task, 0.0, masked_score)


def feature_bias(sz, length):
    row = lax.broadcasted_iota(jnp.int32, (TILE, TILE), 0)
    key = lax.broadcasted_iota(jnp.int32, (TILE, TILE), 1)
    same = (row // sz.feats) == (key // sz.feats)
    return jnp.where(same & (key % sz.feats < length), 0.0, masked_score)


def attend(proj, piece, jobs, probs, mixed):
    masks = head_masks()
    first = piece * QKV
    scores = []
    for rows, bias, place in jobs:
        query = proj[rows, first : first + PAIR]
        key = proj[rows, first + PAIR : first + 2 * PAIR]
        for mask in masks:
            scores.append(dot_nt(jnp.where(mask, query, 0) * SCALE, key) + bias)
    tops = [jnp.max(part, axis=-1, keepdims=True) for part in scores]
    weights = [jnp.exp(part - top) for part, top in zip(scores, tops)]
    shares = [1.0 / jnp.sum(part, axis=-1, keepdims=True) for part in weights]
    weights = [(part * share).astype(BF) for part, share in zip(weights, shares)]
    for at, (rows, bias, place) in enumerate(jobs):
        value = proj[rows, first + 2 * PAIR : first + QKV]
        pair = weights[2 * at : 2 * at + 2]
        for head in range(2):
            probs[piece, place, head] = pair[head]
        mixed[rows, piece * PAIR : (piece + 1) * PAIR] = jnp.where(
            masks[0], dot(pair[0], value), dot(pair[1], value)
        ).astype(BF)


def attend_back(proj, piece, jobs, probs, mixed_grad, proj_grad):
    masks = head_masks()
    first = piece * QKV
    head_grads, weights, weight_grads = [], [], []
    for rows, place in jobs:
        grad = mixed_grad[rows, piece * PAIR : (piece + 1) * PAIR]
        value = proj[rows, first + 2 * PAIR : first + QKV]
        for head, mask in enumerate(masks):
            head_grads.append(jnp.where(mask, grad, 0))
            weights.append(probs[piece, place, head])
            weight_grads.append(dot_nt(head_grads[-1], value))
    score_grads = []
    for low, grad in zip(weights, weight_grads):
        wide = low.astype(F32)
        product = wide * grad
        score_grads.append((product - wide * jnp.sum(product, axis=-1, keepdims=True)).astype(BF))
    for at, (rows, place) in enumerate(jobs):
        query = proj[rows, first : first + PAIR]
        key = proj[rows, first + PAIR : first + 2 * PAIR]
        one, two = score_grads[2 * at : 2 * at + 2]
        queries = jnp.where(masks[0], dot(one, key), dot(two, key)) * SCALE
        keys = dot_tn(one, jnp.where(masks[0], query, 0))
        keys = (keys + dot_tn(two, jnp.where(masks[1], query, 0))) * SCALE
        values = dot_tn(weights[2 * at], head_grads[2 * at])
        values = values + dot_tn(weights[2 * at + 1], head_grads[2 * at + 1])
        proj_grad[rows, first : first + PAIR] = queries.astype(BF)
        proj_grad[rows, first + PAIR : first + 2 * PAIR] = keys.astype(BF)
        proj_grad[rows, first + 2 * PAIR : first + QKV] = values.astype(BF)


def norm_back_rows(state, incoming, gain):
    xhat, rate = normal_rows(state)
    inner = incoming * gain
    back = rate * (
        inner
        - jnp.mean(inner, axis=-1, keepdims=True)
        - xhat * jnp.mean(inner * xhat, axis=-1, keepdims=True)
    )
    return xhat, back


def pack_copies(sz, layer_at, qkv, out, sent, core):
    half = sz.width // 2
    rows = pl.ds(pl.multiple_of(core * half, half), half)
    pairs = []
    for at in range(3):
        pairs.append((qkv.at[layer_at, at, rows, :], sent.at[:, pl.ds(at * PAIR, PAIR)]))
    for block in range(half // TILE):
        lanes = pl.ds(pl.multiple_of(core * half + block * TILE, TILE), TILE)
        pairs.append(
            (out.at[layer_at, :, lanes], sent.at[pl.ds(block * TILE, TILE), pl.ds(QKV, PAIR)])
        )
    return pairs


def start_kernel(sz, tokens, gains, shifts, qkv, out, *rest):
    chunks, rest = rest[: sz.tensor], rest[sz.tensor :]
    tensor_at, core, z = places(sz)
    copies = []
    if sz.fast:
        sent, strips, sems = rest
        copies = begin(pack_copies(sz, 0, qkv, out, sent, core), sems)
    else:
        (strips,) = rest

    def rows_of(rows, kept):
        xhat, unused = normal_rows(tokens[rows, :].astype(F32))
        put_strips(strips, rows, xhat * gains[0, 0:1, :] + shifts[0, 0:1, :])
        return kept

    over_rows(sz.rows, rows_of)
    spread_out(sz, tensor_at, strips, chunks)
    finish(copies)


def pack_units_kernel(sz, layer_at, *rest):
    operands, sent, sems = rest[:-2], rest[-2], rest[-1]
    tensor_at, core, z = places(sz)
    pairs = []
    count = len(operands) // 2
    for unit in range(count):
        target = sent if count == 1 else sent.at[unit]
        pairs += pack_copies(
            sz, layer_at, operands[2 * unit], operands[2 * unit + 1], target, core
        )
    finish(begin(pairs, sems))


def pack_mlp_kernel(sz, layer_at, up, down, sent, sems):
    tensor_at, core, z = places(sz)
    half = sz.width // 2
    rows = pl.ds(pl.multiple_of(core * half, half), half)
    pairs = [(w.at[layer_at, rows, :], sent.at[at]) for at, w in enumerate((up, down))]
    finish(begin(pairs, sems))


def nothing_kernel(sz, *rest):
    pass


def send_near_kernel(sz, mine, other, rows, rows_other, *outs):
    kept = outs[-1]
    count = rows.shape[0]
    small = (rows[...] + rows_other[...]).astype(BF)
    kept[...] = jnp.zeros_like(kept)
    kept[:count, :] = small.astype(F32)
    for piece in range(1, PIECES):
        out = outs[piece - 1]
        for near in range(4):
            value = mine[piece, near, 0].astype(F32) + other[piece, near, 0].astype(F32)
            out[near] = value.astype(BF)
        out[4] = jnp.zeros_like(out[4])
        out[4, :count, :] = small


def pairwise(one, two, three, four):
    return (one + two) + (three + four)


def send_far_kernel(sz, *refs):
    first, last, small, outs = refs[:5], refs[5:10], refs[10], refs[11:]
    kept, rows, sends = outs[0], outs[1], outs[2:]

    def value(unit, at, near):
        mine, other, *got = unit
        out = mine[0, near, 0].astype(F32) + other[0, near, 0].astype(F32)
        for one in got:
            out = out + (one[0, near, 0] if at == 0 else one[near]).astype(F32)
        return out

    x, y, d = (one[4].astype(F32) for one in last[2:])
    low = pairwise(small[...], x, y, d).astype(BF)
    rows[...] = low.astype(F32)
    for at, unit in enumerate((first, last)):
        kept[at] = value(unit, at, 0)
        for near in range(1, 4):
            sends[near - 1][at] = value(unit, at, near).astype(BF)
    for near in range(1, 4):
        sends[near - 1][2] = low


def last_sums_kernel(sz, *refs):
    kept, rows, one, two, three, mlp, mlp_got, upper_mlp, upper = refs[:9]
    s_qkv, s_out, f_qkv, f_out, up, down, gain, shift, bias, up_bias = refs[9:]
    small = pairwise(rows[...], one[2].astype(F32), two[2].astype(F32), three[2].astype(F32))

    def attention(layer_at, value, qkv, out):
        for at in range(3):
            qkv[layer_at, at] = value[:, at * PAIR : (at + 1) * PAIR]
        out[layer_at] = value[:, QKV:]

    for at, (qkv, out) in enumerate(((f_qkv, f_out), (s_qkv, s_out))):
        value = kept[at]
        for got in (one, two, three):
            value = value + got[at].astype(F32)
        attention(0, value, qkv, out)
        attention(1, upper[at].astype(F32), qkv, out)
    for at, w in enumerate((up, down)):
        w[0] = mlp[0, 0, at] + mlp_got[0, 0, at].astype(F32)
        w[1] = upper_mlp[at].astype(F32)
    for layer_at in range(L):
        m, f, s = (24 * layer_at + 8 * at for at in range(3))
        for out, places_in in ((gain, (s, f, m)), (shift, (s + 1, f + 1, m + 1)),
                               (bias, (f + 3, f + 2, m + 2))):
            for at, row in enumerate(places_in):
                out[at, layer_at : layer_at + 1, :] = small[row : row + 1]
        for piece in range(PIECES):
            lanes = slice(piece * sz.width, (piece + 1) * sz.width)
            row = m + 3 + piece
            up_bias[layer_at : layer_at + 1, lanes] = small[row : row + 1]


def unit_parts(sz):
    return 8 if sz.fast else 2


def sample_kernel(sz, layer_at, member, tasks, lengths, *rest):
    n, parts = sz.tensor, unit_parts(sz)
    chunks, weights = rest[:n], rest[n : n + parts]
    outs = rest[n + parts :]
    back, proj, mixed, probs = outs[:n], outs[n], outs[n + 1], outs[n + 2]
    x, bias, w, w_out, sems = outs[n + 3 :]
    tensor_at, core, z = places(sz)
    copies = load_unit(sz, layer_at, member, weights, w, w_out, sems, core)
    by_feature(sz, chunks, x)
    sample_bias(sz, tensor_at, tasks, lengths, bias)
    finish(copies)
    proj[...] = dot(x[...], w[...]).astype(BF)
    jobs = [
        (slice(slot * sz.group, (slot + 1) * sz.group), bias[...], slot)
        for slot in range(sz.own_feats)
    ]
    for piece in range(PIECES):
        attend(proj, piece, jobs, probs, mixed)
    to_chunks(sz, dot(mixed[...], w_out[...]), back)


def feature_kernel(sz, layer_at, member, lengths, state, gains, shifts, out_bias, *rest):
    n, parts = sz.tensor, unit_parts(sz)
    chunks, weights = rest[:n], rest[n : n + parts]
    state_1, state_2, normed_m, proj, mixed, probs = rest[n + parts : n + parts + 6]
    strips, wide, normed, w, w_out, sems = rest[n + parts + 6 :]
    tensor_at, core, z = places(sz)
    copies = load_unit(sz, layer_at, member, weights, w, w_out, sems, core)
    bring_back(sz, tensor_at, chunks, strips)
    at = slice(layer_at, layer_at + 1)

    def before(rows, kept):
        value = state[rows, :].astype(F32) + get_strips(strips, rows) + out_bias[0, at, :]
        state_1[rows, :] = value
        xhat, unused = normal_rows(value)
        normed[rows, :] = (xhat * gains[1, at, :] + shifts[1, at, :]).astype(BF)
        return kept

    over_rows(sz.rows, before)
    biases = [feature_bias(sz, lengths[block]) for block in range(sz.blocks)]
    jobs = [
        (slice(tile * TILE, (tile + 1) * TILE), biases[tile * TILE // sz.block_rows], tile)
        for tile in range(sz.rows // TILE)
    ]
    finish(copies)
    proj[...] = dot(normed[...], w[...]).astype(BF)
    for piece in range(PIECES):
        attend(proj, piece, jobs, probs, mixed)
    wide[...] = dot(mixed[...], w_out[...])

    def after(rows, kept):
        value = state_1[rows, :] + wide[rows, :] + out_bias[1, at, :]
        state_2[rows, :] = value
        xhat, unused = normal_rows(value)
        normed_m[rows, :] = (xhat * gains[2, at, :] + shifts[2, at, :]).astype(BF)
        return kept

    over_rows(sz.rows, after)


def up_bias_rows(sz, tensor_at, piece):
    return (tensor_at ^ piece) if sz.fast else piece


def mlp_kernel(sz, layer_at, state_2, normed_m, up_bias, gains, shifts, out_bias, *rest):
    n = sz.tensor
    parts = 8 if sz.fast else 2
    weights, (state_3, *chunks) = rest[:parts], rest[parts : parts + 1 + n]
    strips, wide, hidden, up, down, sems = rest[parts + 1 + n :]
    tensor_at, core, z = places(sz)
    finish(load_mlp(sz, layer_at, weights, up, down, sems, core))
    width = sz.width
    for piece in range(PIECES):
        lanes = slice(piece * width, (piece + 1) * width)
        wide[...] = dot(normed_m[...], up[:, lanes])
        shift = up_bias[layer_at, pl.ds(up_bias_rows(sz, tensor_at, piece), 1), :]
        value = wide[...] + shift
        half = 0.5 + 0.5 * jnp.tanh(value * (TANH_A + TANH_A * TANH_B * (value * value)))
        hidden[:, lanes] = (value * half).astype(BF)
    wide[...] = dot(hidden[...], down[...])
    at = slice(layer_at, layer_at + 1)
    later = slice(layer_at + 1, layer_at + 2)

    def after(rows, kept):
        value = state_2[rows, :] + wide[rows, :] + out_bias[2, at, :]
        state_3[rows, :] = value
        xhat, unused = normal_rows(value)
        put_strips(strips, rows, xhat * gains[0, later, :] + shifts[0, later, :])
        return kept

    over_rows(sz.rows, after)
    spread_out(sz, tensor_at, strips, chunks)


def mlp_back(
    sz, layer_at, grad, state_2, normed_m, up_bias, gains, up, down, low, wide, other, hidden,
    up_grad, grads, grad_out, outs, small,
):
    tensor_at, core, z = places(sz)
    at = slice(layer_at, layer_at + 1)
    width = sz.width
    nothing = jnp.zeros((8, width), F32)

    def lower(rows, kept):
        part = grad[rows, :].astype(BF)
        low[rows, :] = part
        return kept + fold(part.astype(F32))

    small[...] = jnp.zeros_like(small)
    small[2:3, :] = total(over_rows(sz.rows, lower, nothing))
    for piece in range(PIECES):
        lanes = slice(piece * width, (piece + 1) * width)
        name = up_bias_rows(sz, tensor_at, piece)
        wide[...] = dot(normed_m[...], up[:, lanes])
        other[...] = dot_nt(low[...], down[lanes, :])
        shift = up_bias[layer_at, pl.ds(name, 1), :]
        value = wide[...] + shift
        square = value * value
        half = 0.5 + 0.5 * jnp.tanh(value * (TANH_A + TANH_A * TANH_B * square))
        full = value * half
        hidden[:, lanes] = full.astype(BF)
        slope = half + full * (1.0 - half) * (2.0 * TANH_A + 6.0 * TANH_A * TANH_B * square)
        part = (other[...] * slope).astype(BF)
        up_grad[:, lanes] = part
        small[pl.ds(3 + name, 1), :] = total(fold(part.astype(F32)))
        grads[...] = dot_tn(normed_m[...], up_grad[:, lanes]).astype(BF)
        put_grad(sz, grads, outs, piece, 0, core, z)
        grads[...] = dot_tn(low[...], hidden[:, lanes]).astype(BF)
        put_grad(sz, grads, outs, piece, 1, core, z)
    wide[...] = dot_nt(up_grad[...], up[...])

    def back(rows, kept):
        incoming = wide[rows, :]
        xhat, change = norm_back_rows(state_2[rows, :], incoming, gains[2, at, :])
        grad_out[rows, :] = grad[rows, :] + change
        return kept[0] + fold(incoming * xhat), kept[1] + fold(incoming)

    gain_sum, shift_sum = over_rows(sz.rows, back, (nothing, nothing))
    small[0:1, :] = total(gain_sum)
    small[1:2, :] = total(shift_sum)


def last_mlp_kernel(
    sz, layer_at, sample_lens, feature_lens, cotangent, state_2, normed_m, up_bias, gains, out_bias,
    *rest,
):
    parts, halves = unit_parts(sz), 1
    weights, rest = rest[:parts], rest[parts:]
    output, grad_out, small = rest[:3]
    outs = rest[3 : 3 + halves]
    grad, wide, other, low, hidden, up_grad, grads, up, down, sems = rest[3 + halves :]
    tensor_at, core, z = places(sz)
    copies = load_mlp(sz, layer_at, weights, up, down, sems, core)
    step = 64

    def live_rows(rows, kept):
        index = rows.start + lax.broadcasted_iota(jnp.int32, (step, 1), 0)
        block = index // sz.block_rows
        sample = tensor_at * sz.samples + (index // sz.feats) % sz.samples
        sample_len = jnp.zeros_like(index)
        feature_len = jnp.zeros_like(index)
        for at in range(sz.blocks):
            sample_len = jnp.where(block == at, sample_lens[at], sample_len)
            feature_len = jnp.where(block == at, feature_lens[at], feature_len)
        live = (sample < sample_len) & (index % sz.feats < feature_len)
        grad[rows, :] = jnp.where(live, cotangent[rows, :].astype(F32), 0.0)
        return kept

    over_rows(sz.rows, live_rows, 0, step)
    finish(copies)
    mlp_back(
        sz, layer_at, grad, state_2, normed_m, up_bias, gains, up, down, low, wide, other, hidden,
        up_grad, grads, grad_out, outs, small,
    )
    at = slice(layer_at, layer_at + 1)
    other[...] = dot(hidden[...], down[...])

    def after(rows, kept):
        value = state_2[rows, :] + other[rows, :] + out_bias[2, at, :]
        output[rows, :] = value.astype(BF)
        return kept

    over_rows(sz.rows, after)


def mlp_back_kernel(
    sz, layer_at, grad_in, state_3, state_2, normed_m, up_bias, gains, *rest
):
    n = sz.tensor
    parts, halves = unit_parts(sz), 2 if sz.fast else 1
    chunks, weights, rest = rest[:n], rest[n : n + parts], rest[n + parts :]
    grad_out, small = rest[:2]
    outs = rest[2 : 2 + halves]
    grad, strips, wide, other, low, hidden, up_grad, grads, up, down, sems = rest[2 + halves :]
    tensor_at, core, z = places(sz)
    copies = load_mlp(sz, layer_at, weights, up, down, sems, core)
    sample_norm_back(sz, layer_at + 1, tensor_at, grad_in, state_3, chunks, gains, strips, grad)
    finish(copies)
    mlp_back(
        sz, layer_at, grad, state_2, normed_m, up_bias, gains, up, down, low, wide, other, hidden,
        up_grad, grads, grad_out, outs, small,
    )


def sample_norm_back(sz, layer_at, tensor_at, grad_in, state, chunks, gains, strips, grad):
    bring_back(sz, tensor_at, chunks, strips)
    at = slice(layer_at, layer_at + 1)

    def back(rows, kept):
        incoming = get_strips(strips, rows)
        xhat, change = norm_back_rows(state[rows, :].astype(F32), incoming, gains[0, at, :])
        grad[rows, :] = grad_in[rows, :] + change
        return kept

    over_rows(sz.rows, back)


def last_norm_kernel(sz, grad_in, state, gains, *rest):
    chunks, (grad, strips) = rest[: sz.tensor], rest[sz.tensor :]
    tensor_at, core, z = places(sz)
    sample_norm_back(sz, 0, tensor_at, grad_in, state, chunks, gains, strips, grad)


def feature_back_kernel(sz, layer_at, member, grad, state_1, proj, probs, gains, shifts, *rest):
    n, parts = sz.tensor, unit_parts(sz)
    weights, rest = rest[:parts], rest[parts:]
    grad_out, low, proj_grad, normed, small = rest[:5]
    chunks = rest[5 : 5 + n]
    mixed_grad, strips, wide, w, w_out, sems = rest[5 + n :]
    tensor_at, core, z = places(sz)
    copies = load_unit(sz, layer_at, member, weights, w, w_out, sems, core)
    at = slice(layer_at, layer_at + 1)
    nothing = jnp.zeros((8, sz.width), F32)

    def lower(rows, kept):
        part = grad[rows, :].astype(BF)
        low[rows, :] = part
        return kept + fold(part.astype(F32))

    small[...] = jnp.zeros_like(small)
    small[2:3, :] = total(over_rows(sz.rows, lower, nothing))
    finish(copies)
    mixed_grad[...] = dot_nt(low[...], w_out[...]).astype(BF)
    jobs = [(slice(tile * TILE, (tile + 1) * TILE), tile) for tile in range(sz.rows // TILE)]
    for piece in range(PIECES):
        attend_back(proj, piece, jobs, probs, mixed_grad, proj_grad)
    wide[...] = dot_nt(proj_grad[...], w[...])

    def back(rows, kept):
        incoming = wide[rows, :]
        gain = gains[1, at, :]
        xhat, change = norm_back_rows(state_1[rows, :], incoming, gain)
        value = grad[rows, :] + change
        grad_out[rows, :] = value
        put_strips(strips, rows, value)
        normed[rows, :] = (xhat * gain + shifts[1, at, :]).astype(BF)
        rounded = value.astype(BF).astype(F32)
        return (
            kept[0] + fold(incoming * xhat),
            kept[1] + fold(incoming),
            kept[2] + fold(rounded),
        )

    sums = over_rows(sz.rows, back, (nothing, nothing, nothing))
    small[0:1, :] = total(sums[0])
    small[1:2, :] = total(sums[1])
    small[3:4, :] = total(sums[2])
    spread_out(sz, tensor_at, strips, chunks)


def sample_back_kernel(sz, layer_at, member, proj, probs, gains, shifts, *rest):
    n, parts = sz.tensor, unit_parts(sz)
    chunks, rows_in, rest = rest[:n], rest[n : 2 * n], rest[2 * n :]
    weights, rest = rest[:parts], rest[parts:]
    back, low, proj_grad, small = rest[:n], rest[n], rest[n + 1], rest[n + 2]
    mixed_grad, normed, w, w_out, sems = rest[n + 3 :]
    tensor_at, core, z = places(sz)
    copies = load_unit(sz, layer_at, member, weights, w, w_out, sems, core)
    by_feature(sz, chunks, low)
    by_feature(sz, rows_in, normed)
    finish(copies)
    mixed_grad[...] = dot_nt(low[...], w_out[...]).astype(BF)
    jobs = [
        (slice(slot * sz.group, (slot + 1) * sz.group), slot) for slot in range(sz.own_feats)
    ]
    for piece in range(PIECES):
        attend_back(proj, piece, jobs, probs, mixed_grad, proj_grad)
    normed_grad = dot_nt(proj_grad[...], w[...])
    to_chunks(sz, normed_grad, back)
    at = slice(layer_at, layer_at + 1)
    shift_sum = total(fold(normed_grad))
    gain_sum = total(fold(normed_grad * normed[...].astype(F32)))
    small[...] = jnp.zeros_like(small)
    small[0:1, :] = (gain_sum - shifts[0, at, :] * shift_sum) / gains[0, at, :]
    small[1:2, :] = shift_sum


def matrix_grad_kernel(sz, count, direct, proj_grad, low, mixed, *rest):
    halves = 2 if sz.fast else 1
    rows, outs, rest = rest[:count], rest[count : count + halves], rest[count + halves :]
    tensor_at, core, z = places(sz)
    if count == 1:
        (grads,) = rest
        (normed,) = rows
    else:
        grads, normed = rest
        by_feature(sz, rows, normed)
    for piece in range(PIECES):
        lanes = slice(piece * QKV, (piece + 1) * QKV)
        grads[piece, :, :QKV] = dot_tn(normed[...], proj_grad[:, lanes]).astype(BF)
        lanes = slice(piece * PAIR, (piece + 1) * PAIR)
        grads[piece, :, QKV:] = dot_tn(low[...], mixed[:, lanes]).astype(BF)
        put_grad(sz, grads.at[piece], outs, piece, 0, core, z, direct)


def shaped(shape, dtype):
    return jax.ShapeDtypeStruct(shape, dtype)


class Job:
    def __init__(self, groups, outs, split, then):
        self.groups, self.outs, self.split, self.then = groups, outs, split, then
        self.terms = [term for group in groups for term in group]

    def scratch(self):
        shapes = [
            (count, array.shape[1], members, *array.shape[3:])
            for array, first, count, member, members in self.terms
        ]
        return [
            pltpu.VMEM(shape, term[0].dtype) for shape, term in zip(shapes, self.terms)
        ] + [pltpu.SemaphoreType.DMA((len(self.terms),))]

    def start(self, refs, scratch):
        pairs = []
        for ref, term, target in zip(refs, self.terms, scratch):
            array, first, count, member, members = term
            pairs.append((ref.at[pl.ds(first, count), :, pl.ds(member, members)], target))
        return begin(pairs, scratch[-1])

    def finish(self, copies, outs, scratch):
        finish(copies)
        at = place = 0
        for group in self.groups:
            refs = scratch[at : at + len(group)]
            at += len(group)
            lead, near, members = refs[0].shape[:3]
            for one in range(lead):
                for two in range(near):
                    for member in range(members):
                        value = refs[0][one, two, member].astype(F32)
                        for ref in refs[1:]:
                            value = value + ref[one, two, member].astype(F32)
                        out, index, lead_at = outs[0], two, one
                        if self.split == 1:
                            out, lead_at = outs[one], 0
                        elif self.split < 0:
                            index = lax.div(lax.axis_index("dp"), 2) ^ (0, 2, 1, 3)[two]
                        elif self.split and two >= near // 2:
                            out, index = outs[1], two - near // 2
                        out[lead_at, index, place + member] = value.astype(out.dtype)
            place += members


def launch(kernel, name, operands, specs, outs, scratch, micros, after=(), jobs=()):
    after, outs = list(after), list(outs)
    sums = [term[0] for job in jobs for term in job.terms]
    job_outs = [out for job in jobs for out in job.outs]
    job_scratch = [job.scratch() for job in jobs]
    count, plain = len(operands), len(scratch)
    skip = count + len(sums) + len(after)

    def whole(*refs):
        given, results = refs[count : count + len(sums)], refs[skip : skip + len(outs)]
        extra = refs[skip + len(outs) : skip + len(outs) + len(job_outs)]
        rest = refs[skip + len(outs) + len(job_outs) :]
        own, rest = rest[:plain], rest[plain:]
        started = []
        for job, buffers in zip(jobs, job_scratch):
            mine, rest = rest[: len(buffers)], rest[len(buffers) :]
            started.append((job, mine, job.start(given[: len(job.terms)], mine)))
            given = given[len(job.terms) :]
        kernel(*refs[:count], *results, *own)
        for job, mine, copies in started:
            job.finish(copies, extra[: len(job.outs)], mine)
            extra = extra[len(job.outs) :]

    results = pl.pallas_call(
        whole,
        out_shape=outs + job_outs,
        in_specs=list(specs) + [ANY] * (len(sums) + len(after)),
        out_specs=[VMEM] * (len(outs) + len(job_outs)),
        scratch_shapes=list(scratch) + [buffer for buffers in job_scratch for buffer in buffers],
        name=name,
        cost_estimate=pl.CostEstimate(
            flops=int(micros * 8e9), bytes_accessed=1_000_000, transcendentals=0
        ),
        compiler_params=pltpu.CompilerParams(vmem_limit_bytes=VMEM_GRANT),
    )(*operands, *sums, *after)
    results, extra = results[: len(outs)], results[len(outs) :]
    for job in jobs:
        job.then(*extra[: len(job.outs)])
        extra = extra[len(job.outs) :]
    return results


def grad_shapes(sz, members, background=False):
    if sz.fast and background:
        return [shaped((2, PIECES, 4, members, 64, sz.width), BF)]
    if sz.fast:
        return [shaped((PIECES, 4, members, 64, sz.width), BF)] * 2
    return [shaped((PIECES, members, sz.width, sz.width), BF)]


def swap_cores(sz, v):
    return lax.ppermute(v, "dp", [(at, at ^ 1) for at in range(sz.dp)])


def swap_near(sz, v, distance):
    return lax.ppermute(v, "tensor", [(at, at ^ distance) for at in range(sz.tensor)])


def swap_far(sz, v, distance):
    return lax.ppermute(v, "dp", [(at, at ^ (2 * distance)) for at in range(sz.dp)])


def swap_turn(sz, v, turn):
    pairs = []
    for dp_at in range(sz.dp):
        distance = 1 + ((dp_at + turn) % 2)
        for at in range(sz.tensor):
            base = dp_at * sz.tensor
            pairs.append((base + at, base + (at ^ distance)))
    return lax.ppermute(v, ("dp", "tensor"), pairs)


def exchange(sz, chunks):
    return [chunks[0]] + [swap_near(sz, chunks[at], at) for at in range(1, sz.tensor)]


def gather_unit(sz, half):
    first = swap_turn(sz, half, 0)
    second = swap_turn(sz, half, 1)
    third = swap_turn(sz, first, 1)
    got = [first, second, third]
    return got + [swap_cores(sz, v) for v in got]


class Reduction:
    def __init__(self, sz, *units):
        self.sz = sz
        self.units = [(mine, swap_cores(sz, theirs), mine.shape[2]) for mine, theirs in units]
        self.members = sum(unit[2] for unit in self.units)
        self.tail = units[0][0].shape[3:]

    def groups(self, first, count, extra):
        groups, place = [], 0
        for mine, other, members in self.units:
            group = [(mine, first, count, 0, members), (other, first, count, 0, members)]
            group += [(array, at, count, place, members) for array, at in extra]
            groups.append(group)
            place += members
        return groups

    def shape(self, lead, near, dtype=BF):
        return shaped((lead, near, self.members, *self.tail), dtype)

    def job(self, step):
        return getattr(self, f"step_{step}")()

    def step_1(self):
        def then(out):
            self.sent, self.far = out, swap_turn(self.sz, out, 1)

        return Job(self.groups(2, 2, []), [self.shape(2, 4)], 0, then)

    def step_2(self):
        def then(out):
            self.sent, self.near = out, swap_turn(self.sz, out, 0)

        return Job(self.groups(1, 1, [(self.far, 1)]), [self.shape(1, 4)], 0, then)

    def step_3(self):
        def then(kept, out):
            self.kept, self.got = kept, swap_far(self.sz, out, 1)

        groups = self.groups(0, 1, [(self.far, 0), (self.near, 0)])
        return Job(groups, [self.shape(1, 2)] * 2, 2, then)

    def step_4(self):
        def then(kept, out):
            self.kept, self.got = kept, swap_far(self.sz, out, 2)

        groups = [[(array, 0, 1, 0, self.members) for array in (self.kept, self.got)]]
        return Job(groups, [self.shape(1, 1, F32), self.shape(1, 1)], 2, then)

    def result(self):
        return (self.kept + self.got.astype(F32)).reshape(self.members, *self.tail)


class Direct:
    def __init__(self, sz, mine, theirs):
        self.sz, self.mine = sz, mine
        self.other = swap_cores(sz, theirs)

    def job(self, step):
        def then(*sent):
            self.got = [swap_near(self.sz, v, at + 1) for at, v in enumerate(sent)]

        group = [(array, 1, 3, 0, 1) for array in (self.mine, self.other)]
        shape = shaped((1, *self.mine.shape[1:]), BF)
        return Job([group], [shape] * 3, 1, then)


def join(sz, *parts):
    one = object.__new__(Reduction)
    one.sz, one.tail = sz, (64, sz.width)
    plain = [not isinstance(part, Reduction) for part in parts]
    one.members = sum(p.shape[2] if alone else p.members for p, alone in zip(parts, plain))

    def step_3():
        def then(kept, out):
            one.kept, one.got = kept, swap_far(sz, out, 1)

        groups = []
        for part, alone in zip(parts, plain):
            if alone:
                groups.append([(part, 0, 1, 0, part.shape[2])])
            else:
                groups += part.groups(0, 1, [(part.far, 0), (part.near, 0)])
        return Job(groups, [one.shape(1, 2)] * 2, 2, then)

    def step_0():
        def then(out):
            one.out = out

        groups = []
        for part in parts:
            groups += part.groups(0, 1, [(part.far, 0), (part.near, 0)])
        return Job(groups, [one.shape(1, 4)], -1, then)

    one.step_3, one.step_0 = step_3, step_0
    return one


def reduce_cores(sz, full):
    pairs = [[at, at + 1] for at in range(0, sz.dp, 2)]
    full = lax.psum_scatter(
        full, "dp", scatter_dimension=0, axis_index_groups=pairs, tiled=True
    )
    return full.reshape(full.shape[1:])


def reduce_lines(sz, part):
    lines = [[2 * at + core for at in range(sz.dp // 2)] for core in range(2)]
    part = lax.psum_scatter(
        part, "dp", scatter_dimension=0, axis_index_groups=lines, tiled=True
    )
    return part.reshape(part.shape[1:]).astype(F32)


def reduce_near(sz, part):
    part = lax.psum_scatter(part, "tensor", scatter_dimension=0, tiled=True)
    return part.reshape(part.shape[1:])


def reduce_whole(sz, full):
    members, width = full.shape[1], full.shape[2]
    full = full.transpose(1, 2, 0, 3)
    part = lax.psum_scatter(full, "dp", scatter_dimension=1, tiled=True)
    return lax.psum(part, "tensor").astype(F32)


def gathered_unit(qkv, out):
    qkv = lax.all_gather(qkv, "tensor", axis=2, tiled=True)
    out = lax.all_gather(out, "tensor", axis=0, tiled=True)
    width = qkv.shape[1]
    qkv = qkv.reshape(3, width, PIECES, PAIR).transpose(1, 2, 0, 3)
    return [qkv.reshape(width, PIECES * QKV), out]


def body(
    tokens,
    cotangent,
    block_task,
    sample_len,
    feature_len,
    norm_gain,
    norm_shift,
    sample_qkv,
    sample_out,
    feature_qkv,
    feature_out,
    out_bias,
    up_weight,
    up_bias,
    down_weight,
):
    shape = tokens.shape
    sz = Sizes(shape, lax.axis_size("tensor"), lax.axis_size("dp"))
    rows, width, n = sz.rows, sz.width, sz.tensor
    tokens = tokens.reshape(rows, width)
    cotangent = cotangent.reshape(rows, width)
    gains, shifts, biases = (
        jnp.transpose(v, (1, 0, 2)) for v in (norm_gain, norm_shift, out_bias)
    )
    up_rows = up_bias.reshape(L, PIECES, -1)
    qkvs = [jnp.transpose(v, (0, 2, 1, 3)) for v in (sample_qkv, feature_qkv)]
    outs = [sample_out, feature_out]
    part = functools.partial
    wide = pltpu.VMEM((rows, width), F32)
    strips = pltpu.VMEM((width // TILE, rows, TILE), F32)
    slim = pltpu.VMEM((rows, width), BF)
    dma = pltpu.SemaphoreType.DMA
    row_f32 = shaped((rows, width), F32)
    row_bf = shaped((rows, width), BF)
    chunk_shapes = [shaped((sz.chunk, width), BF)] * n
    proj_shape = shaped((rows, PIECES * QKV), BF)
    small_shape = shaped((8, width), F32)
    half_unit = (width // 2, width)
    sends = [shaped(half_unit, BF)] if sz.fast else []

    *chunks, sent = launch(
        part(start_kernel, sz), "start", (tokens, gains, shifts, qkvs[0], outs[0]),
        [VMEM] * 3 + [ANY] * 2, chunk_shapes + sends, [strips] + [dma((5,))] * len(sends), 3,
    ) if sz.fast else [*launch(
        part(start_kernel, sz), "start", (tokens, gains, shifts, qkvs[0], outs[0]),
        [VMEM] * 3 + [ANY] * 2, chunk_shapes, [strips], 3,
    ), None]

    units = [[None, None] for _ in range(L)]
    members = [[None, None]] + [[0, 1]] * (L - 1)
    mlps = [None] * L
    if sz.fast:

        def pack_units(layer_at, kinds, after):
            operands = []
            for kind in kinds:
                operands += [qkvs[kind], outs[kind]]
            shapes = half_unit if len(kinds) == 1 else (len(kinds), *half_unit)
            return launch(
                part(pack_units_kernel, sz, layer_at), f"pack_units_{layer_at}", operands,
                [ANY] * len(operands), [shaped(shapes, BF)], [dma((5 * len(kinds),))], 2, after,
            )[0]

        def pack_mlp(layer_at, after):
            return launch(
                part(pack_mlp_kernel, sz, layer_at), f"pack_mlp_{layer_at}",
                [up_weight, down_weight], [ANY] * 2, [shaped((2, *half_unit), BF)], [dma((2,))],
                2, after,
            )[0]

        got = gather_unit(sz, sent)
        units[0][0] = [qkvs[0], outs[0]] + got
    else:
        for layer_at in range(L):
            for kind in range(2):
                units[layer_at][kind] = gathered_unit(qkvs[kind][layer_at], outs[kind][layer_at])
            up = lax.all_gather(up_weight[layer_at], "tensor", axis=1, tiled=True)
            down = lax.all_gather(down_weight[layer_at], "tensor", axis=0, tiled=True)
            mlps[layer_at] = [up, down]

    def gather_units(layer_at, kinds, after):
        if not sz.fast:
            return []
        sent = pack_units(layer_at, kinds, after)
        got = gather_unit(sz, sent)
        for kind in kinds:
            units[layer_at][kind] = [qkvs[kind], outs[kind]] + got
        return [sent]

    def gather_mlp(layer_at, after):
        if not sz.fast:
            return []
        sent = pack_mlp(layer_at, after)
        mlps[layer_at] = [up_weight, down_weight] + gather_unit(sz, sent)
        return [sent]

    def arrived(parts, count):
        return parts[2 : 2 + count] if sz.fast else []

    unit_specs = [ANY] * unit_parts(sz)
    mlp_specs = [ANY] * unit_parts(sz)
    unit_scratch = [
        pltpu.VMEM((width, PIECES * QKV), BF),
        pltpu.VMEM((width, width), BF),
        dma((22 if sz.fast else 2,)),
    ]
    mlp_scratch = [
        pltpu.VMEM((width, PIECES * width), BF),
        pltpu.VMEM((PIECES * width, width), BF),
        dma((14 if sz.fast else 2,)),
    ]
    hidden = pltpu.VMEM((rows, PIECES * width), BF)
    square = pltpu.VMEM((width, width), BF)

    state = tokens
    kept = []
    for layer_at in range(L):
        entry = state
        got = exchange(sz, chunks)
        slots = sz.own_feats
        if layer_at == 0:
            began = gather_units(0, (1,), got[1:] + arrived(units[0][0], 2))
            began += gather_mlp(0, began + arrived(units[0][0], 3))
        else:
            began = gather_mlp(layer_at, got[1:] + arrived(units[layer_at][0], 2))
        *back, proj_s, mixed_s, probs_s = launch(
            part(sample_kernel, sz, layer_at, members[layer_at][0]), f"sample_{layer_at}",
            (block_task, sample_len, *got, *units[layer_at][0]),
            [SMEM] * 2 + [VMEM] * n + unit_specs,
            chunk_shapes
            + [proj_shape, row_bf, shaped((PIECES, slots, 2, sz.group, sz.group), BF)],
            [slim, pltpu.VMEM((sz.group, sz.group), F32), *unit_scratch],
            8, began,
        )
        back = exchange(sz, back)
        tiles = rows // TILE
        began = []
        if layer_at < L - 1:
            after = back[1:] + arrived(mlps[layer_at], 2)
            began = gather_units(layer_at + 1, (0, 1), after)
        state_1, state_2, normed_m, proj_f, mixed_f, probs_f = launch(
            part(feature_kernel, sz, layer_at, members[layer_at][1]), f"feature_{layer_at}",
            (feature_len, state, gains, shifts, biases, *back, *units[layer_at][1]),
            [SMEM] + [VMEM] * (4 + n) + unit_specs,
            [row_f32, row_f32, row_bf, proj_shape, row_bf,
             shaped((PIECES, tiles, 2, TILE, TILE), BF)],
            [strips, wide, slim, *unit_scratch],
            9, began,
        )
        if layer_at < L - 1:
            state, *chunks = launch(
                part(mlp_kernel, sz, layer_at), f"mlp_{layer_at}",
                (state_2, normed_m, up_rows, gains, shifts, biases, *mlps[layer_at]),
                [VMEM] * 6 + mlp_specs,
                [row_f32] + chunk_shapes,
                [strips, wide, hidden, *mlp_scratch],
                9,
            )
        kept.append((entry, got, proj_s, mixed_s, probs_s, state_1, state_2, normed_m,
                     proj_f, mixed_f, probs_f))

    reductions, whole, done = {}, {}, {}
    cores, near = {}, {}

    def reduction(layer_at, kind, parts):
        if sz.fast and len(parts) == 1:
            cores[layer_at] = reduce_cores(sz, *parts)
        elif sz.fast and layer_at == 0 and kind < 2:
            reductions[layer_at, kind] = Direct(sz, *parts)
        elif sz.fast:
            reductions[layer_at, kind] = Reduction(sz, parts)
        else:
            (whole[layer_at, kind],) = parts

    def jobs(*steps):
        return [reductions[at[:2]].job(at[2]) for at in steps if at[:2] in reductions]

    def add_up(name, after, *steps, extra=()):
        todo = jobs(*steps) + list(extra)
        if not todo:
            return []
        launch(part(nothing_kernel, sz), name, [], [], [], [], 0.05, after, todo)
        return None

    smalls = [None] * L
    sides = []

    def small_rows():
        return jnp.concatenate([one for layer in smalls for one in layer], axis=0)

    for layer_at in reversed(range(L)):
        (entry, got, proj_s, mixed_s, probs_s, state_1, state_2, normed_m,
         proj_f, mixed_f, probs_f) = kept[layer_at]
        above = layer_at + 1
        if layer_at == L - 1:
            output, grad, small_m, *parts = launch(
                part(last_mlp_kernel, sz, layer_at), f"last_mlp_{layer_at}",
                (sample_len, feature_len, cotangent, state_2, normed_m, up_rows, gains, biases,
                 *mlps[layer_at]),
                [SMEM] * 2 + [VMEM] * 6 + mlp_specs,
                [row_bf, row_f32, small_shape] + grad_shapes(sz, 2, True),
                [wide, wide, wide, slim, hidden, hidden, square, *mlp_scratch],
                15,
            )
        else:
            grad, small_m, *parts = launch(
                part(mlp_back_kernel, sz, layer_at), f"mlp_back_{layer_at}",
                (grad, kept[above][0], state_2, normed_m, up_rows, gains, *back,
                 *mlps[layer_at]),
                [VMEM] * (6 + n) + mlp_specs,
                [row_f32, small_shape] + grad_shapes(sz, 2),
                [wide, strips, wide, wide, slim, hidden, hidden, square, *mlp_scratch],
                15, parts[:1],
            )
        reduction(layer_at, 2, parts)
        began = []
        if layer_at < L - 1 and sz.fast:
            add_up(f"sums_{layer_at}", [grad], (above, 1, 2), (above, 0, 1))
            began = [reductions[above, 1].sent, reductions[above, 0].sent]
        grad, low, proj_grad, normed, small_f, *chunks = launch(
            part(feature_back_kernel, sz, layer_at, members[layer_at][1]),
            f"feature_back_{layer_at}",
            (grad, state_1, proj_f, probs_f, gains, shifts, *units[layer_at][1]),
            [VMEM] * 6 + unit_specs,
            [row_f32, row_bf, proj_shape, row_bf, small_shape] + chunk_shapes,
            [slim, strips, wide, *unit_scratch],
            9, began,
        )
        smalls[layer_at] = [small_m, small_f]
        chunks = exchange(sz, chunks)
        parts = launch(
            part(matrix_grad_kernel, sz, 1, layer_at == 0), f"feature_matrix_{layer_at}",
            (proj_grad, low, mixed_f, normed), [VMEM] * 4, grad_shapes(sz, 1),
            [pltpu.VMEM((PIECES, width, width), BF)], 0.7, near.values(),
            jobs((layer_at, 2, 1), (above, 0, 2)),
        )
        if above in near:
            done[above, 2] = reduce_lines(sz, near[above])
        reduction(layer_at, 1, parts)
        *back, low, proj_grad, small_s = launch(
            part(sample_back_kernel, sz, layer_at, members[layer_at][0]),
            f"sample_back_{layer_at}",
            (proj_s, probs_s, gains, shifts, *chunks, *got, *units[layer_at][0]),
            [VMEM] * (4 + 2 * n) + unit_specs,
            chunk_shapes + [row_bf, proj_shape, small_shape],
            [slim, slim, *unit_scratch],
            9, list(parts[:1]) + [cores[at] for at in cores if at == layer_at],
        )
        smalls[layer_at].append(small_s)
        back = exchange(sz, back)
        if layer_at in cores:
            near[layer_at] = reduce_near(sz, cores[layer_at])
        if sz.fast and layer_at == 0:
            upper = join(sz, reductions[1, 1], reductions[1, 0])
            sides = [upper.job(0)]
            rows_small = small_rows()
            rows_other = swap_cores(sz, rows_small)
        parts = launch(
            part(matrix_grad_kernel, sz, n, layer_at == 0), f"sample_matrix_{layer_at}",
            (proj_grad, low, mixed_s, *got), [VMEM] * (3 + n), grad_shapes(sz, 1),
            [pltpu.VMEM((PIECES, width, width), BF), slim], 0.7,
            jobs=jobs((layer_at, 1, 1), *(((0, 2, 2),) if layer_at == 0 else ())) + sides,
        )
        reduction(layer_at, 0, parts)
    (tokens_grad,) = launch(
        part(last_norm_kernel, sz), "last_norm", (grad, tokens, gains, *back), [VMEM] * (3 + n),
        [row_f32], [strips], 5,
    )
    if sz.fast:
        upper = reduce_lines(sz, upper.out[0])
        first, last = reductions[0, 1], reductions[0, 0]
        block = shaped((64, width), F32)
        *sent, rows_kept = launch(
            part(send_near_kernel, sz), "send_near",
            (last.mine, last.other, rows_small, rows_other), [VMEM] * 4,
            [shaped((5, 64, width), BF)] * 3 + [block], [], 0.05, [tokens_grad],
        )
        last.got = [swap_near(sz, v, at + 1) for at, v in enumerate(sent)]
        add_up("sums_mlp", [rows_kept], (0, 2, 3))
        attention_kept, rows_kept, *sent = launch(
            part(send_far_kernel, sz), "send_far",
            (first.mine, first.other, *first.got, last.mine, last.other, *last.got, rows_kept),
            [VMEM] * 11, [shaped((2, 64, width), F32), block] + [shaped((3, 64, width), BF)] * 3,
            [], 0.05, [], jobs((0, 2, 4)),
        )
        got = [swap_far(sz, v, at + 1) for at, v in enumerate(sent)]
        mlp = reductions[0, 2]
        qkv_shape, out_shape = shaped((L, 3, 64, PAIR), F32), shaped((L, 64, PAIR), F32)
        wide_shape, row_shape = shaped((L, 64, width), F32), shaped((3, L, width), F32)
        (s_qkv, s_out, f_qkv, f_out, up, down, gain_total, shift_total, bias_total,
         up_bias_total) = launch(
            part(last_sums_kernel, sz), "last_sums",
            (attention_kept, rows_kept, *got, mlp.kept, mlp.got, done[1, 2], upper), [VMEM] * 9,
            [qkv_shape, out_shape, qkv_shape, out_shape, wide_shape, wide_shape,
             row_shape, row_shape, row_shape, shaped((L, PIECES * width), F32)], [], 0.05,
        )

        def turned(v):
            return jnp.transpose(v, (0, 2, 1))

        gain_total, shift_total, bias_total = (
            jnp.transpose(v, (1, 0, 2)) for v in (gain_total, shift_total, bias_total)
        )
        return (
            output.reshape(shape), tokens_grad.reshape(shape), gain_total, shift_total,
            jnp.transpose(s_qkv, (0, 2, 1, 3)), turned(s_out),
            jnp.transpose(f_qkv, (0, 2, 1, 3)), turned(f_out),
            bias_total, up, up_bias_total, turned(down),
        )
    early = lax.psum(small_rows(), ("dp", "tensor"))
    early = early.reshape(-1, 8, width)
    by_layer = []
    at = 0
    for layer_at in range(L):
        count = len(smalls[layer_at])
        sums = [early[at + member] for member in range(count)]
        at += count
        by_layer.append(sums)
    gain_total, shift_total = (
        jnp.stack([jnp.stack([s[row], f[row], m[row]]) for m, f, s in by_layer])
        for row in range(2)
    )
    bias_total = jnp.stack([jnp.stack([f[3], f[2], m[2]]) for m, f, s in by_layer])
    up_bias_total = jnp.stack([m[3 : 3 + PIECES].reshape(-1) for m, f, s in by_layer])

    if not sz.fast:
        for key, full in whole.items():
            done[key] = reduce_whole(sz, full)

    def attention_grads(kind):
        qkv, out = [], []
        for layer_at in range(L):
            if sz.fast:
                value = done[layer_at, kind][0]
                qkv.append(value[:, :QKV].reshape(-1, 3, PAIR))
                out.append(value[:, QKV:].T)
            else:
                value = done[layer_at, kind][0]
                columns = width // n
                start = lax.axis_index("tensor") * columns
                whole = value[:, :, :QKV].reshape(-1, PIECES, 3, PAIR).transpose(0, 2, 1, 3)
                whole = whole.reshape(-1, 3, width)
                qkv.append(lax.dynamic_slice_in_dim(whole, start, columns, 2))
                whole = value[:, :, QKV:].reshape(-1, width)
                out.append(lax.dynamic_slice_in_dim(whole, start, columns, 1).T)
        return jnp.stack(qkv), jnp.stack(out)

    sample_qkv_grad, sample_out_grad = attention_grads(0)
    feature_qkv_grad, feature_out_grad = attention_grads(1)
    ups, downs = [], []
    for layer_at in range(L):
        value = done[layer_at, 2]
        if not sz.fast:
            columns = PIECES * width // n
            start = lax.axis_index("tensor") * columns
            value = value.reshape(2, -1, PIECES * width)
            value = lax.dynamic_slice_in_dim(value, start, columns, 2)
        ups.append(value[0])
        downs.append(value[1].T)
    return (
        output.reshape(shape),
        tokens_grad.reshape(shape),
        gain_total,
        shift_total,
        sample_qkv_grad,
        sample_out_grad,
        feature_qkv_grad,
        feature_out_grad,
        bias_total,
        jnp.stack(ups),
        up_bias_total,
        jnp.stack(downs),
    )


def solution(mesh):
    placed = (
        P("dp", "tensor", None, None),
        P("dp", "tensor", None, None),
        P("dp"),
        P("dp"),
        P("dp"),
        P(),
        P(),
        P(None, None, None, "tensor"),
        P(None, "tensor", None),
        P(None, None, None, "tensor"),
        P(None, "tensor", None),
        P(),
        P(None, None, "tensor"),
        P(),
        P(None, "tensor", None),
    )
    return jax.shard_map(
        body,
        mesh=mesh,
        in_specs=placed,
        out_specs=(
            P("dp", "tensor", None, None),
            P("dp", "tensor", None, None),
            P(),
            P(),
            P(None, "dp", None, "tensor"),
            P(None, "tensor", "dp"),
            P(None, "dp", None, "tensor"),
            P(None, "tensor", "dp"),
            P(),
            P(None, "dp", "tensor"),
            P(),
            P(None, "tensor", "dp"),
        ),
        check_vma=False,
    )
```

```python
import functools

import jax
import jax.numpy as jnp
from jax import lax
from jax.experimental import pallas as pl
from jax.experimental.pallas import tpu as pltpu
from jax.sharding import PartitionSpec as P

HD = 64
L = 2
PIECES = 4
PAIR = 2 * HD
QKV = 3 * PAIR
TILE = 128

epsilon = 1e-05
masked_score = -1e30
SCALE = HD ** (-0.5)
F32 = jnp.float32
BF = jnp.bfloat16
NT = (((1,), (1,)), ((), ()))
TN = (((0,), (0,)), ((), ()))
TANH_A = 0.7978845608028654
TANH_B = 0.044715
VMEM_GRANT = 66584576
SMALL = ((0, 0, 7), (7, 8, 4), (11, 16, 2))
VMEM = pl.BlockSpec(memory_space=pltpu.VMEM)
SMEM = pl.BlockSpec(memory_space=pltpu.SMEM)
ANY = pl.BlockSpec(memory_space=pl.ANY)


class Sizes:
    def __init__(self, shape, tensor, dp):
        self.blocks, self.samples, self.feats, self.width = shape
        self.tensor, self.dp = tensor, dp
        self.rows = self.blocks * self.samples * self.feats
        self.own_feats = self.feats // tensor
        self.run = self.blocks * self.samples
        self.chunk = self.own_feats * self.run
        self.group = tensor * self.run
        self.block_rows = self.samples * self.feats
        self.fast = tensor == 4 and dp == 8


def places(z):
    tensor_at = lax.axis_index("tensor")
    dp_at = lax.axis_index("dp")
    return tensor_at, lax.rem(dp_at, 2), lax.div(dp_at, 2)


def dot(a, b):
    return jnp.dot(a, b, preferred_element_type=F32)


def dot_nt(a, b):
    return lax.dot_general(a, b, NT, preferred_element_type=F32)


def dot_tn(a, b):
    return lax.dot_general(a, b, TN, preferred_element_type=F32)


def normal_rows(x):
    centre = x - jnp.mean(x, axis=-1, keepdims=True)
    spread = jnp.mean(centre * centre, axis=-1, keepdims=True)
    rate = lax.rsqrt(spread + epsilon)
    return centre * rate, rate


def over_rows(rows, fn, carry=0, step=64):
    for at in range(rows // step):
        carry = fn(slice(at * step, (at + 1) * step), carry)
    return carry


def fold(x):
    return jnp.sum(x.reshape(-1, 8, x.shape[-1]), axis=0)


def total(x):
    return jnp.sum(x, axis=0, keepdims=True)


def put_strips(strips, rows, value):
    for lane in range(value.shape[1] // TILE):
        strips[lane, rows, :] = value[:, lane * TILE : (lane + 1) * TILE]


def get_strips(strips, rows):
    return jnp.concatenate([strips[lane, rows, :] for lane in range(strips.shape[0])], axis=1)


def feature_slot(sz, tensor_at, at, slot):
    return (tensor_at ^ at) * sz.own_feats + slot


def spread_out(sz, tensor_at, wide, chunks):
    for at in range(sz.tensor):
        for slot in range(sz.own_feats):
            first = feature_slot(sz, tensor_at, at, slot)
            for lane in range(sz.width // TILE):
                rows = wide[lane, pl.ds(first, sz.run, stride=sz.feats), :]
                chunks[at][
                    slot * sz.run : (slot + 1) * sz.run, lane * TILE : (lane + 1) * TILE
                ] = rows.astype(BF)


def bring_back(sz, tensor_at, chunks, wide):
    for at in range(sz.tensor):
        for slot in range(sz.own_feats):
            first = feature_slot(sz, tensor_at, at, slot)
            for lane in range(sz.width // TILE):
                rows = chunks[at][
                    slot * sz.run : (slot + 1) * sz.run, lane * TILE : (lane + 1) * TILE
                ]
                wide[lane, pl.ds(first, sz.run, stride=sz.feats), :] = rows.astype(F32)


def by_feature(sz, chunks, x):
    for at in range(sz.tensor):
        for slot in range(sz.own_feats):
            first = slot * sz.group + at * sz.run
            x[first : first + sz.run, :] = chunks[at][slot * sz.run : (slot + 1) * sz.run, :]


def to_chunks(sz, value, chunks):
    for at in range(sz.tensor):
        for slot in range(sz.own_feats):
            first = slot * sz.group + at * sz.run
            chunks[at][slot * sz.run : (slot + 1) * sz.run, :] = value[
                first : first + sz.run
            ].astype(BF)


def where_halves(core):
    other = 1 - core
    return (
        (1 + core, core),
        (2 - core, core),
        (3, core),
        (1 + other, other),
        (2 - other, other),
        (3, other),
    )


def load_unit(sz, layer_at, member, parts, w, w_out, sems, core):
    pairs = []
    if not sz.fast:
        pairs += [(parts[0], w), (parts[1], w_out)]
    else:
        qkv, out = parts[:2]
        for at in range(3):
            pairs.append((qkv.at[layer_at, at], w.at[:, pl.ds(at * PAIR, PAIR)]))
        pairs.append((out.at[layer_at], w_out.at[pl.ds(0, PAIR), :]))
        half_rows = sz.width // 2
        for source, (piece, half) in zip(parts[2:], where_halves(core)):
            if member is not None:
                source = source.at[member]
            start = pl.multiple_of(half * half_rows, half_rows)
            first = pl.multiple_of(piece * QKV, TILE)
            pairs.append(
                (source.at[:, pl.ds(0, QKV)], w.at[pl.ds(start, half_rows), pl.ds(first, QKV)])
            )
            first = pl.multiple_of(piece * PAIR, TILE)
            for block in range(half_rows // TILE):
                lanes = pl.ds(pl.multiple_of(start + block * TILE, TILE), TILE)
                pairs.append(
                    (
                        source.at[pl.ds(block * TILE, TILE), pl.ds(QKV, PAIR)],
                        w_out.at[pl.ds(first, PAIR), lanes],
                    )
                )
    return begin(pairs, sems)


def begin(pairs, sems):
    copies = []
    for source, target in pairs:
        copies.append(pltpu.make_async_copy(source, target, sems.at[len(copies)]))
        copies[-1].start()
    return copies


def finish(copies):
    for copy in copies:
        copy.wait()


def load_mlp(sz, layer_at, parts, up, down, sems, core):
    pairs = []
    if not sz.fast:
        pairs += [(parts[0], up), (parts[1], down)]
    else:
        width = sz.width
        pairs.append((parts[0].at[layer_at], up.at[:, pl.ds(0, width)]))
        pairs.append((parts[1].at[layer_at], down.at[pl.ds(0, width), :]))
        half_rows = width // 2
        for source, (piece, half) in zip(parts[2:], where_halves(core)):
            start = pl.multiple_of(half * half_rows, half_rows)
            first = pl.multiple_of(piece * width, width)
            pairs.append(
                (source.at[0], up.at[pl.ds(start, half_rows), pl.ds(first, width)])
            )
            rows = pl.ds(pl.multiple_of(first + start, half_rows), half_rows)
            pairs.append((source.at[1], down.at[rows, :]))
    return begin(pairs, sems)


def put_grad(sz, grads, outs, piece, member, core, z, direct=False):
    if not sz.fast:
        outs[0][piece, member] = grads[...]
        return
    mine, theirs = outs
    if direct or piece in (0, 3):
        at_mine = at_theirs = piece
    elif piece == 1:
        at_mine, at_theirs = 1 + core, 2 - core
    else:
        at_mine, at_theirs = 2 - core, 1 + core
    for place, near in enumerate((0, 1, 2, 3) if direct else (0, 2, 1, 3)):
        first = (z ^ near) * 128
        rows_mine = pl.ds(pl.multiple_of(first + core * 64, 64), 64)
        rows_theirs = pl.ds(pl.multiple_of(first + (1 - core) * 64, 64), 64)
        mine[at_mine, place, member] = grads[rows_mine, :]
        theirs[at_theirs, place, member] = grads[rows_theirs, :]
    flush(mine, at_mine, slice(None), member)
    flush(theirs, at_theirs, slice(None), member)


def head_masks():
    lane = lax.broadcasted_iota(jnp.int32, (1, PAIR), 1)
    return lane < HD, lane >= HD


def sample_bias(sz, tensor_at, tasks, lengths, bias):
    def of(index):
        run_at = index // sz.run
        block = (index // sz.samples) % sz.blocks
        sample = (run_at ^ tensor_at) * sz.samples + index % sz.samples
        task = jnp.zeros_like(index)
        length = jnp.zeros_like(index)
        for at in range(sz.blocks):
            task = jnp.where(block == at, tasks[at], task)
            length = jnp.where(block == at, lengths[at], length)
        return task, sample < length

    row_task, unused = of(lax.broadcasted_iota(jnp.int32, (sz.group, 1), 0))
    key_task, key_live = of(lax.broadcasted_iota(jnp.int32, (1, sz.group), 1))
    key_task = jnp.where(key_live, key_task, -1)
    bias[...] = jnp.where(row_task == key_task, 0.0, masked_score)


def feature_bias(sz, length):
    row = lax.broadcasted_iota(jnp.int32, (TILE, TILE), 0)
    key = lax.broadcasted_iota(jnp.int32, (TILE, TILE), 1)
    same = (row // sz.feats) == (key // sz.feats)
    return jnp.where(same & (key % sz.feats < length), 0.0, masked_score)


def attend(proj, piece, jobs, probs, mixed):
    masks = head_masks()
    first = piece * QKV
    scores = []
    for rows, bias, place in jobs:
        query = proj[rows, first : first + PAIR]
        key = proj[rows, first + PAIR : first + 2 * PAIR]
        for mask in masks:
            scores.append(dot_nt(jnp.where(mask, query, 0) * SCALE, key) + bias)
    tops = [jnp.max(part, axis=-1, keepdims=True) for part in scores]
    weights = [jnp.exp(part - top) for part, top in zip(scores, tops)]
    shares = [1.0 / jnp.sum(part, axis=-1, keepdims=True) for part in weights]
    weights = [(part * share).astype(BF) for part, share in zip(weights, shares)]
    for at, (rows, bias, place) in enumerate(jobs):
        value = proj[rows, first + 2 * PAIR : first + QKV]
        pair = weights[2 * at : 2 * at + 2]
        for head in range(2):
            probs[piece, place, head] = pair[head]
        mixed[rows, piece * PAIR : (piece + 1) * PAIR] = jnp.where(
            masks[0], dot(pair[0], value), dot(pair[1], value)
        ).astype(BF)
    flush(probs, piece)
    flush(mixed, slice(None), pl.ds(piece * PAIR, PAIR))


def attend_back(proj, piece, jobs, probs, mixed_grad, proj_grad):
    masks = head_masks()
    first = piece * QKV
    head_grads, weights, weight_grads = [], [], []
    for rows, place in jobs:
        grad = mixed_grad[rows, piece * PAIR : (piece + 1) * PAIR]
        value = proj[rows, first + 2 * PAIR : first + QKV]
        for head, mask in enumerate(masks):
            head_grads.append(jnp.where(mask, grad, 0))
            weights.append(probs[piece, place, head])
            weight_grads.append(dot_nt(head_grads[-1], value))
    score_grads = []
    for low, grad in zip(weights, weight_grads):
        wide = low.astype(F32)
        product = wide * grad
        score_grads.append((product - wide * jnp.sum(product, axis=-1, keepdims=True)).astype(BF))
    for at, (rows, place) in enumerate(jobs):
        query = proj[rows, first : first + PAIR]
        key = proj[rows, first + PAIR : first + 2 * PAIR]
        one, two = score_grads[2 * at : 2 * at + 2]
        queries = jnp.where(masks[0], dot(one, key), dot(two, key)) * SCALE
        keys = dot_tn(one, jnp.where(masks[0], query, 0))
        keys = (keys + dot_tn(two, jnp.where(masks[1], query, 0))) * SCALE
        values = dot_tn(weights[2 * at], head_grads[2 * at])
        values = values + dot_tn(weights[2 * at + 1], head_grads[2 * at + 1])
        proj_grad[rows, first : first + PAIR] = queries.astype(BF)
        proj_grad[rows, first + PAIR : first + 2 * PAIR] = keys.astype(BF)
        proj_grad[rows, first + 2 * PAIR : first + QKV] = values.astype(BF)
    flush(proj_grad, slice(None), pl.ds(first, QKV))


def norm_back_rows(state, incoming, gain):
    xhat, rate = normal_rows(state)
    inner = incoming * gain
    back = rate * (
        inner
        - jnp.mean(inner, axis=-1, keepdims=True)
        - xhat * jnp.mean(inner * xhat, axis=-1, keepdims=True)
    )
    return xhat, back


def pack_copies(sz, layer_at, qkv, out, sent, core):
    half = sz.width // 2
    rows = pl.ds(pl.multiple_of(core * half, half), half)
    pairs = []
    for at in range(3):
        pairs.append((qkv.at[layer_at, at, rows, :], sent.at[:, pl.ds(at * PAIR, PAIR)]))
    for block in range(half // TILE):
        lanes = pl.ds(pl.multiple_of(core * half + block * TILE, TILE), TILE)
        pairs.append(
            (out.at[layer_at, :, lanes], sent.at[pl.ds(block * TILE, TILE), pl.ds(QKV, PAIR)])
        )
    return pairs


def start_kernel(sz, tokens, gains, shifts, qkv, out, *rest):
    chunks, rest = rest[: sz.tensor], rest[sz.tensor :]
    tensor_at, core, z = places(sz)
    copies = []
    if sz.fast:
        sent, strips, sems = rest
        copies = begin(pack_copies(sz, 0, qkv, out, sent, core), sems)
    else:
        (strips,) = rest

    def rows_of(rows, kept):
        xhat, unused = normal_rows(tokens[rows, :].astype(F32))
        put_strips(strips, rows, xhat * gains[0, 0:1, :] + shifts[0, 0:1, :])
        return kept

    over_rows(sz.rows, rows_of)
    spread_out(sz, tensor_at, strips, chunks)
    finish(copies)


def pack_units_kernel(sz, layer_at, *rest):
    operands, sent, sems = rest[:-2], rest[-2], rest[-1]
    tensor_at, core, z = places(sz)
    pairs = []
    count = len(operands) // 2
    for unit in range(count):
        target = sent if count == 1 else sent.at[unit]
        pairs += pack_copies(
            sz, layer_at, operands[2 * unit], operands[2 * unit + 1], target, core
        )
    finish(begin(pairs, sems))


def pack_mlp_kernel(sz, layer_at, up, down, sent, sems):
    tensor_at, core, z = places(sz)
    half = sz.width // 2
    rows = pl.ds(pl.multiple_of(core * half, half), half)
    pairs = [(w.at[layer_at, rows, :], sent.at[at]) for at, w in enumerate((up, down))]
    finish(begin(pairs, sems))


def nothing_kernel(sz, *rest):
    pass


def send_near_kernel(sz, mine, other, rows, rows_other, *outs):
    kept = outs[-1]
    kept[...] = jnp.zeros_like(kept)
    for layer_at in range(L):
        for at, first, count in SMALL:
            here = slice(24 * layer_at + first, 24 * layer_at + first + count)
            there = slice(16 * layer_at + at, 16 * layer_at + at + count)
            kept[there, :] = rows[here, :] + rows_other[here, :]
    small = kept[...].astype(BF)
    kept[...] = small.astype(F32)
    for piece in range(1, PIECES):
        out = outs[piece - 1]
        for near in range(4):
            value = mine[piece, near, 0].astype(F32) + other[piece, near, 0].astype(F32)
            out[near * 64 : near * 64 + 64, :] = value.astype(BF)
        out[256:, :] = small


def pairwise(one, two, three, four):
    return (one + two) + (three + four)


def send_far_kernel(sz, *refs):
    first, last, small, outs = refs[:5], refs[5:10], refs[10], refs[11:]
    kept, rows, sends = outs[0], outs[1], outs[2:]

    def value(unit, at, near):
        mine, other, *got = unit
        out = mine[0, near, 0].astype(F32) + other[0, near, 0].astype(F32)
        for one in got:
            got_here = one[0, near, 0] if at == 0 else one[near * 64 : near * 64 + 64, :]
            out = out + got_here.astype(F32)
        return out

    x, y, d = (one[256:, :].astype(F32) for one in last[2:])
    low = pairwise(small[...], x, y, d).astype(BF)
    rows[...] = low.astype(F32)
    for at, unit in enumerate((first, last)):
        kept[at] = value(unit, at, 0)
        for near in range(1, 4):
            sends[near - 1][at * 64 : at * 64 + 64, :] = value(unit, at, near).astype(BF)
    for near in range(1, 4):
        sends[near - 1][128:, :] = low


def last_sums_kernel(sz, *refs):
    kept, rows, one, two, three, mlp, mlp_got, upper_mlp, upper_mlp_got = refs[:9]
    upper, upper_got = refs[9:11]
    s_qkv, s_out, f_qkv, f_out, up, down, gain, shift, bias, up_bias = refs[11:]
    small = pairwise(rows[...], *(got[128:, :].astype(F32) for got in (one, two, three)))

    def attention(layer_at, value, qkv, out):
        for at in range(3):
            qkv[layer_at, at] = value[:, at * PAIR : (at + 1) * PAIR]
        out[layer_at] = value[:, QKV:]

    for at, (qkv, out) in enumerate(((f_qkv, f_out), (s_qkv, s_out))):
        value = kept[at]
        for got in (one, two, three):
            value = value + got[at * 64 : at * 64 + 64, :].astype(F32)
        attention(0, value, qkv, out)
        attention(1, upper[0, 0, at] + upper_got[0, 0, at].astype(F32), qkv, out)
    for at, w in enumerate((up, down)):
        w[0] = mlp[0, 0, at] + mlp_got[0, 0, at].astype(F32)
        w[1] = upper_mlp[0, 0, at] + upper_mlp_got[0, 0, at].astype(F32)
    for layer_at in range(L):
        m, f, s = (16 * layer_at + at for at, first, count in SMALL)
        for out, places_in in ((gain, (s, f, m)), (shift, (s + 1, f + 1, m + 1)),
                               (bias, (f + 3, f + 2, m + 2))):
            for at, row in enumerate(places_in):
                out[at, layer_at : layer_at + 1, :] = small[row : row + 1]
        for piece in range(PIECES):
            lanes = slice(piece * sz.width, (piece + 1) * sz.width)
            row = m + 3 + piece
            up_bias[layer_at : layer_at + 1, lanes] = small[row : row + 1]


def unit_parts(sz):
    return 8 if sz.fast else 2


def sample_kernel(sz, layer_at, member, tasks, lengths, *rest):
    n, parts = sz.tensor, unit_parts(sz)
    chunks, weights = rest[:n], rest[n : n + parts]
    outs = rest[n + parts :]
    back, proj, mixed, probs = outs[:n], outs[n], outs[n + 1], outs[n + 2]
    x, bias, w, w_out, sems = outs[n + 3 :]
    tensor_at, core, z = places(sz)
    copies = load_unit(sz, layer_at, member, weights, w, w_out, sems, core)
    by_feature(sz, chunks, x)
    sample_bias(sz, tensor_at, tasks, lengths, bias)
    finish(copies)
    proj[...] = dot(x[...], w[...]).astype(BF)
    flush(proj)
    jobs = [
        (slice(slot * sz.group, (slot + 1) * sz.group), bias[...], slot)
        for slot in range(sz.own_feats)
    ]
    for piece in range(PIECES):
        attend(proj, piece, jobs, probs, mixed)
    to_chunks(sz, dot(mixed[...], w_out[...]), back)


def feature_kernel(sz, layer_at, member, lengths, state, gains, shifts, out_bias, *rest):
    n, parts = sz.tensor, unit_parts(sz)
    chunks, weights = rest[:n], rest[n : n + parts]
    state_1, state_2, normed_m, proj, mixed, probs = rest[n + parts : n + parts + 6]
    strips, wide, normed, w, w_out, sems = rest[n + parts + 6 :]
    tensor_at, core, z = places(sz)
    copies = load_unit(sz, layer_at, member, weights, w, w_out, sems, core)
    bring_back(sz, tensor_at, chunks, strips)
    at = slice(layer_at, layer_at + 1)

    def before(rows, kept):
        value = state[rows, :].astype(F32) + get_strips(strips, rows) + out_bias[0, at, :]
        state_1[rows, :] = value
        xhat, unused = normal_rows(value)
        normed[rows, :] = (xhat * gains[1, at, :] + shifts[1, at, :]).astype(BF)
        return kept

    over_rows(sz.rows, before)
    biases = [feature_bias(sz, lengths[block]) for block in range(sz.blocks)]
    jobs = [
        (slice(tile * TILE, (tile + 1) * TILE), biases[tile * TILE // sz.block_rows], tile)
        for tile in range(sz.rows // TILE)
    ]
    finish(copies)
    flush(state_1)
    proj[...] = dot(normed[...], w[...]).astype(BF)
    flush(proj)
    for piece in range(PIECES):
        attend(proj, piece, jobs, probs, mixed)
    wide[...] = dot(mixed[...], w_out[...])

    def after(rows, kept):
        value = state_1[rows, :] + wide[rows, :] + out_bias[1, at, :]
        state_2[rows, :] = value
        xhat, unused = normal_rows(value)
        normed_m[rows, :] = (xhat * gains[2, at, :] + shifts[2, at, :]).astype(BF)
        return kept

    over_rows(sz.rows, after)


def up_bias_rows(sz, tensor_at, piece):
    return (tensor_at ^ piece) if sz.fast else piece


def mlp_kernel(sz, layer_at, state_2, normed_m, up_bias, gains, shifts, out_bias, *rest):
    n = sz.tensor
    parts = 8 if sz.fast else 2
    weights, (state_3, *chunks) = rest[:parts], rest[parts : parts + 1 + n]
    strips, wide, hidden, up, down, sems = rest[parts + 1 + n :]
    tensor_at, core, z = places(sz)
    finish(load_mlp(sz, layer_at, weights, up, down, sems, core))
    width = sz.width
    for piece in range(PIECES):
        lanes = slice(piece * width, (piece + 1) * width)
        wide[...] = dot(normed_m[...], up[:, lanes])
        shift = up_bias[layer_at, pl.ds(up_bias_rows(sz, tensor_at, piece), 1), :]
        value = wide[...] + shift
        half = 0.5 + 0.5 * jnp.tanh(value * (TANH_A + TANH_A * TANH_B * (value * value)))
        hidden[:, lanes] = (value * half).astype(BF)
    wide[...] = dot(hidden[...], down[...])
    at = slice(layer_at, layer_at + 1)
    later = slice(layer_at + 1, layer_at + 2)

    def after(rows, kept):
        value = state_2[rows, :] + wide[rows, :] + out_bias[2, at, :]
        state_3[rows, :] = value
        xhat, unused = normal_rows(value)
        put_strips(strips, rows, xhat * gains[0, later, :] + shifts[0, later, :])
        return kept

    over_rows(sz.rows, after)
    spread_out(sz, tensor_at, strips, chunks)


def mlp_back(
    sz, layer_at, grad, state_2, normed_m, up_bias, gains, up, down, low, wide, other, hidden,
    up_grad, grads, grad_out, outs, small,
):
    tensor_at, core, z = places(sz)
    at = slice(layer_at, layer_at + 1)
    width = sz.width
    nothing = jnp.zeros((8, width), F32)

    def lower(rows, kept):
        part = grad[rows, :].astype(BF)
        low[rows, :] = part
        return kept + fold(part.astype(F32))

    small[...] = jnp.zeros_like(small)
    small[2:3, :] = total(over_rows(sz.rows, lower, nothing))
    for piece in range(PIECES):
        lanes = slice(piece * width, (piece + 1) * width)
        name = up_bias_rows(sz, tensor_at, piece)
        wide[...] = dot(normed_m[...], up[:, lanes])
        other[...] = dot_nt(low[...], down[lanes, :])
        shift = up_bias[layer_at, pl.ds(name, 1), :]
        value = wide[...] + shift
        square = value * value
        half = 0.5 + 0.5 * jnp.tanh(value * (TANH_A + TANH_A * TANH_B * square))
        full = value * half
        hidden[:, lanes] = full.astype(BF)
        slope = half + full * (1.0 - half) * (2.0 * TANH_A + 6.0 * TANH_A * TANH_B * square)
        part = (other[...] * slope).astype(BF)
        up_grad[:, lanes] = part
        small[pl.ds(3 + name, 1), :] = total(fold(part.astype(F32)))
        grads[...] = dot_tn(normed_m[...], up_grad[:, lanes]).astype(BF)
        put_grad(sz, grads, outs, piece, 0, core, z)
        grads[...] = dot_tn(low[...], hidden[:, lanes]).astype(BF)
        put_grad(sz, grads, outs, piece, 1, core, z)
    wide[...] = dot_nt(up_grad[...], up[...])

    def back(rows, kept):
        incoming = wide[rows, :]
        xhat, change = norm_back_rows(state_2[rows, :], incoming, gains[2, at, :])
        grad_out[rows, :] = grad[rows, :] + change
        return kept[0] + fold(incoming * xhat), kept[1] + fold(incoming)

    gain_sum, shift_sum = over_rows(sz.rows, back, (nothing, nothing))
    small[0:1, :] = total(gain_sum)
    small[1:2, :] = total(shift_sum)


def last_mlp_kernel(
    sz, layer_at, sample_lens, feature_lens, cotangent, state_2, normed_m, up_bias, gains, out_bias,
    *rest,
):
    parts, halves = unit_parts(sz), 2 if sz.fast else 1
    weights, rest = rest[:parts], rest[parts:]
    output, grad_out, small = rest[:3]
    outs = rest[3 : 3 + halves]
    grad, wide, other, low, hidden, up_grad, grads, up, down, sems = rest[3 + halves :]
    tensor_at, core, z = places(sz)
    copies = load_mlp(sz, layer_at, weights, up, down, sems, core)
    step = 64

    def live_rows(rows, kept):
        index = rows.start + lax.broadcasted_iota(jnp.int32, (step, 1), 0)
        block = index // sz.block_rows
        sample = tensor_at * sz.samples + (index // sz.feats) % sz.samples
        sample_len = jnp.zeros_like(index)
        feature_len = jnp.zeros_like(index)
        for at in range(sz.blocks):
            sample_len = jnp.where(block == at, sample_lens[at], sample_len)
            feature_len = jnp.where(block == at, feature_lens[at], feature_len)
        live = (sample < sample_len) & (index % sz.feats < feature_len)
        grad[rows, :] = jnp.where(live, cotangent[rows, :].astype(F32), 0.0)
        return kept

    over_rows(sz.rows, live_rows, 0, step)
    finish(copies)
    mlp_back(
        sz, layer_at, grad, state_2, normed_m, up_bias, gains, up, down, low, wide, other, hidden,
        up_grad, grads, grad_out, outs, small,
    )
    at = slice(layer_at, layer_at + 1)
    other[...] = dot(hidden[...], down[...])

    def after(rows, kept):
        value = state_2[rows, :] + other[rows, :] + out_bias[2, at, :]
        output[rows, :] = value.astype(BF)
        return kept

    over_rows(sz.rows, after)


def mlp_back_kernel(
    sz, layer_at, grad_in, state_3, state_2, normed_m, up_bias, gains, *rest
):
    n = sz.tensor
    parts, halves = unit_parts(sz), 2 if sz.fast else 1
    chunks, weights, rest = rest[:n], rest[n : n + parts], rest[n + parts :]
    grad_out, small = rest[:2]
    outs = rest[2 : 2 + halves]
    grad, strips, wide, other, low, hidden, up_grad, grads, up, down, sems = rest[2 + halves :]
    tensor_at, core, z = places(sz)
    copies = load_mlp(sz, layer_at, weights, up, down, sems, core)
    sample_norm_back(sz, layer_at + 1, tensor_at, grad_in, state_3, chunks, gains, strips, grad)
    finish(copies)
    mlp_back(
        sz, layer_at, grad, state_2, normed_m, up_bias, gains, up, down, low, wide, other, hidden,
        up_grad, grads, grad_out, outs, small,
    )


def sample_norm_back(sz, layer_at, tensor_at, grad_in, state, chunks, gains, strips, grad):
    bring_back(sz, tensor_at, chunks, strips)
    at = slice(layer_at, layer_at + 1)

    def back(rows, kept):
        incoming = get_strips(strips, rows)
        xhat, change = norm_back_rows(state[rows, :].astype(F32), incoming, gains[0, at, :])
        grad[rows, :] = grad_in[rows, :] + change
        return kept

    over_rows(sz.rows, back)


def last_norm_kernel(sz, grad_in, state, gains, *rest):
    chunks, (grad, strips) = rest[: sz.tensor], rest[sz.tensor :]
    tensor_at, core, z = places(sz)
    sample_norm_back(sz, 0, tensor_at, grad_in, state, chunks, gains, strips, grad)


def feature_back_kernel(sz, layer_at, member, grad, state_1, proj, probs, gains, shifts, *rest):
    n, parts = sz.tensor, unit_parts(sz)
    weights, rest = rest[:parts], rest[parts:]
    grad_out, low, proj_grad, normed, small = rest[:5]
    chunks = rest[5 : 5 + n]
    mixed_grad, strips, wide, w, w_out, sems = rest[5 + n :]
    tensor_at, core, z = places(sz)
    copies = load_unit(sz, layer_at, member, weights, w, w_out, sems, core)
    at = slice(layer_at, layer_at + 1)
    nothing = jnp.zeros((8, sz.width), F32)

    def lower(rows, kept):
        part = grad[rows, :].astype(BF)
        low[rows, :] = part
        return kept + fold(part.astype(F32))

    small[...] = jnp.zeros_like(small)
    small[2:3, :] = total(over_rows(sz.rows, lower, nothing))
    flush(low)
    finish(copies)
    mixed_grad[...] = dot_nt(low[...], w_out[...]).astype(BF)
    jobs = [(slice(tile * TILE, (tile + 1) * TILE), tile) for tile in range(sz.rows // TILE)]
    for piece in range(PIECES):
        attend_back(proj, piece, jobs, probs, mixed_grad, proj_grad)
    wide[...] = dot_nt(proj_grad[...], w[...])

    def back(rows, kept):
        incoming = wide[rows, :]
        gain = gains[1, at, :]
        xhat, change = norm_back_rows(state_1[rows, :], incoming, gain)
        value = grad[rows, :] + change
        grad_out[rows, :] = value
        put_strips(strips, rows, value)
        normed[rows, :] = (xhat * gain + shifts[1, at, :]).astype(BF)
        rounded = value.astype(BF).astype(F32)
        return (
            kept[0] + fold(incoming * xhat),
            kept[1] + fold(incoming),
            kept[2] + fold(rounded),
        )

    sums = over_rows(sz.rows, back, (nothing, nothing, nothing))
    small[0:1, :] = total(sums[0])
    small[1:2, :] = total(sums[1])
    small[3:4, :] = total(sums[2])
    spread_out(sz, tensor_at, strips, chunks)


def sample_back_kernel(sz, layer_at, member, proj, probs, gains, shifts, *rest):
    n, parts = sz.tensor, unit_parts(sz)
    chunks, rows_in, rest = rest[:n], rest[n : 2 * n], rest[2 * n :]
    weights, rest = rest[:parts], rest[parts:]
    back, low, proj_grad, small = rest[:n], rest[n], rest[n + 1], rest[n + 2]
    mixed_grad, normed, w, w_out, sems = rest[n + 3 :]
    tensor_at, core, z = places(sz)
    copies = load_unit(sz, layer_at, member, weights, w, w_out, sems, core)
    by_feature(sz, chunks, low)
    by_feature(sz, rows_in, normed)
    flush(low)
    finish(copies)
    mixed_grad[...] = dot_nt(low[...], w_out[...]).astype(BF)
    jobs = [
        (slice(slot * sz.group, (slot + 1) * sz.group), slot) for slot in range(sz.own_feats)
    ]
    for piece in range(PIECES):
        attend_back(proj, piece, jobs, probs, mixed_grad, proj_grad)
    normed_grad = dot_nt(proj_grad[...], w[...])
    to_chunks(sz, normed_grad, back)
    at = slice(layer_at, layer_at + 1)
    shift_sum = total(fold(normed_grad))
    gain_sum = total(fold(normed_grad * normed[...].astype(F32)))
    small[...] = jnp.zeros_like(small)
    small[0:1, :] = (gain_sum - shifts[0, at, :] * shift_sum) / gains[0, at, :]
    small[1:2, :] = shift_sum


def matrix_grad_kernel(sz, count, direct, proj_grad, low, mixed, *rest):
    halves = 2 if sz.fast else 1
    rows, outs, rest = rest[:count], rest[count : count + halves], rest[count + halves :]
    tensor_at, core, z = places(sz)
    if count == 1:
        (grads,) = rest
        (normed,) = rows
    else:
        grads, normed = rest
        by_feature(sz, rows, normed)
    for piece in range(PIECES):
        lanes = slice(piece * QKV, (piece + 1) * QKV)
        grads[piece, :, :QKV] = dot_tn(normed[...], proj_grad[:, lanes]).astype(BF)
        lanes = slice(piece * PAIR, (piece + 1) * PAIR)
        grads[piece, :, QKV:] = dot_tn(low[...], mixed[:, lanes]).astype(BF)
        put_grad(sz, grads.at[piece], outs, piece, 0, core, z, direct)


def shaped(shape, dtype):
    return jax.ShapeDtypeStruct(shape, dtype)


class Early:
    def __init__(self, target, held, sems):
        self.target, self.held, self.sems, self.copies = target, held, sems, []
        self.shape, self.dtype = held.shape, held.dtype

    def __getitem__(self, index):
        return self.held[index]

    def __setitem__(self, index, value):
        self.held[index] = value

    def flush(self, *index):
        source, target = self.held, self.target
        if index:
            source, target = source.at[index], target.at[index]
        copy = pltpu.make_async_copy(source, target, self.sems.at[len(self.copies)])
        copy.start()
        self.copies.append(copy)


def flush(ref, *index):
    if isinstance(ref, Early):
        ref.flush(*index)


class Job:
    def __init__(self, groups, outs, split, then):
        self.groups, self.outs, self.split, self.then = groups, outs, split, then
        self.terms = [term for group in groups for term in group]

    def scratch(self):
        shapes = [
            (count, array.shape[1], members, *array.shape[3:])
            for array, first, count, member, members in self.terms
        ]
        return [
            pltpu.VMEM(shape, term[0].dtype) for shape, term in zip(shapes, self.terms)
        ] + [pltpu.SemaphoreType.DMA((len(self.terms),))]

    def start(self, refs, scratch):
        pairs = []
        for ref, term, target in zip(refs, self.terms, scratch):
            array, first, count, member, members = term
            pairs.append((ref.at[pl.ds(first, count), :, pl.ds(member, members)], target))
        return begin(pairs, scratch[-1])

    def finish(self, copies, outs, scratch):
        finish(copies)
        at = place = 0
        for group in self.groups:
            refs = scratch[at : at + len(group)]
            at += len(group)
            lead, near, members = refs[0].shape[:3]
            for one in range(lead):
                for two in range(near):
                    for member in range(members):
                        value = refs[0][one, two, member].astype(F32)
                        for ref in refs[1:]:
                            value = value + ref[one, two, member].astype(F32)
                        out, index, lead_at = outs[0], two, one
                        if self.split == 1:
                            out, lead_at = outs[one], 0
                        elif self.split and two >= near // 2:
                            out, index = outs[1], two - near // 2
                        out[lead_at, index, place + member] = value.astype(out.dtype)
            place += members


def launch(kernel, name, operands, specs, outs, scratch, micros, after=(), jobs=(), early=None):
    after, outs = list(after), list(outs)
    sums = [term[0] for job in jobs for term in job.terms]
    job_outs = [out for job in jobs for out in job.outs]
    job_scratch = [job.scratch() for job in jobs]
    count, plain = len(operands), len(scratch)
    skip = count + len(sums) + len(after)
    early = early or {}
    held = []
    for at, parts in early.items():
        held += [pltpu.VMEM(outs[at].shape, outs[at].dtype), pltpu.SemaphoreType.DMA((parts,))]

    def whole(*refs):
        given, results = refs[count : count + len(sums)], refs[skip : skip + len(outs)]
        extra = refs[skip + len(outs) : skip + len(outs) + len(job_outs)]
        rest = refs[skip + len(outs) + len(job_outs) :]
        own, rest = rest[:plain], rest[plain:]
        results = list(results)
        for at in early:
            results[at] = Early(results[at], *rest[:2])
            rest = rest[2:]
        started = []
        for job, buffers in zip(jobs, job_scratch):
            mine, rest = rest[: len(buffers)], rest[len(buffers) :]
            started.append((job, mine, job.start(given[: len(job.terms)], mine)))
            given = given[len(job.terms) :]
        kernel(*refs[:count], *results, *own)
        for job, mine, copies in started:
            job.finish(copies, extra[: len(job.outs)], mine)
            extra = extra[len(job.outs) :]
        for at in early:
            finish(results[at].copies)

    results = pl.pallas_call(
        whole,
        out_shape=outs + job_outs,
        in_specs=list(specs) + [ANY] * (len(sums) + len(after)),
        out_specs=[ANY if at in early else VMEM for at in range(len(outs))]
        + [VMEM] * len(job_outs),
        scratch_shapes=list(scratch) + held + [buffer for buffers in job_scratch for buffer in buffers],
        name=name,
        cost_estimate=pl.CostEstimate(
            flops=int(micros * 8e9), bytes_accessed=1_000_000, transcendentals=0
        ),
        compiler_params=pltpu.CompilerParams(vmem_limit_bytes=VMEM_GRANT),
    )(*operands, *sums, *after)
    results, extra = results[: len(outs)], results[len(outs) :]
    for job in jobs:
        job.then(*extra[: len(job.outs)])
        extra = extra[len(job.outs) :]
    return results


def grad_shapes(sz, members):
    if sz.fast:
        return [shaped((PIECES, 4, members, 64, sz.width), BF)] * 2
    return [shaped((PIECES, members, sz.width, sz.width), BF)]


def swap_cores(sz, v):
    return lax.ppermute(v, "dp", [(at, at ^ 1) for at in range(sz.dp)])


def swap_near(sz, v, distance):
    return lax.ppermute(v, "tensor", [(at, at ^ distance) for at in range(sz.tensor)])


def swap_far(sz, v, distance):
    return lax.ppermute(v, "dp", [(at, at ^ (2 * distance)) for at in range(sz.dp)])


def swap_turn(sz, v, turn):
    pairs = []
    for dp_at in range(sz.dp):
        distance = 1 + ((dp_at + turn) % 2)
        for at in range(sz.tensor):
            base = dp_at * sz.tensor
            pairs.append((base + at, base + (at ^ distance)))
    return lax.ppermute(v, ("dp", "tensor"), pairs)


def exchange(sz, chunks):
    return [chunks[0]] + [swap_near(sz, chunks[at], at) for at in range(1, sz.tensor)]


def gather_unit(sz, half):
    first = swap_turn(sz, half, 0)
    second = swap_turn(sz, half, 1)
    third = swap_turn(sz, first, 1)
    got = [first, second, third]
    return got + [swap_cores(sz, v) for v in got]


class Reduction:
    def __init__(self, sz, *units):
        self.sz = sz
        self.units = [(mine, swap_cores(sz, theirs), mine.shape[2]) for mine, theirs in units]
        self.members = sum(unit[2] for unit in self.units)
        self.tail = units[0][0].shape[3:]

    def groups(self, first, count, extra):
        groups, place = [], 0
        for mine, other, members in self.units:
            group = [(mine, first, count, 0, members), (other, first, count, 0, members)]
            group += [(array, at, count, place, members) for array, at in extra]
            groups.append(group)
            place += members
        return groups

    def shape(self, lead, near, dtype=BF):
        return shaped((lead, near, self.members, *self.tail), dtype)

    def job(self, step):
        return getattr(self, f"step_{step}")()

    def step_1(self):
        def then(out):
            self.sent, self.far = out, swap_turn(self.sz, out, 1)

        return Job(self.groups(2, 2, []), [self.shape(2, 4)], 0, then)

    def step_2(self):
        def then(out):
            self.sent, self.near = out, swap_turn(self.sz, out, 0)

        return Job(self.groups(1, 1, [(self.far, 1)]), [self.shape(1, 4)], 0, then)

    def step_3(self):
        def then(kept, out):
            self.kept, self.got = kept, swap_far(self.sz, out, 1)

        groups = self.groups(0, 1, [(self.far, 0), (self.near, 0)])
        return Job(groups, [self.shape(1, 2)] * 2, 2, then)

    def step_4(self):
        def then(kept, out):
            self.kept, self.got = kept, swap_far(self.sz, out, 2)

        groups = [[(array, 0, 1, 0, self.members) for array in (self.kept, self.got)]]
        return Job(groups, [self.shape(1, 1, F32), self.shape(1, 1)], 2, then)

    def result(self):
        return (self.kept + self.got.astype(F32)).reshape(self.members, *self.tail)


class Direct:
    def __init__(self, sz, mine, theirs):
        self.sz, self.mine = sz, mine
        self.other = swap_cores(sz, theirs)

    def job(self, step):
        def then(*sent):
            self.got = [swap_near(self.sz, v, at + 1) for at, v in enumerate(sent)]

        group = [(array, 1, 3, 0, 1) for array in (self.mine, self.other)]
        shape = shaped((1, *self.mine.shape[1:]), BF)
        return Job([group], [shape] * 3, 1, then)


def join(sz, *parts):
    one = object.__new__(Reduction)
    one.sz, one.tail = sz, (64, sz.width)
    plain = [not isinstance(part, Reduction) for part in parts]
    one.members = sum(p.shape[2] if alone else p.members for p, alone in zip(parts, plain))

    def step_3():
        def then(kept, out):
            one.kept, one.got = kept, swap_far(sz, out, 1)

        groups = []
        for part, alone in zip(parts, plain):
            if alone:
                groups.append([(part, 0, 1, 0, part.shape[2])])
            else:
                groups += part.groups(0, 1, [(part.far, 0), (part.near, 0)])
        return Job(groups, [one.shape(1, 2)] * 2, 2, then)

    one.step_3 = step_3
    return one


def reduce_whole(sz, full):
    members, width = full.shape[1], full.shape[2]
    full = full.transpose(1, 2, 0, 3)
    part = lax.psum_scatter(full, "dp", scatter_dimension=1, tiled=True)
    return lax.psum(part, "tensor").astype(F32)


def gathered_unit(qkv, out):
    qkv = lax.all_gather(qkv, "tensor", axis=2, tiled=True)
    out = lax.all_gather(out, "tensor", axis=0, tiled=True)
    width = qkv.shape[1]
    qkv = qkv.reshape(3, width, PIECES, PAIR).transpose(1, 2, 0, 3)
    return [qkv.reshape(width, PIECES * QKV), out]


def body(
    tokens,
    cotangent,
    block_task,
    sample_len,
    feature_len,
    norm_gain,
    norm_shift,
    sample_qkv,
    sample_out,
    feature_qkv,
    feature_out,
    out_bias,
    up_weight,
    up_bias,
    down_weight,
):
    shape = tokens.shape
    sz = Sizes(shape, lax.axis_size("tensor"), lax.axis_size("dp"))
    rows, width, n = sz.rows, sz.width, sz.tensor
    tokens = tokens.reshape(rows, width)
    cotangent = cotangent.reshape(rows, width)
    gains, shifts, biases = (
        jnp.transpose(v, (1, 0, 2)) for v in (norm_gain, norm_shift, out_bias)
    )
    up_rows = up_bias.reshape(L, PIECES, -1)
    qkvs = [jnp.transpose(v, (0, 2, 1, 3)) for v in (sample_qkv, feature_qkv)]
    outs = [sample_out, feature_out]
    part = functools.partial
    wide = pltpu.VMEM((rows, width), F32)
    strips = pltpu.VMEM((width // TILE, rows, TILE), F32)
    slim = pltpu.VMEM((rows, width), BF)
    dma = pltpu.SemaphoreType.DMA
    row_f32 = shaped((rows, width), F32)
    row_bf = shaped((rows, width), BF)
    chunk_shapes = [shaped((sz.chunk, width), BF)] * n
    proj_shape = shaped((rows, PIECES * QKV), BF)
    small_shape = shaped((8, width), F32)
    half_unit = (width // 2, width)
    sends = [shaped(half_unit, BF)] if sz.fast else []

    *chunks, sent = launch(
        part(start_kernel, sz), "start", (tokens, gains, shifts, qkvs[0], outs[0]),
        [VMEM] * 3 + [ANY] * 2, chunk_shapes + sends, [strips] + [dma((5,))] * len(sends), 3,
    ) if sz.fast else [*launch(
        part(start_kernel, sz), "start", (tokens, gains, shifts, qkvs[0], outs[0]),
        [VMEM] * 3 + [ANY] * 2, chunk_shapes, [strips], 3,
    ), None]

    units = [[None, None] for _ in range(L)]
    members = [[None, None]] + [[0, 1]] * (L - 1)
    mlps = [None] * L
    if sz.fast:

        def pack_units(layer_at, kinds, after):
            operands = []
            for kind in kinds:
                operands += [qkvs[kind], outs[kind]]
            shapes = half_unit if len(kinds) == 1 else (len(kinds), *half_unit)
            return launch(
                part(pack_units_kernel, sz, layer_at), f"pack_units_{layer_at}", operands,
                [ANY] * len(operands), [shaped(shapes, BF)], [dma((5 * len(kinds),))], 2, after,
            )[0]

        def pack_mlp(layer_at, after):
            return launch(
                part(pack_mlp_kernel, sz, layer_at), f"pack_mlp_{layer_at}",
                [up_weight, down_weight], [ANY] * 2, [shaped((2, *half_unit), BF)], [dma((2,))],
                2, after,
            )[0]

        got = gather_unit(sz, sent)
        units[0][0] = [qkvs[0], outs[0]] + got
    else:
        for layer_at in range(L):
            for kind in range(2):
                units[layer_at][kind] = gathered_unit(qkvs[kind][layer_at], outs[kind][layer_at])
            up = lax.all_gather(up_weight[layer_at], "tensor", axis=1, tiled=True)
            down = lax.all_gather(down_weight[layer_at], "tensor", axis=0, tiled=True)
            mlps[layer_at] = [up, down]

    def gather_units(layer_at, kinds, after):
        if not sz.fast:
            return []
        sent = pack_units(layer_at, kinds, after)
        got = gather_unit(sz, sent)
        for kind in kinds:
            units[layer_at][kind] = [qkvs[kind], outs[kind]] + got
        return [sent]

    def gather_mlp(layer_at, after):
        if not sz.fast:
            return []
        sent = pack_mlp(layer_at, after)
        mlps[layer_at] = [up_weight, down_weight] + gather_unit(sz, sent)
        return [sent]

    def arrived(parts, count):
        return parts[2 : 2 + count] if sz.fast else []

    unit_specs = [ANY] * unit_parts(sz)
    mlp_specs = [ANY] * unit_parts(sz)
    unit_scratch = [
        pltpu.VMEM((width, PIECES * QKV), BF),
        pltpu.VMEM((width, width), BF),
        dma((22 if sz.fast else 2,)),
    ]
    mlp_scratch = [
        pltpu.VMEM((width, PIECES * width), BF),
        pltpu.VMEM((PIECES * width, width), BF),
        dma((14 if sz.fast else 2,)),
    ]
    hidden = pltpu.VMEM((rows, PIECES * width), BF)
    square = pltpu.VMEM((width, width), BF)

    state = tokens
    kept = []
    for layer_at in range(L):
        entry = state
        got = exchange(sz, chunks)
        slots = sz.own_feats
        if layer_at == 0:
            began = gather_units(0, (1,), got[1:] + arrived(units[0][0], 2))
            began += gather_mlp(0, began + arrived(units[0][0], 3))
        else:
            began = gather_mlp(layer_at, got[1:] + arrived(units[layer_at][0], 2))
        *back, proj_s, mixed_s, probs_s = launch(
            part(sample_kernel, sz, layer_at, members[layer_at][0]), f"sample_{layer_at}",
            (block_task, sample_len, *got, *units[layer_at][0]),
            [SMEM] * 2 + [VMEM] * n + unit_specs,
            chunk_shapes
            + [proj_shape, row_bf, shaped((PIECES, slots, 2, sz.group, sz.group), BF)],
            [slim, pltpu.VMEM((sz.group, sz.group), F32), *unit_scratch],
            8, began, early={n: 1, n + 1: PIECES, n + 2: PIECES},
        )
        back = exchange(sz, back)
        tiles = rows // TILE
        state_1, state_2, normed_m, proj_f, mixed_f, probs_f = launch(
            part(feature_kernel, sz, layer_at, members[layer_at][1]), f"feature_{layer_at}",
            (feature_len, state, gains, shifts, biases, *back, *units[layer_at][1]),
            [SMEM] + [VMEM] * (4 + n) + unit_specs,
            [row_f32, row_f32, row_bf, proj_shape, row_bf,
             shaped((PIECES, tiles, 2, TILE, TILE), BF)],
            [strips, wide, slim, *unit_scratch],
            9,
        )
        if layer_at < L - 1:
            after = [state_2] + arrived(mlps[layer_at], 2)
            began = gather_units(layer_at + 1, (0, 1), after)
            state, *chunks = launch(
                part(mlp_kernel, sz, layer_at), f"mlp_{layer_at}",
                (state_2, normed_m, up_rows, gains, shifts, biases, *mlps[layer_at]),
                [VMEM] * 6 + mlp_specs,
                [row_f32] + chunk_shapes,
                [strips, wide, hidden, *mlp_scratch],
                9, began,
            )
        kept.append((entry, got, proj_s, mixed_s, probs_s, state_1, state_2, normed_m,
                     proj_f, mixed_f, probs_f))

    reductions, whole, done = {}, {}, {}

    def reduction(layer_at, kind, parts):
        if sz.fast and layer_at == 0 and kind < 2:
            reductions[layer_at, kind] = Direct(sz, *parts)
        elif sz.fast:
            reductions[layer_at, kind] = Reduction(sz, parts)
        else:
            (whole[layer_at, kind],) = parts

    def jobs(*steps):
        return [reductions[at[:2]].job(at[2]) for at in steps if at[:2] in reductions]

    def add_up(name, after, *steps, extra=()):
        todo = jobs(*steps) + list(extra)
        if not todo:
            return []
        launch(part(nothing_kernel, sz), name, [], [], [], [], 0.05, after, todo)
        return None

    smalls = [None] * L

    def small_rows():
        return jnp.concatenate([one for layer in smalls for one in layer], axis=0)

    for layer_at in reversed(range(L)):
        (entry, got, proj_s, mixed_s, probs_s, state_1, state_2, normed_m,
         proj_f, mixed_f, probs_f) = kept[layer_at]
        above = layer_at + 1
        if layer_at == L - 1:
            output, grad, small_m, *parts = launch(
                part(last_mlp_kernel, sz, layer_at), f"last_mlp_{layer_at}",
                (sample_len, feature_len, cotangent, state_2, normed_m, up_rows, gains, biases,
                 *mlps[layer_at]),
                [SMEM] * 2 + [VMEM] * 6 + mlp_specs,
                [row_bf, row_f32, small_shape] + grad_shapes(sz, 2),
                [wide, wide, wide, slim, hidden, hidden, square, *mlp_scratch],
                15,
            )
        else:
            grad, small_m, *parts = launch(
                part(mlp_back_kernel, sz, layer_at), f"mlp_back_{layer_at}",
                (grad, kept[above][0], state_2, normed_m, up_rows, gains, *back,
                 *mlps[layer_at]),
                [VMEM] * (6 + n) + mlp_specs,
                [row_f32, small_shape] + grad_shapes(sz, 2),
                [wide, strips, wide, wide, slim, hidden, hidden, square, *mlp_scratch],
                15, parts[:1], early={2: 2 * PIECES, 3: 2 * PIECES} if sz.fast else None,
            )
        reduction(layer_at, 2, parts)
        began = []
        if layer_at < L - 1 and sz.fast:
            add_up(f"sums_{layer_at}", [grad], (above, 2, 3), (above, 1, 2), (above, 0, 1))
            began = [reductions[above, 1].sent, reductions[above, 0].sent]
        grad, low, proj_grad, normed, small_f, *chunks = launch(
            part(feature_back_kernel, sz, layer_at, members[layer_at][1]),
            f"feature_back_{layer_at}",
            (grad, state_1, proj_f, probs_f, gains, shifts, *units[layer_at][1]),
            [VMEM] * 6 + unit_specs,
            [row_f32, row_bf, proj_shape, row_bf, small_shape] + chunk_shapes,
            [slim, strips, wide, *unit_scratch],
            9, began,
        )
        smalls[layer_at] = [small_m, small_f]
        chunks = exchange(sz, chunks)
        parts = launch(
            part(matrix_grad_kernel, sz, 1, layer_at == 0), f"feature_matrix_{layer_at}",
            (proj_grad, low, mixed_f, normed), [VMEM] * 4, grad_shapes(sz, 1),
            [pltpu.VMEM((PIECES, width, width), BF)], 0.7,
            jobs=jobs((layer_at, 2, 1), (above, 0, 2), (above, 2, 4)),
        )
        reduction(layer_at, 1, parts)
        *back, low, proj_grad, small_s = launch(
            part(sample_back_kernel, sz, layer_at, members[layer_at][0]),
            f"sample_back_{layer_at}",
            (proj_s, probs_s, gains, shifts, *chunks, *got, *units[layer_at][0]),
            [VMEM] * (4 + 2 * n) + unit_specs,
            chunk_shapes + [row_bf, proj_shape, small_shape],
            [slim, slim, *unit_scratch],
            9, parts[:1],
        )
        smalls[layer_at].append(small_s)
        back = exchange(sz, back)
        began = []
        if sz.fast and layer_at == 0:
            reductions[1, 3] = upper = join(sz, reductions[1, 1], reductions[1, 0])
            began = [reductions[1, 2].got]
            rows_small = small_rows()
            rows_other = swap_cores(sz, rows_small)
        parts = launch(
            part(matrix_grad_kernel, sz, n, layer_at == 0), f"sample_matrix_{layer_at}",
            (proj_grad, low, mixed_s, *got), [VMEM] * (3 + n), grad_shapes(sz, 1),
            [pltpu.VMEM((PIECES, width, width), BF), slim], 0.7, began,
            jobs((layer_at, 2, 2), (layer_at, 1, 1)),
        )
        reduction(layer_at, 0, parts)
    (tokens_grad,) = launch(
        part(last_norm_kernel, sz), "last_norm", (grad, tokens, gains, *back), [VMEM] * (3 + n),
        [row_f32], [strips], 5,
    )
    if sz.fast:
        first, last = reductions[0, 1], reductions[0, 0]
        block = shaped((16 * L, width), F32)
        *sent, rows_kept = launch(
            part(send_near_kernel, sz), "send_near",
            (last.mine, last.other, rows_small, rows_other), [VMEM] * 4,
            [shaped((256 + 16 * L, width), BF)] * 3 + [block], [], 0.05, [tokens_grad], jobs((1, 3, 3)),
        )
        last.got = [swap_near(sz, v, at + 1) for at, v in enumerate(sent)]
        add_up("sums_mlp", [rows_kept], (0, 2, 3))
        add_up("sums_late", [rows_kept], (0, 2, 4), (1, 3, 4))
        attention_kept, rows_kept, *sent = launch(
            part(send_far_kernel, sz), "send_far",
            (first.mine, first.other, *first.got, last.mine, last.other, *last.got, rows_kept),
            [VMEM] * 11, [shaped((2, 64, width), F32), block] + [shaped((128 + 16 * L, width), BF)] * 3,
            [], 0.05, [reductions[0, 2].got, upper.got],
        )
        got = [swap_far(sz, v, at + 1) for at, v in enumerate(sent)]
        mlp, upper_mlp = reductions[0, 2], reductions[1, 2]
        qkv_shape, out_shape = shaped((L, 3, 64, PAIR), F32), shaped((L, 64, PAIR), F32)
        wide_shape, row_shape = shaped((L, 64, width), F32), shaped((3, L, width), F32)
        (s_qkv, s_out, f_qkv, f_out, up, down, gain_total, shift_total, bias_total,
         up_bias_total) = launch(
            part(last_sums_kernel, sz), "last_sums",
            (attention_kept, rows_kept, *got, mlp.kept, mlp.got, upper_mlp.kept, upper_mlp.got,
             upper.kept, upper.got), [VMEM] * 11,
            [qkv_shape, out_shape, qkv_shape, out_shape, wide_shape, wide_shape,
             row_shape, row_shape, row_shape, shaped((L, PIECES * width), F32)], [], 0.05,
        )

        def turned(v):
            return jnp.transpose(v, (0, 2, 1))

        gain_total, shift_total, bias_total = (
            jnp.transpose(v, (1, 0, 2)) for v in (gain_total, shift_total, bias_total)
        )
        return (
            output.reshape(shape), tokens_grad.reshape(shape), gain_total, shift_total,
            jnp.transpose(s_qkv, (0, 2, 1, 3)), turned(s_out),
            jnp.transpose(f_qkv, (0, 2, 1, 3)), turned(f_out),
            bias_total, up, up_bias_total, turned(down),
        )
    early = lax.psum(small_rows(), ("dp", "tensor"))
    early = early.reshape(-1, 8, width)
    by_layer = []
    at = 0
    for layer_at in range(L):
        count = len(smalls[layer_at])
        sums = [early[at + member] for member in range(count)]
        at += count
        by_layer.append(sums)
    gain_total, shift_total = (
        jnp.stack([jnp.stack([s[row], f[row], m[row]]) for m, f, s in by_layer])
        for row in range(2)
    )
    bias_total = jnp.stack([jnp.stack([f[3], f[2], m[2]]) for m, f, s in by_layer])
    up_bias_total = jnp.stack([m[3 : 3 + PIECES].reshape(-1) for m, f, s in by_layer])

    if not sz.fast:
        for key, full in whole.items():
            done[key] = reduce_whole(sz, full)

    def attention_grads(kind):
        qkv, out = [], []
        for layer_at in range(L):
            if sz.fast:
                value = done[layer_at, kind][0]
                qkv.append(value[:, :QKV].reshape(-1, 3, PAIR))
                out.append(value[:, QKV:].T)
            else:
                value = done[layer_at, kind][0]
                columns = width // n
                start = lax.axis_index("tensor") * columns
                whole = value[:, :, :QKV].reshape(-1, PIECES, 3, PAIR).transpose(0, 2, 1, 3)
                whole = whole.reshape(-1, 3, width)
                qkv.append(lax.dynamic_slice_in_dim(whole, start, columns, 2))
                whole = value[:, :, QKV:].reshape(-1, width)
                out.append(lax.dynamic_slice_in_dim(whole, start, columns, 1).T)
        return jnp.stack(qkv), jnp.stack(out)

    sample_qkv_grad, sample_out_grad = attention_grads(0)
    feature_qkv_grad, feature_out_grad = attention_grads(1)
    ups, downs = [], []
    for layer_at in range(L):
        value = done[layer_at, 2]
        if not sz.fast:
            columns = PIECES * width // n
            start = lax.axis_index("tensor") * columns
            value = value.reshape(2, -1, PIECES * width)
            value = lax.dynamic_slice_in_dim(value, start, columns, 2)
        ups.append(value[0])
        downs.append(value[1].T)
    return (
        output.reshape(shape),
        tokens_grad.reshape(shape),
        gain_total,
        shift_total,
        sample_qkv_grad,
        sample_out_grad,
        feature_qkv_grad,
        feature_out_grad,
        bias_total,
        jnp.stack(ups),
        up_bias_total,
        jnp.stack(downs),
    )


def solution(mesh):
    placed = (
        P("dp", "tensor", None, None),
        P("dp", "tensor", None, None),
        P("dp"),
        P("dp"),
        P("dp"),
        P(),
        P(),
        P(None, None, None, "tensor"),
        P(None, "tensor", None),
        P(None, None, None, "tensor"),
        P(None, "tensor", None),
        P(),
        P(None, None, "tensor"),
        P(),
        P(None, "tensor", None),
    )
    return jax.shard_map(
        body,
        mesh=mesh,
        in_specs=placed,
        out_specs=(
            P("dp", "tensor", None, None),
            P("dp", "tensor", None, None),
            P(),
            P(),
            P(None, "dp", None, "tensor"),
            P(None, "tensor", "dp"),
            P(None, "dp", None, "tensor"),
            P(None, "tensor", "dp"),
            P(),
            P(None, "dp", "tensor"),
            P(),
            P(None, "tensor", "dp"),
        ),
        check_vma=False,
    )
```

```python
import functools

import jax
import jax.numpy as jnp
from jax import lax
from jax.experimental import pallas as pl
from jax.experimental.pallas import tpu as pltpu
from jax.sharding import PartitionSpec as P

HD = 64
L = 2
PIECES = 4
PAIR = 2 * HD
QKV = 3 * PAIR
TILE = 128

epsilon = 1e-05
masked_score = -1e30
SCALE = HD ** (-0.5)
F32 = jnp.float32
BF = jnp.bfloat16
NT = (((1,), (1,)), ((), ()))
TN = (((0,), (0,)), ((), ()))
TANH_A = 0.7978845608028654
TANH_B = 0.044715
VMEM_GRANT = 66977792
SMALL = ((0, 0, 7), (7, 8, 4), (11, 16, 2))
VMEM = pl.BlockSpec(memory_space=pltpu.VMEM)
SMEM = pl.BlockSpec(memory_space=pltpu.SMEM)
ANY = pl.BlockSpec(memory_space=pl.ANY)


class Sizes:
    def __init__(self, shape, tensor, dp):
        self.blocks, self.samples, self.feats, self.width = shape
        self.tensor, self.dp = tensor, dp
        self.rows = self.blocks * self.samples * self.feats
        self.own_feats = self.feats // tensor
        self.run = self.blocks * self.samples
        self.chunk = self.own_feats * self.run
        self.group = tensor * self.run
        self.block_rows = self.samples * self.feats
        self.fast = tensor == 4 and dp == 8


def places(z):
    tensor_at = lax.axis_index("tensor")
    dp_at = lax.axis_index("dp")
    return tensor_at, lax.rem(dp_at, 2), lax.div(dp_at, 2)


def dot(a, b):
    return jnp.dot(a, b, preferred_element_type=F32)


def dot_nt(a, b):
    return lax.dot_general(a, b, NT, preferred_element_type=F32)


def dot_tn(a, b):
    return lax.dot_general(a, b, TN, preferred_element_type=F32)


def normal_rows(x):
    centre = x - jnp.mean(x, axis=-1, keepdims=True)
    spread = jnp.mean(centre * centre, axis=-1, keepdims=True)
    rate = lax.rsqrt(spread + epsilon)
    return centre * rate, rate


def over_rows(rows, fn, carry=0, step=64):
    for at in range(rows // step):
        carry = fn(slice(at * step, (at + 1) * step), carry)
    return carry


def fold(x):
    return jnp.sum(x.reshape(-1, 8, x.shape[-1]), axis=0)


def total(x):
    return jnp.sum(x, axis=0, keepdims=True)


def put_strips(strips, rows, value):
    for lane in range(value.shape[1] // TILE):
        strips[lane, rows, :] = value[:, lane * TILE : (lane + 1) * TILE]


def get_strips(strips, rows):
    return jnp.concatenate([strips[lane, rows, :] for lane in range(strips.shape[0])], axis=1)


def feature_slot(sz, tensor_at, at, slot):
    return (tensor_at ^ at) * sz.own_feats + slot


def spread_out(sz, tensor_at, wide, chunks):
    for at in range(sz.tensor):
        for slot in range(sz.own_feats):
            first = feature_slot(sz, tensor_at, at, slot)
            for lane in range(sz.width // TILE):
                rows = wide[lane, pl.ds(first, sz.run, stride=sz.feats), :]
                chunks[at][
                    slot * sz.run : (slot + 1) * sz.run, lane * TILE : (lane + 1) * TILE
                ] = rows.astype(BF)


def bring_back(sz, tensor_at, chunks, wide):
    for at in range(sz.tensor):
        for slot in range(sz.own_feats):
            first = feature_slot(sz, tensor_at, at, slot)
            for lane in range(sz.width // TILE):
                rows = chunks[at][
                    slot * sz.run : (slot + 1) * sz.run, lane * TILE : (lane + 1) * TILE
                ]
                wide[lane, pl.ds(first, sz.run, stride=sz.feats), :] = rows.astype(F32)


def by_feature(sz, chunks, x):
    for at in range(sz.tensor):
        for slot in range(sz.own_feats):
            first = slot * sz.group + at * sz.run
            x[first : first + sz.run, :] = chunks[at][slot * sz.run : (slot + 1) * sz.run, :]


def to_chunks(sz, value, chunks):
    for at in range(sz.tensor):
        for slot in range(sz.own_feats):
            first = slot * sz.group + at * sz.run
            chunks[at][slot * sz.run : (slot + 1) * sz.run, :] = value[
                first : first + sz.run
            ].astype(BF)


def where_halves(core):
    other = 1 - core
    return (
        (1 + core, core),
        (2 - core, core),
        (3, core),
        (1 + other, other),
        (2 - other, other),
        (3, other),
    )


def load_unit(sz, layer_at, member, parts, w, w_out, sems, core):
    pairs = []
    if not sz.fast:
        pairs += [(parts[0], w), (parts[1], w_out)]
    else:
        qkv, out = parts[:2]
        for at in range(3):
            pairs.append((qkv.at[layer_at, at], w.at[:, pl.ds(at * PAIR, PAIR)]))
        pairs.append((out.at[layer_at], w_out.at[pl.ds(0, PAIR), :]))
        half_rows = sz.width // 2
        for source, (piece, half) in zip(parts[2:], where_halves(core)):
            if member is not None:
                source = source.at[member]
            start = pl.multiple_of(half * half_rows, half_rows)
            first = pl.multiple_of(piece * QKV, TILE)
            pairs.append(
                (source.at[:, pl.ds(0, QKV)], w.at[pl.ds(start, half_rows), pl.ds(first, QKV)])
            )
            first = pl.multiple_of(piece * PAIR, TILE)
            for block in range(half_rows // TILE):
                lanes = pl.ds(pl.multiple_of(start + block * TILE, TILE), TILE)
                pairs.append(
                    (
                        source.at[pl.ds(block * TILE, TILE), pl.ds(QKV, PAIR)],
                        w_out.at[pl.ds(first, PAIR), lanes],
                    )
                )
    return begin(pairs, sems)


def begin(pairs, sems):
    copies = []
    for source, target in pairs:
        copies.append(pltpu.make_async_copy(source, target, sems.at[len(copies)]))
        copies[-1].start()
    return copies


def finish(copies):
    for copy in copies:
        copy.wait()


def load_mlp(sz, layer_at, parts, up, down, sems, core):
    pairs = []
    if not sz.fast:
        pairs += [(parts[0], up), (parts[1], down)]
    else:
        width = sz.width
        pairs.append((parts[0].at[layer_at], up.at[:, pl.ds(0, width)]))
        pairs.append((parts[1].at[layer_at], down.at[pl.ds(0, width), :]))
        half_rows = width // 2
        for source, (piece, half) in zip(parts[2:], where_halves(core)):
            start = pl.multiple_of(half * half_rows, half_rows)
            first = pl.multiple_of(piece * width, width)
            pairs.append(
                (source.at[0], up.at[pl.ds(start, half_rows), pl.ds(first, width)])
            )
            rows = pl.ds(pl.multiple_of(first + start, half_rows), half_rows)
            pairs.append((source.at[1], down.at[rows, :]))
    return begin(pairs, sems)


def put_grad(sz, grads, outs, piece, member, core, z, direct=False):
    if not sz.fast:
        outs[0][piece, member] = grads[...]
        return
    mine, theirs = outs
    if direct or piece in (0, 3):
        at_mine = at_theirs = piece
    elif piece == 1:
        at_mine, at_theirs = 1 + core, 2 - core
    else:
        at_mine, at_theirs = 2 - core, 1 + core
    for place, near in enumerate((0, 1, 2, 3) if direct else (0, 2, 1, 3)):
        first = (z ^ near) * 128
        rows_mine = pl.ds(pl.multiple_of(first + core * 64, 64), 64)
        rows_theirs = pl.ds(pl.multiple_of(first + (1 - core) * 64, 64), 64)
        mine[at_mine, place, member] = grads[rows_mine, :]
        theirs[at_theirs, place, member] = grads[rows_theirs, :]
    flush(mine, at_mine, slice(None), member)
    flush(theirs, at_theirs, slice(None), member)


def head_masks():
    lane = lax.broadcasted_iota(jnp.int32, (1, PAIR), 1)
    return lane < HD, lane >= HD


def sample_bias(sz, tensor_at, tasks, lengths, bias):
    def of(index):
        run_at = index // sz.run
        block = (index // sz.samples) % sz.blocks
        sample = (run_at ^ tensor_at) * sz.samples + index % sz.samples
        task = jnp.zeros_like(index)
        length = jnp.zeros_like(index)
        for at in range(sz.blocks):
            task = jnp.where(block == at, tasks[at], task)
            length = jnp.where(block == at, lengths[at], length)
        return task, sample < length

    row_task, unused = of(lax.broadcasted_iota(jnp.int32, (sz.group, 1), 0))
    key_task, key_live = of(lax.broadcasted_iota(jnp.int32, (1, sz.group), 1))
    key_task = jnp.where(key_live, key_task, -1)
    bias[...] = jnp.where(row_task == key_task, 0.0, masked_score)


def feature_bias(sz, length):
    row = lax.broadcasted_iota(jnp.int32, (TILE, TILE), 0)
    key = lax.broadcasted_iota(jnp.int32, (TILE, TILE), 1)
    same = (row // sz.feats) == (key // sz.feats)
    return jnp.where(same & (key % sz.feats < length), 0.0, masked_score)


def attend(proj, piece, jobs, probs, mixed):
    masks = head_masks()
    first = piece * QKV
    scores = []
    for rows, bias, place in jobs:
        query = proj[rows, first : first + PAIR]
        key = proj[rows, first + PAIR : first + 2 * PAIR]
        for mask in masks:
            scores.append(dot_nt(jnp.where(mask, query, 0) * SCALE, key) + bias)
    tops = [jnp.max(part, axis=-1, keepdims=True) for part in scores]
    weights = [jnp.exp(part - top) for part, top in zip(scores, tops)]
    shares = [1.0 / jnp.sum(part, axis=-1, keepdims=True) for part in weights]
    weights = [(part * share).astype(BF) for part, share in zip(weights, shares)]
    for at, (rows, bias, place) in enumerate(jobs):
        value = proj[rows, first + 2 * PAIR : first + QKV]
        pair = weights[2 * at : 2 * at + 2]
        for head in range(2):
            probs[piece, place, head] = pair[head]
        mixed[rows, piece * PAIR : (piece + 1) * PAIR] = jnp.where(
            masks[0], dot(pair[0], value), dot(pair[1], value)
        ).astype(BF)
    flush(probs, piece)
    flush(mixed, slice(None), pl.ds(piece * PAIR, PAIR))


def attend_back(proj, piece, jobs, probs, mixed_grad, proj_grad):
    masks = head_masks()
    first = piece * QKV
    head_grads, weights, weight_grads = [], [], []
    for rows, place in jobs:
        grad = mixed_grad[rows, piece * PAIR : (piece + 1) * PAIR]
        value = proj[rows, first + 2 * PAIR : first + QKV]
        for head, mask in enumerate(masks):
            head_grads.append(jnp.where(mask, grad, 0))
            weights.append(probs[piece, place, head])
            weight_grads.append(dot_nt(head_grads[-1], value))
    score_grads = []
    for low, grad in zip(weights, weight_grads):
        wide = low.astype(F32)
        product = wide * grad
        score_grads.append((product - wide * jnp.sum(product, axis=-1, keepdims=True)).astype(BF))
    for at, (rows, place) in enumerate(jobs):
        query = proj[rows, first : first + PAIR]
        key = proj[rows, first + PAIR : first + 2 * PAIR]
        one, two = score_grads[2 * at : 2 * at + 2]
        queries = jnp.where(masks[0], dot(one, key), dot(two, key)) * SCALE
        keys = dot_tn(one, jnp.where(masks[0], query, 0))
        keys = (keys + dot_tn(two, jnp.where(masks[1], query, 0))) * SCALE
        values = dot_tn(weights[2 * at], head_grads[2 * at])
        values = values + dot_tn(weights[2 * at + 1], head_grads[2 * at + 1])
        proj_grad[rows, first : first + PAIR] = queries.astype(BF)
        proj_grad[rows, first + PAIR : first + 2 * PAIR] = keys.astype(BF)
        proj_grad[rows, first + 2 * PAIR : first + QKV] = values.astype(BF)
    flush(proj_grad, slice(None), pl.ds(first, QKV))


def norm_back_rows(state, incoming, gain):
    xhat, rate = normal_rows(state)
    inner = incoming * gain
    back = rate * (
        inner
        - jnp.mean(inner, axis=-1, keepdims=True)
        - xhat * jnp.mean(inner * xhat, axis=-1, keepdims=True)
    )
    return xhat, back


def pack_copies(sz, layer_at, qkv, out, sent, core):
    half = sz.width // 2
    rows = pl.ds(pl.multiple_of(core * half, half), half)
    pairs = []
    for at in range(3):
        pairs.append((qkv.at[layer_at, at, rows, :], sent.at[:, pl.ds(at * PAIR, PAIR)]))
    for block in range(half // TILE):
        lanes = pl.ds(pl.multiple_of(core * half + block * TILE, TILE), TILE)
        pairs.append(
            (out.at[layer_at, :, lanes], sent.at[pl.ds(block * TILE, TILE), pl.ds(QKV, PAIR)])
        )
    return pairs


def start_kernel(sz, tokens, gains, shifts, qkv, out, *rest):
    chunks, rest = rest[: sz.tensor], rest[sz.tensor :]
    tensor_at, core, z = places(sz)
    copies = []
    if sz.fast:
        sent, strips, sems = rest
        copies = begin(pack_copies(sz, 0, qkv, out, sent, core), sems)
    else:
        (strips,) = rest

    def rows_of(rows, kept):
        xhat, unused = normal_rows(tokens[rows, :].astype(F32))
        put_strips(strips, rows, xhat * gains[0, 0:1, :] + shifts[0, 0:1, :])
        return kept

    over_rows(sz.rows, rows_of)
    spread_out(sz, tensor_at, strips, chunks)
    finish(copies)


def pack_mlp_kernel(sz, layer_at, up, down, sent, sems):
    tensor_at, core, z = places(sz)
    finish(begin(mlp_pairs(sz, layer_at, up, down, sent, core), sems))


def mlp_pairs(sz, layer_at, up, down, sent, core):
    half = sz.width // 2
    rows = pl.ds(pl.multiple_of(core * half, half), half)
    return [(w.at[layer_at, rows, :], sent.at[at]) for at, w in enumerate((up, down))]


def pack_early_kernel(sz, sample_qkv, sample_out, feature_qkv, feature_out, up, down, *rest):
    first, mlp, units, sems = rest
    tensor_at, core, z = places(sz)
    pairs = pack_copies(sz, 0, feature_qkv, feature_out, first, core)
    pairs += mlp_pairs(sz, 0, up, down, mlp, core)
    pairs += pack_copies(sz, 1, sample_qkv, sample_out, units.at[0], core)
    pairs += pack_copies(sz, 1, feature_qkv, feature_out, units.at[1], core)
    finish(begin(pairs, sems))


def nothing_kernel(sz, *rest):
    pass


def send_near_kernel(sz, mine, other, rows, rows_other, *outs):
    kept = outs[-1]
    kept[...] = jnp.zeros_like(kept)
    for layer_at in range(L):
        for at, first, count in SMALL:
            here = slice(24 * layer_at + first, 24 * layer_at + first + count)
            there = slice(16 * layer_at + at, 16 * layer_at + at + count)
            kept[there, :] = rows[here, :] + rows_other[here, :]
    small = kept[...].astype(BF)
    kept[...] = small.astype(F32)
    for piece in range(1, PIECES):
        out = outs[piece - 1]
        for near in range(4):
            value = mine[piece, near, 0].astype(F32) + other[piece, near, 0].astype(F32)
            out[near * 64 : near * 64 + 64, :] = value.astype(BF)
        out[256:, :] = small


def pairwise(one, two, three, four):
    return (one + two) + (three + four)


def send_far_kernel(sz, *refs):
    first, last, small, outs = refs[:5], refs[5:10], refs[10], refs[11:]
    kept, rows, sends = outs[0], outs[1], outs[2:]

    def value(unit, at, near):
        mine, other, *got = unit
        out = mine[0, near, 0].astype(F32) + other[0, near, 0].astype(F32)
        for one in got:
            got_here = one[0, near, 0] if at == 0 else one[near * 64 : near * 64 + 64, :]
            out = out + got_here.astype(F32)
        return out

    x, y, d = (one[256:, :].astype(F32) for one in last[2:])
    low = pairwise(small[...], x, y, d).astype(BF)
    rows[...] = low.astype(F32)
    for at, unit in enumerate((first, last)):
        kept[at] = value(unit, at, 0)
        for near in range(1, 4):
            sends[near - 1][at * 64 : at * 64 + 64, :] = value(unit, at, near).astype(BF)
    for near in range(1, 4):
        sends[near - 1][128:, :] = low


def last_sums_kernel(sz, *refs):
    kept, rows, one, two, three, mlp, mlp_got, upper_mlp, upper_mlp_got = refs[:9]
    upper, upper_got = refs[9:11]
    s_qkv, s_out, f_qkv, f_out, up, down, gain, shift, bias, up_bias = refs[11:]
    small = pairwise(rows[...], *(got[128:, :].astype(F32) for got in (one, two, three)))

    def attention(layer_at, value, qkv, out):
        for at in range(3):
            qkv[layer_at, at] = value[:, at * PAIR : (at + 1) * PAIR]
        out[layer_at] = value[:, QKV:]

    for at, (qkv, out) in enumerate(((f_qkv, f_out), (s_qkv, s_out))):
        value = kept[at]
        for got in (one, two, three):
            value = value + got[at * 64 : at * 64 + 64, :].astype(F32)
        attention(0, value, qkv, out)
        attention(1, upper[0, 0, at] + upper_got[0, 0, at].astype(F32), qkv, out)
    for at, w in enumerate((up, down)):
        w[0] = mlp[0, 0, at] + mlp_got[0, 0, at].astype(F32)
        w[1] = upper_mlp[0, 0, at] + upper_mlp_got[0, 0, at].astype(F32)
    for layer_at in range(L):
        m, f, s = (16 * layer_at + at for at, first, count in SMALL)
        for out, places_in in ((gain, (s, f, m)), (shift, (s + 1, f + 1, m + 1)),
                               (bias, (f + 3, f + 2, m + 2))):
            for at, row in enumerate(places_in):
                out[at, layer_at : layer_at + 1, :] = small[row : row + 1]
        for piece in range(PIECES):
            lanes = slice(piece * sz.width, (piece + 1) * sz.width)
            row = m + 3 + piece
            up_bias[layer_at : layer_at + 1, lanes] = small[row : row + 1]


def unit_parts(sz):
    return 8 if sz.fast else 2


def sample_kernel(sz, layer_at, member, tasks, lengths, *rest):
    n, parts = sz.tensor, unit_parts(sz)
    chunks, weights = rest[:n], rest[n : n + parts]
    outs = rest[n + parts :]
    back, proj, mixed, probs = outs[:n], outs[n], outs[n + 1], outs[n + 2]
    x, bias, w, w_out, sems = outs[n + 3 :]
    tensor_at, core, z = places(sz)
    copies = load_unit(sz, layer_at, member, weights, w, w_out, sems, core)
    by_feature(sz, chunks, x)
    sample_bias(sz, tensor_at, tasks, lengths, bias)
    finish(copies)
    proj[...] = dot(x[...], w[...]).astype(BF)
    flush(proj)
    jobs = [
        (slice(slot * sz.group, (slot + 1) * sz.group), bias[...], slot)
        for slot in range(sz.own_feats)
    ]
    for piece in range(PIECES):
        attend(proj, piece, jobs, probs, mixed)
    to_chunks(sz, dot(mixed[...], w_out[...]), back)


def feature_kernel(sz, layer_at, member, lengths, state, gains, shifts, out_bias, *rest):
    n, parts = sz.tensor, unit_parts(sz)
    chunks, weights = rest[:n], rest[n : n + parts]
    state_1, state_2, normed_m, proj, mixed, probs = rest[n + parts : n + parts + 6]
    strips, wide, normed, w, w_out, sems = rest[n + parts + 6 :]
    tensor_at, core, z = places(sz)
    copies = load_unit(sz, layer_at, member, weights, w, w_out, sems, core)
    bring_back(sz, tensor_at, chunks, strips)
    at = slice(layer_at, layer_at + 1)

    def before(rows, kept):
        value = state[rows, :].astype(F32) + get_strips(strips, rows) + out_bias[0, at, :]
        state_1[rows, :] = value
        xhat, unused = normal_rows(value)
        normed[rows, :] = (xhat * gains[1, at, :] + shifts[1, at, :]).astype(BF)
        return kept

    over_rows(sz.rows, before)
    biases = [feature_bias(sz, lengths[block]) for block in range(sz.blocks)]
    jobs = [
        (slice(tile * TILE, (tile + 1) * TILE), biases[tile * TILE // sz.block_rows], tile)
        for tile in range(sz.rows // TILE)
    ]
    finish(copies)
    flush(state_1)
    proj[...] = dot(normed[...], w[...]).astype(BF)
    flush(proj)
    for piece in range(PIECES):
        attend(proj, piece, jobs, probs, mixed)
    wide[...] = dot(mixed[...], w_out[...])

    def after(rows, kept):
        value = state_1[rows, :] + wide[rows, :] + out_bias[1, at, :]
        state_2[rows, :] = value
        xhat, unused = normal_rows(value)
        normed_m[rows, :] = (xhat * gains[2, at, :] + shifts[2, at, :]).astype(BF)
        return kept

    over_rows(sz.rows, after)


def up_bias_rows(sz, tensor_at, piece):
    return (tensor_at ^ piece) if sz.fast else piece


def mlp_kernel(sz, layer_at, state_2, normed_m, up_bias, gains, shifts, out_bias, *rest):
    n = sz.tensor
    parts = 8 if sz.fast else 2
    weights, (state_3, *chunks) = rest[:parts], rest[parts : parts + 1 + n]
    strips, wide, hidden, up, down, sems = rest[parts + 1 + n :]
    tensor_at, core, z = places(sz)
    finish(load_mlp(sz, layer_at, weights, up, down, sems, core))
    width = sz.width
    for piece in range(PIECES):
        lanes = slice(piece * width, (piece + 1) * width)
        wide[...] = dot(normed_m[...], up[:, lanes])
        shift = up_bias[layer_at, pl.ds(up_bias_rows(sz, tensor_at, piece), 1), :]
        value = wide[...] + shift
        half = 0.5 + 0.5 * jnp.tanh(value * (TANH_A + TANH_A * TANH_B * (value * value)))
        hidden[:, lanes] = (value * half).astype(BF)
    wide[...] = dot(hidden[...], down[...])
    at = slice(layer_at, layer_at + 1)
    later = slice(layer_at + 1, layer_at + 2)

    def after(rows, kept):
        value = state_2[rows, :] + wide[rows, :] + out_bias[2, at, :]
        state_3[rows, :] = value
        xhat, unused = normal_rows(value)
        put_strips(strips, rows, xhat * gains[0, later, :] + shifts[0, later, :])
        return kept

    over_rows(sz.rows, after)
    spread_out(sz, tensor_at, strips, chunks)


def mlp_back(
    sz, layer_at, grad, state_2, normed_m, up_bias, gains, up, down, low, wide, other, hidden,
    up_grad, grads, grad_out, outs, small,
):
    tensor_at, core, z = places(sz)
    at = slice(layer_at, layer_at + 1)
    width = sz.width
    nothing = jnp.zeros((8, width), F32)

    def lower(rows, kept):
        part = grad[rows, :].astype(BF)
        low[rows, :] = part
        return kept + fold(part.astype(F32))

    small[...] = jnp.zeros_like(small)
    small[2:3, :] = total(over_rows(sz.rows, lower, nothing))
    for piece in range(PIECES):
        lanes = slice(piece * width, (piece + 1) * width)
        name = up_bias_rows(sz, tensor_at, piece)
        wide[...] = dot(normed_m[...], up[:, lanes])
        other[...] = dot_nt(low[...], down[lanes, :])
        shift = up_bias[layer_at, pl.ds(name, 1), :]
        value = wide[...] + shift
        square = value * value
        half = 0.5 + 0.5 * jnp.tanh(value * (TANH_A + TANH_A * TANH_B * square))
        full = value * half
        hidden[:, lanes] = full.astype(BF)
        slope = half + full * (1.0 - half) * (2.0 * TANH_A + 6.0 * TANH_A * TANH_B * square)
        part = (other[...] * slope).astype(BF)
        up_grad[:, lanes] = part
        small[pl.ds(3 + name, 1), :] = total(fold(part.astype(F32)))
        grads[...] = dot_tn(normed_m[...], up_grad[:, lanes]).astype(BF)
        put_grad(sz, grads, outs, piece, 0, core, z)
        grads[...] = dot_tn(low[...], hidden[:, lanes]).astype(BF)
        put_grad(sz, grads, outs, piece, 1, core, z)
    wide[...] = dot_nt(up_grad[...], up[...])

    def back(rows, kept):
        incoming = wide[rows, :]
        xhat, change = norm_back_rows(state_2[rows, :], incoming, gains[2, at, :])
        grad_out[rows, :] = grad[rows, :] + change
        return kept[0] + fold(incoming * xhat), kept[1] + fold(incoming)

    gain_sum, shift_sum = over_rows(sz.rows, back, (nothing, nothing))
    small[0:1, :] = total(gain_sum)
    small[1:2, :] = total(shift_sum)


def last_mlp_kernel(
    sz, layer_at, sample_lens, feature_lens, cotangent, state_2, normed_m, up_bias, gains, out_bias,
    *rest,
):
    parts, halves = unit_parts(sz), 2 if sz.fast else 1
    weights, rest = rest[:parts], rest[parts:]
    output, grad_out, small = rest[:3]
    outs = rest[3 : 3 + halves]
    grad, wide, other, low, hidden, up_grad, grads, up, down, sems = rest[3 + halves :]
    tensor_at, core, z = places(sz)
    copies = load_mlp(sz, layer_at, weights, up, down, sems, core)
    step = 64

    def live_rows(rows, kept):
        index = rows.start + lax.broadcasted_iota(jnp.int32, (step, 1), 0)
        block = index // sz.block_rows
        sample = tensor_at * sz.samples + (index // sz.feats) % sz.samples
        sample_len = jnp.zeros_like(index)
        feature_len = jnp.zeros_like(index)
        for at in range(sz.blocks):
            sample_len = jnp.where(block == at, sample_lens[at], sample_len)
            feature_len = jnp.where(block == at, feature_lens[at], feature_len)
        live = (sample < sample_len) & (index % sz.feats < feature_len)
        grad[rows, :] = jnp.where(live, cotangent[rows, :].astype(F32), 0.0)
        return kept

    over_rows(sz.rows, live_rows, 0, step)
    finish(copies)
    mlp_back(
        sz, layer_at, grad, state_2, normed_m, up_bias, gains, up, down, low, wide, other, hidden,
        up_grad, grads, grad_out, outs, small,
    )
    at = slice(layer_at, layer_at + 1)
    other[...] = dot(hidden[...], down[...])

    def after(rows, kept):
        value = state_2[rows, :] + other[rows, :] + out_bias[2, at, :]
        output[rows, :] = value.astype(BF)
        return kept

    over_rows(sz.rows, after)


def mlp_back_kernel(
    sz, layer_at, grad_in, state_3, state_2, normed_m, up_bias, gains, *rest
):
    n = sz.tensor
    parts, halves = unit_parts(sz), 2 if sz.fast else 1
    chunks, weights, rest = rest[:n], rest[n : n + parts], rest[n + parts :]
    grad_out, small = rest[:2]
    outs = rest[2 : 2 + halves]
    grad, strips, wide, other, low, hidden, up_grad, grads, up, down, sems = rest[2 + halves :]
    tensor_at, core, z = places(sz)
    copies = load_mlp(sz, layer_at, weights, up, down, sems, core)
    sample_norm_back(sz, layer_at + 1, tensor_at, grad_in, state_3, chunks, gains, strips, grad)
    finish(copies)
    mlp_back(
        sz, layer_at, grad, state_2, normed_m, up_bias, gains, up, down, low, wide, other, hidden,
        up_grad, grads, grad_out, outs, small,
    )


def sample_norm_back(sz, layer_at, tensor_at, grad_in, state, chunks, gains, strips, grad):
    bring_back(sz, tensor_at, chunks, strips)
    at = slice(layer_at, layer_at + 1)

    def back(rows, kept):
        incoming = get_strips(strips, rows)
        xhat, change = norm_back_rows(state[rows, :].astype(F32), incoming, gains[0, at, :])
        grad[rows, :] = grad_in[rows, :] + change
        return kept

    over_rows(sz.rows, back)


def last_norm_kernel(sz, grad_in, state, gains, *rest):
    chunks, (grad, strips) = rest[: sz.tensor], rest[sz.tensor :]
    tensor_at, core, z = places(sz)
    sample_norm_back(sz, 0, tensor_at, grad_in, state, chunks, gains, strips, grad)


def feature_back_kernel(sz, layer_at, member, grad, state_1, proj, probs, gains, shifts, *rest):
    n, parts = sz.tensor, unit_parts(sz)
    weights, rest = rest[:parts], rest[parts:]
    grad_out, low, proj_grad, normed, small = rest[:5]
    chunks = rest[5 : 5 + n]
    mixed_grad, strips, wide, w, w_out, sems = rest[5 + n :]
    tensor_at, core, z = places(sz)
    copies = load_unit(sz, layer_at, member, weights, w, w_out, sems, core)
    at = slice(layer_at, layer_at + 1)
    nothing = jnp.zeros((8, sz.width), F32)

    def lower(rows, kept):
        part = grad[rows, :].astype(BF)
        low[rows, :] = part
        return kept + fold(part.astype(F32))

    small[...] = jnp.zeros_like(small)
    small[2:3, :] = total(over_rows(sz.rows, lower, nothing))
    flush(low)
    finish(copies)
    mixed_grad[...] = dot_nt(low[...], w_out[...]).astype(BF)
    jobs = [(slice(tile * TILE, (tile + 1) * TILE), tile) for tile in range(sz.rows // TILE)]
    for piece in range(PIECES):
        attend_back(proj, piece, jobs, probs, mixed_grad, proj_grad)
    wide[...] = dot_nt(proj_grad[...], w[...])

    def back(rows, kept):
        incoming = wide[rows, :]
        gain = gains[1, at, :]
        xhat, change = norm_back_rows(state_1[rows, :], incoming, gain)
        value = grad[rows, :] + change
        grad_out[rows, :] = value
        put_strips(strips, rows, value)
        normed[rows, :] = (xhat * gain + shifts[1, at, :]).astype(BF)
        rounded = value.astype(BF).astype(F32)
        return (
            kept[0] + fold(incoming * xhat),
            kept[1] + fold(incoming),
            kept[2] + fold(rounded),
        )

    sums = over_rows(sz.rows, back, (nothing, nothing, nothing))
    small[0:1, :] = total(sums[0])
    small[1:2, :] = total(sums[1])
    small[3:4, :] = total(sums[2])
    spread_out(sz, tensor_at, strips, chunks)


def sample_back_kernel(sz, layer_at, member, extra, proj, probs, gains, shifts, *rest):
    n, parts = sz.tensor, unit_parts(sz)
    others, rest = rest[:extra], rest[extra:]
    chunks, rows_in, rest = rest[:n], rest[n : 2 * n], rest[2 * n :]
    weights, rest = rest[:parts], rest[parts:]
    back, low, proj_grad, small = rest[:n], rest[n], rest[n + 1], rest[n + 2]
    mixed_grad, normed, w, w_out, sems = rest[n + 3 :]
    tensor_at, core, z = places(sz)
    copies = load_unit(sz, layer_at, member, weights, w, w_out, sems, core)
    by_feature(sz, chunks, low)
    by_feature(sz, rows_in, normed)
    flush(low)
    finish(copies)
    mixed_grad[...] = dot_nt(low[...], w_out[...]).astype(BF)
    jobs = [
        (slice(slot * sz.group, (slot + 1) * sz.group), slot) for slot in range(sz.own_feats)
    ]
    for piece in range(PIECES):
        attend_back(proj, piece, jobs, probs, mixed_grad, proj_grad)
    normed_grad = dot_nt(proj_grad[...], w[...])
    to_chunks(sz, normed_grad, back)
    at = slice(layer_at, layer_at + 1)
    shift_sum = total(fold(normed_grad))
    gain_sum = total(fold(normed_grad * normed[...].astype(F32)))
    small[...] = jnp.zeros_like(small)
    first = 16 if extra else 0
    small[first : first + 1, :] = (gain_sum - shifts[0, at, :] * shift_sum) / gains[0, at, :]
    small[first + 1 : first + 2, :] = shift_sum
    for at, other in enumerate(others):
        place = at if at < 2 else at + 1
        small[8 * place : 8 * place + 8, :] = other[...]


def matrix_grad_kernel(sz, count, direct, proj_grad, low, mixed, *rest):
    halves = 2 if sz.fast else 1
    rows, outs, rest = rest[:count], rest[count : count + halves], rest[count + halves :]
    tensor_at, core, z = places(sz)
    if count == 1:
        (grads,) = rest
        (normed,) = rows
    else:
        grads, normed = rest
        by_feature(sz, rows, normed)
    for piece in range(PIECES):
        lanes = slice(piece * QKV, (piece + 1) * QKV)
        grads[piece, :, :QKV] = dot_tn(normed[...], proj_grad[:, lanes]).astype(BF)
        lanes = slice(piece * PAIR, (piece + 1) * PAIR)
        grads[piece, :, QKV:] = dot_tn(low[...], mixed[:, lanes]).astype(BF)
        put_grad(sz, grads.at[piece], outs, piece, 0, core, z, direct)


def shaped(shape, dtype):
    return jax.ShapeDtypeStruct(shape, dtype)


class Early:
    def __init__(self, target, held, sems):
        self.target, self.held, self.sems, self.copies = target, held, sems, []
        self.shape, self.dtype = held.shape, held.dtype

    def __getitem__(self, index):
        return self.held[index]

    def __setitem__(self, index, value):
        self.held[index] = value

    def flush(self, *index):
        source, target = self.held, self.target
        if index:
            source, target = source.at[index], target.at[index]
        copy = pltpu.make_async_copy(source, target, self.sems.at[len(self.copies)])
        copy.start()
        self.copies.append(copy)


def flush(ref, *index):
    if isinstance(ref, Early):
        ref.flush(*index)


class Job:
    def __init__(self, groups, outs, split, then):
        self.groups, self.outs, self.split, self.then = groups, outs, split, then
        self.terms = [term for group in groups for term in group]

    def scratch(self):
        shapes = [
            (count, array.shape[1], members, *array.shape[3:])
            for array, first, count, member, members in self.terms
        ]
        return [
            pltpu.VMEM(shape, term[0].dtype) for shape, term in zip(shapes, self.terms)
        ] + [pltpu.SemaphoreType.DMA((len(self.terms),))]

    def start(self, refs, scratch):
        pairs = []
        for ref, term, target in zip(refs, self.terms, scratch):
            array, first, count, member, members = term
            pairs.append((ref.at[pl.ds(first, count), :, pl.ds(member, members)], target))
        return begin(pairs, scratch[-1])

    def finish(self, copies, outs, scratch):
        finish(copies)
        at = place = 0
        for group in self.groups:
            refs = scratch[at : at + len(group)]
            at += len(group)
            lead, near, members = refs[0].shape[:3]
            for one in range(lead):
                for two in range(near):
                    for member in range(members):
                        value = refs[0][one, two, member].astype(F32)
                        for ref in refs[1:]:
                            value = value + ref[one, two, member].astype(F32)
                        out, index, lead_at = outs[0], two, one
                        if self.split == 1:
                            out, lead_at = outs[one], 0
                        elif self.split and two >= near // 2:
                            out, index = outs[1], two - near // 2
                        out[lead_at, index, place + member] = value.astype(out.dtype)
            place += members


def launch(
    kernel, name, operands, specs, outs, scratch, micros, after=(), jobs=(), early=None, through=(),
    defer=False,
):
    after, outs = list(after), list(outs)
    sums = [term[0] for job in jobs for term in job.terms]
    job_outs = [out for job in jobs for out in job.outs]
    job_scratch = [job.scratch() for job in jobs]
    count, plain = len(operands), len(scratch)
    before = count + len(sums) + len(after)
    skip = before + len(through)
    early = early or {}
    held = []
    for at, parts in early.items():
        held += [pltpu.VMEM(outs[at].shape, outs[at].dtype), pltpu.SemaphoreType.DMA((parts,))]

    def whole(*refs):
        given, results = refs[count : count + len(sums)], refs[skip : skip + len(outs)]
        extra = refs[skip + len(outs) : skip + len(outs) + len(job_outs)]
        rest = refs[skip + len(outs) + len(job_outs) + len(through) :]
        own, rest = rest[:plain], rest[plain:]
        results = list(results)
        for at in early:
            results[at] = Early(results[at], *rest[:2])
            rest = rest[2:]
        started = []
        for job, buffers in zip(jobs, job_scratch):
            mine, rest = rest[: len(buffers)], rest[len(buffers) :]
            started.append((job, mine, job.start(given[: len(job.terms)], mine)))
            given = given[len(job.terms) :]
        kernel(*refs[:count], *results, *own)
        for job, mine, copies in started:
            job.finish(copies, extra[: len(job.outs)], mine)
            extra = extra[len(job.outs) :]
        for at in early:
            finish(results[at].copies)

    results = pl.pallas_call(
        whole,
        out_shape=outs + job_outs + [shaped(v.shape, v.dtype) for v in through],
        input_output_aliases={
            before + at: len(outs) + len(job_outs) + at for at in range(len(through))
        },
        in_specs=list(specs) + [ANY] * (len(sums) + len(after) + len(through)),
        out_specs=[ANY if at in early else VMEM for at in range(len(outs))]
        + [VMEM] * len(job_outs)
        + [ANY] * len(through),
        scratch_shapes=list(scratch) + held + [buffer for buffers in job_scratch for buffer in buffers],
        name=name,
        cost_estimate=pl.CostEstimate(
            flops=int(micros * 8e9), bytes_accessed=1_000_000, transcendentals=0
        ),
        compiler_params=pltpu.CompilerParams(vmem_limit_bytes=VMEM_GRANT),
    )(*operands, *sums, *after, *through)
    results, extra = results[: len(outs)], results[len(outs) :]
    through = extra[len(job_outs) :]
    if defer:
        return list(results), list(extra[: len(job_outs)])
    for job in jobs:
        job.then(*extra[: len(job.outs)])
        extra = extra[len(job.outs) :]
    return list(results) + list(through)


def grad_shapes(sz, members):
    if sz.fast:
        return [shaped((PIECES, 4, members, 64, sz.width), BF)] * 2
    return [shaped((PIECES, members, sz.width, sz.width), BF)]


def swap_cores(sz, v):
    return lax.ppermute(v, "dp", [(at, at ^ 1) for at in range(sz.dp)])


def swap_near(sz, v, distance):
    return lax.ppermute(v, "tensor", [(at, at ^ distance) for at in range(sz.tensor)])


def swap_far(sz, v, distance):
    return lax.ppermute(v, "dp", [(at, at ^ (2 * distance)) for at in range(sz.dp)])


def swap_turn(sz, v, turn):
    pairs = []
    for dp_at in range(sz.dp):
        distance = 1 + ((dp_at + turn) % 2)
        for at in range(sz.tensor):
            base = dp_at * sz.tensor
            pairs.append((base + at, base + (at ^ distance)))
    return lax.ppermute(v, ("dp", "tensor"), pairs)


def exchange(sz, chunks):
    return [chunks[0]] + [swap_near(sz, chunks[at], at) for at in range(1, sz.tensor)]


def gather_unit(sz, half):
    first = swap_turn(sz, half, 0)
    second = swap_turn(sz, half, 1)
    third = swap_turn(sz, first, 1)
    got = [first, second, third]
    return got + [swap_cores(sz, v) for v in got]


class Reduction:
    def __init__(self, sz, *units):
        self.sz = sz
        self.units = [(mine, swap_cores(sz, theirs), mine.shape[2]) for mine, theirs in units]
        self.members = sum(unit[2] for unit in self.units)
        self.tail = units[0][0].shape[3:]

    def groups(self, first, count, extra):
        groups, place = [], 0
        for mine, other, members in self.units:
            group = [(mine, first, count, 0, members), (other, first, count, 0, members)]
            group += [(array, at, count, place, members) for array, at in extra]
            groups.append(group)
            place += members
        return groups

    def shape(self, lead, near, dtype=BF):
        return shaped((lead, near, self.members, *self.tail), dtype)

    def job(self, step):
        return getattr(self, f"step_{step}")()

    def step_1(self):
        def then(out):
            self.sent, self.far = out, swap_turn(self.sz, out, 1)

        return Job(self.groups(2, 2, []), [self.shape(2, 4)], 0, then)

    def step_2(self):
        def then(out):
            self.sent, self.near = out, swap_turn(self.sz, out, 0)

        return Job(self.groups(1, 1, [(self.far, 1)]), [self.shape(1, 4)], 0, then)

    def step_3(self):
        def then(kept, out):
            self.kept, self.got = kept, swap_far(self.sz, out, 1)

        groups = self.groups(0, 1, [(self.far, 0), (self.near, 0)])
        return Job(groups, [self.shape(1, 2)] * 2, 2, then)

    def step_4(self):
        def then(kept, out):
            self.kept, self.got = kept, swap_far(self.sz, out, 2)

        groups = [[(array, 0, 1, 0, self.members) for array in (self.kept, self.got)]]
        return Job(groups, [self.shape(1, 1, F32), self.shape(1, 1)], 2, then)

    def result(self):
        return (self.kept + self.got.astype(F32)).reshape(self.members, *self.tail)


class Direct:
    def __init__(self, sz, mine, theirs):
        self.sz, self.mine, self.theirs = sz, mine, theirs

    def job(self, step):
        def then(*sent):
            self.sent = sent

        group = [(array, 1, 3, 0, 1) for array in (self.mine, self.other)]
        shape = shaped((1, *self.mine.shape[1:]), BF)
        return Job([group], [shape] * 3, 1, then)


def join(sz, *parts):
    one = object.__new__(Reduction)
    one.sz, one.tail = sz, (64, sz.width)
    plain = [not isinstance(part, Reduction) for part in parts]
    one.members = sum(p.shape[2] if alone else p.members for p, alone in zip(parts, plain))

    def step_3():
        def then(kept, out):
            one.kept, one.sent = kept, out

        groups = []
        for part, alone in zip(parts, plain):
            if alone:
                groups.append([(part, 0, 1, 0, part.shape[2])])
            else:
                groups += part.groups(0, 1, [(part.far, 0), (part.near, 0)])
        return Job(groups, [one.shape(1, 2)] * 2, 2, then)

    one.step_3 = step_3
    return one


def region(flag, fn, *args):
    def nothing(*unused):
        return jax.tree.map(lambda v: jnp.zeros(v.shape, v.dtype), jax.eval_shape(fn, *args))

    return lax.cond(flag, fn, nothing, *args)


def reduce_whole(sz, full):
    members, width = full.shape[1], full.shape[2]
    full = full.transpose(1, 2, 0, 3)
    part = lax.psum_scatter(full, "dp", scatter_dimension=1, tiled=True)
    return lax.psum(part, "tensor").astype(F32)


def gathered_unit(qkv, out):
    qkv = lax.all_gather(qkv, "tensor", axis=2, tiled=True)
    out = lax.all_gather(out, "tensor", axis=0, tiled=True)
    width = qkv.shape[1]
    qkv = qkv.reshape(3, width, PIECES, PAIR).transpose(1, 2, 0, 3)
    return [qkv.reshape(width, PIECES * QKV), out]


def body(
    tokens,
    cotangent,
    block_task,
    sample_len,
    feature_len,
    norm_gain,
    norm_shift,
    sample_qkv,
    sample_out,
    feature_qkv,
    feature_out,
    out_bias,
    up_weight,
    up_bias,
    down_weight,
):
    shape = tokens.shape
    sz = Sizes(shape, lax.axis_size("tensor"), lax.axis_size("dp"))
    rows, width, n = sz.rows, sz.width, sz.tensor
    tokens = tokens.reshape(rows, width)
    cotangent = cotangent.reshape(rows, width)
    gains, shifts, biases = (
        jnp.transpose(v, (1, 0, 2)) for v in (norm_gain, norm_shift, out_bias)
    )
    up_rows = up_bias.reshape(L, PIECES, -1)
    qkvs = [jnp.transpose(v, (0, 2, 1, 3)) for v in (sample_qkv, feature_qkv)]
    outs = [sample_out, feature_out]
    part = functools.partial
    wide = pltpu.VMEM((rows, width), F32)
    strips = pltpu.VMEM((width // TILE, rows, TILE), F32)
    slim = pltpu.VMEM((rows, width), BF)
    dma = pltpu.SemaphoreType.DMA
    row_f32 = shaped((rows, width), F32)
    row_bf = shaped((rows, width), BF)
    chunk_shapes = [shaped((sz.chunk, width), BF)] * n
    proj_shape = shaped((rows, PIECES * QKV), BF)
    small_shape = shaped((8, width), F32)
    half_unit = (width // 2, width)
    sends = [shaped(half_unit, BF)] if sz.fast else []

    *chunks, sent = launch(
        part(start_kernel, sz), "start", (tokens, gains, shifts, qkvs[0], outs[0]),
        [VMEM] * 3 + [ANY] * 2, chunk_shapes + sends, [strips] + [dma((5,))] * len(sends), 3,
    ) if sz.fast else [*launch(
        part(start_kernel, sz), "start", (tokens, gains, shifts, qkvs[0], outs[0]),
        [VMEM] * 3 + [ANY] * 2, chunk_shapes, [strips], 3,
    ), None]

    units = [[None, None] for _ in range(L)]
    members = [[None, None]] + [[0, 1]] * (L - 1)
    mlps = [None] * L
    if sz.fast:

        def pack_mlp(layer_at, after):
            return launch(
                part(pack_mlp_kernel, sz, layer_at), f"pack_mlp_{layer_at}",
                [up_weight, down_weight], [ANY] * 2, [shaped((2, *half_unit), BF)], [dma((2,))],
                2, after,
            )[0]

        got = gather_unit(sz, sent)
        units[0][0] = [qkvs[0], outs[0]] + got
    else:
        for layer_at in range(L):
            for kind in range(2):
                units[layer_at][kind] = gathered_unit(qkvs[kind][layer_at], outs[kind][layer_at])
            up = lax.all_gather(up_weight[layer_at], "tensor", axis=1, tiled=True)
            down = lax.all_gather(down_weight[layer_at], "tensor", axis=0, tiled=True)
            mlps[layer_at] = [up, down]

    def gather_units(layer_at, kinds, sent):
        got = gather_unit(sz, sent)
        for kind in kinds:
            units[layer_at][kind] = [qkvs[kind], outs[kind]] + got

    def gather_mlp(layer_at, sent):
        mlps[layer_at] = [up_weight, down_weight] + gather_unit(sz, sent)

    def arrived(parts, count):
        return parts[2 : 2 + count] if sz.fast else []

    unit_specs = [ANY] * unit_parts(sz)
    mlp_specs = [ANY] * unit_parts(sz)
    unit_scratch = [
        pltpu.VMEM((width, PIECES * QKV), BF),
        pltpu.VMEM((width, width), BF),
        dma((22 if sz.fast else 2,)),
    ]
    mlp_scratch = [
        pltpu.VMEM((width, PIECES * width), BF),
        pltpu.VMEM((PIECES * width, width), BF),
        dma((14 if sz.fast else 2,)),
    ]
    hidden = pltpu.VMEM((rows, PIECES * width), BF)
    square = pltpu.VMEM((width, width), BF)

    state = tokens
    kept = []
    for layer_at in range(L):
        entry = state
        got = exchange(sz, chunks)
        slots = sz.own_feats
        began = []
        if sz.fast and layer_at == 0:
            half_mlp, half_units = shaped((2, *half_unit), BF), shaped((2, *half_unit), BF)
            sent, sent_mlp, *waiting = launch(
                part(pack_early_kernel, sz), "pack_early",
                (qkvs[0], outs[0], qkvs[1], outs[1], up_weight, down_weight), [ANY] * 6,
                [shaped(half_unit, BF), half_mlp, half_units], [dma((17,))], 2,
                got[1:] + arrived(units[0][0], 2),
            )
            gather_units(0, (1,), sent)
            gather_mlp(0, sent_mlp)
            began = [sent, sent_mlp]
        elif sz.fast:
            sent = pack_mlp(layer_at, got[1:] + arrived(units[layer_at][0], 2))
            gather_mlp(layer_at, sent)
            began = [sent]
        *back, proj_s, mixed_s, probs_s = launch(
            part(sample_kernel, sz, layer_at, members[layer_at][0]), f"sample_{layer_at}",
            (block_task, sample_len, *got, *units[layer_at][0]),
            [SMEM] * 2 + [VMEM] * n + unit_specs,
            chunk_shapes
            + [proj_shape, row_bf, shaped((PIECES, slots, 2, sz.group, sz.group), BF)],
            [slim, pltpu.VMEM((sz.group, sz.group), F32), *unit_scratch],
            8, began, early={n: 1, n + 1: PIECES, n + 2: PIECES},
        )
        back = exchange(sz, back)
        tiles = rows // TILE
        passed = waiting if sz.fast and layer_at < L - 1 else []
        state_1, state_2, normed_m, proj_f, mixed_f, probs_f, *passed = launch(
            part(feature_kernel, sz, layer_at, members[layer_at][1]), f"feature_{layer_at}",
            (feature_len, state, gains, shifts, biases, *back, *units[layer_at][1]),
            [SMEM] + [VMEM] * (4 + n) + unit_specs,
            [row_f32, row_f32, row_bf, proj_shape, row_bf,
             shaped((PIECES, tiles, 2, TILE, TILE), BF)],
            [strips, wide, slim, *unit_scratch],
            9, through=passed,
        )
        if layer_at < L - 1:
            if sz.fast:
                gather_units(layer_at + 1, (0, 1), passed[0])
            state, *chunks = launch(
                part(mlp_kernel, sz, layer_at), f"mlp_{layer_at}",
                (state_2, normed_m, up_rows, gains, shifts, biases, *mlps[layer_at]),
                [VMEM] * 6 + mlp_specs,
                [row_f32] + chunk_shapes,
                [strips, wide, hidden, *mlp_scratch],
                9,
            )
        kept.append((entry, got, proj_s, mixed_s, probs_s, state_1, state_2, normed_m,
                     proj_f, mixed_f, probs_f))

    reductions, whole, done = {}, {}, {}

    def reduction(layer_at, kind, parts):
        if sz.fast and layer_at == 0 and kind < 2:
            reductions[layer_at, kind] = Direct(sz, *parts)
        elif sz.fast:
            reductions[layer_at, kind] = Reduction(sz, parts)
        else:
            (whole[layer_at, kind],) = parts

    def jobs(*steps):
        return [reductions[at[:2]].job(at[2]) for at in steps if at[:2] in reductions]

    def add_up(name, after, *steps, through=()):
        todo = jobs(*steps)
        if not todo:
            return []
        return launch(
            part(nothing_kernel, sz), name, [], [], [], [], 0.05, after, todo, through=through
        )

    smalls = [None] * L

    def small_rows():
        return jnp.concatenate([one for layer in smalls for one in layer], axis=0)

    for layer_at in reversed(range(L)):
        (entry, got, proj_s, mixed_s, probs_s, state_1, state_2, normed_m,
         proj_f, mixed_f, probs_f) = kept[layer_at]
        above = layer_at + 1
        if layer_at == L - 1:
            output, grad, small_m, *parts = launch(
                part(last_mlp_kernel, sz, layer_at), f"last_mlp_{layer_at}",
                (sample_len, feature_len, cotangent, state_2, normed_m, up_rows, gains, biases,
                 *mlps[layer_at]),
                [SMEM] * 2 + [VMEM] * 6 + mlp_specs,
                [row_bf, row_f32, small_shape] + grad_shapes(sz, 2),
                [wide, wide, wide, slim, hidden, hidden, square, *mlp_scratch],
                15,
            )
        else:
            grad, small_m, *parts = launch(
                part(mlp_back_kernel, sz, layer_at), f"mlp_back_{layer_at}",
                (grad, kept[above][0], state_2, normed_m, up_rows, gains, *back,
                 *mlps[layer_at]),
                [VMEM] * (6 + n) + mlp_specs,
                [row_f32, small_shape] + grad_shapes(sz, 2),
                [wide, strips, wide, wide, slim, hidden, hidden, square, *mlp_scratch],
                15, parts[:1], early={2: 2 * PIECES, 3: 2 * PIECES} if sz.fast else None,
            )
        reduction(layer_at, 2, parts)
        began = []
        if layer_at < L - 1 and sz.fast:
            add_up(f"sums_{layer_at}", [grad], (above, 2, 3), (above, 1, 2), (above, 0, 1))
            began = [reductions[above, 1].sent, reductions[above, 0].sent]
        grad, low, proj_grad, normed, small_f, *chunks = launch(
            part(feature_back_kernel, sz, layer_at, members[layer_at][1]),
            f"feature_back_{layer_at}",
            (grad, state_1, proj_f, probs_f, gains, shifts, *units[layer_at][1]),
            [VMEM] * 6 + unit_specs,
            [row_f32, row_bf, proj_shape, row_bf, small_shape] + chunk_shapes,
            [slim, strips, wide, *unit_scratch],
            9, began,
        )
        smalls[layer_at] = [small_m, small_f]
        chunks = exchange(sz, chunks)
        parts = launch(
            part(matrix_grad_kernel, sz, 1, layer_at == 0), f"feature_matrix_{layer_at}",
            (proj_grad, low, mixed_f, normed), [VMEM] * 4, grad_shapes(sz, 1),
            [pltpu.VMEM((PIECES, width, width), BF)], 0.7,
            jobs=jobs((layer_at, 2, 1), (above, 0, 2), (above, 2, 4)),
        )
        reduction(layer_at, 1, parts)
        others = []
        if layer_at == 0 and sz.fast:
            others = [one for layer in smalls for one in layer]
        *back, low, proj_grad, small_s = launch(
            part(sample_back_kernel, sz, layer_at, members[layer_at][0], len(others)),
            f"sample_back_{layer_at}",
            (proj_s, probs_s, gains, shifts, *others, *chunks, *got, *units[layer_at][0]),
            [VMEM] * (4 + len(others) + 2 * n) + unit_specs,
            chunk_shapes + [row_bf, proj_shape, shaped((24 * L, width), F32) if others else small_shape],
            [slim, slim, *unit_scratch],
            9, parts[:1],
        )
        smalls[layer_at].append(small_s)
        began = []
        if not sz.fast or layer_at > 0:
            back = exchange(sz, back)
        if sz.fast and layer_at == 0:
            reductions[1, 3] = upper = join(sz, reductions[1, 1], reductions[1, 0])
            began = [reductions[1, 2].got, reductions[1, 1].near, reductions[1, 0].near]
            rows_small = small_s
            reductions[0, 1].other = swap_cores(sz, reductions[0, 1].theirs)
        parts = launch(
            part(matrix_grad_kernel, sz, n, layer_at == 0), f"sample_matrix_{layer_at}",
            (proj_grad, low, mixed_s, *got), [VMEM] * (3 + n), grad_shapes(sz, 1),
            [pltpu.VMEM((PIECES, width, width), BF), slim], 0.7, began,
            jobs((layer_at, 1, 1), *(((layer_at, 2, 2),) if layer_at else ((1, 3, 3),))),
        )
        reduction(layer_at, 0, parts)
    def last_norm(back):
        (tokens_grad,) = launch(
            part(last_norm_kernel, sz), "last_norm", (grad, tokens, gains, *back),
            [VMEM] * (3 + n), [row_f32], [strips], 5,
        )
        return tokens_grad

    if sz.fast:
        first, last = reductions[0, 1], reductions[0, 0]
        block = shaped((16 * L, width), F32)
        mlp = reductions[0, 2]

        def near_region(pieces, mine, theirs, rows_own):
            got = [swap_near(sz, v, at + 1) for at, v in enumerate(pieces)]
            other, rows_other = swap_cores(sz, theirs), swap_cores(sz, rows_own)
            results, (mlp_sent,) = launch(
                part(send_near_kernel, sz), "send_near", (mine, other, rows_own, rows_other),
                [VMEM] * 4, [shaped((256 + 16 * L, width), BF)] * 3 + [block], [], 5, [],
                [mlp.job(2)], defer=True,
            )
            return got, other, results, mlp_sent

        upper.got = swap_far(sz, upper.sent, 1)
        first.got, last.other, (*sent, rows_kept), mlp_sent = region(
            sample_len[0] > 0, near_region, first.sent, last.mine, last.theirs, rows_small
        )
        mlp.near = swap_turn(sz, mlp_sent, 0)
        last.got = [swap_near(sz, v, at + 1) for at, v in enumerate(sent)]
        add_up("sums_upper", [rows_kept], (1, 3, 4))
        back = add_up("sums_mlp", [rows_kept, upper.kept], (0, 2, 3), through=back)
        attention_kept, rows_kept, *sent = launch(
            part(send_far_kernel, sz), "send_far",
            (first.mine, first.other, *first.got, last.mine, last.other, *last.got, rows_kept),
            [VMEM] * 11, [shaped((2, 64, width), F32), block] + [shaped((128 + 16 * L, width), BF)] * 3,
            [], 0.05, [mlp.kept, upper.got],
        )
        add_up("sums_late", [rows_kept], (0, 2, 4))
        got = [swap_far(sz, v, at + 1) for at, v in enumerate(sent)]
        tokens_grad = last_norm(exchange(sz, back))
        upper_mlp = reductions[1, 2]
        qkv_shape, out_shape = shaped((L, 3, 64, PAIR), F32), shaped((L, 64, PAIR), F32)
        wide_shape, row_shape = shaped((L, 64, width), F32), shaped((3, L, width), F32)
        (s_qkv, s_out, f_qkv, f_out, up, down, gain_total, shift_total, bias_total,
         up_bias_total) = launch(
            part(last_sums_kernel, sz), "last_sums",
            (attention_kept, rows_kept, *got, mlp.kept, mlp.got, upper_mlp.kept, upper_mlp.got,
             upper.kept, upper.got), [VMEM] * 11,
            [qkv_shape, out_shape, qkv_shape, out_shape, wide_shape, wide_shape,
             row_shape, row_shape, row_shape, shaped((L, PIECES * width), F32)], [], 0.05,
        )

        def turned(v):
            return jnp.transpose(v, (0, 2, 1))

        gain_total, shift_total, bias_total = (
            jnp.transpose(v, (1, 0, 2)) for v in (gain_total, shift_total, bias_total)
        )
        return (
            output.reshape(shape), tokens_grad.reshape(shape), gain_total, shift_total,
            jnp.transpose(s_qkv, (0, 2, 1, 3)), turned(s_out),
            jnp.transpose(f_qkv, (0, 2, 1, 3)), turned(f_out),
            bias_total, up, up_bias_total, turned(down),
        )
    tokens_grad = last_norm(back)
    early = lax.psum(small_rows(), ("dp", "tensor"))
    early = early.reshape(-1, 8, width)
    by_layer = []
    at = 0
    for layer_at in range(L):
        count = len(smalls[layer_at])
        sums = [early[at + member] for member in range(count)]
        at += count
        by_layer.append(sums)
    gain_total, shift_total = (
        jnp.stack([jnp.stack([s[row], f[row], m[row]]) for m, f, s in by_layer])
        for row in range(2)
    )
    bias_total = jnp.stack([jnp.stack([f[3], f[2], m[2]]) for m, f, s in by_layer])
    up_bias_total = jnp.stack([m[3 : 3 + PIECES].reshape(-1) for m, f, s in by_layer])

    if not sz.fast:
        for key, full in whole.items():
            done[key] = reduce_whole(sz, full)

    def attention_grads(kind):
        qkv, out = [], []
        for layer_at in range(L):
            if sz.fast:
                value = done[layer_at, kind][0]
                qkv.append(value[:, :QKV].reshape(-1, 3, PAIR))
                out.append(value[:, QKV:].T)
            else:
                value = done[layer_at, kind][0]
                columns = width // n
                start = lax.axis_index("tensor") * columns
                whole = value[:, :, :QKV].reshape(-1, PIECES, 3, PAIR).transpose(0, 2, 1, 3)
                whole = whole.reshape(-1, 3, width)
                qkv.append(lax.dynamic_slice_in_dim(whole, start, columns, 2))
                whole = value[:, :, QKV:].reshape(-1, width)
                out.append(lax.dynamic_slice_in_dim(whole, start, columns, 1).T)
        return jnp.stack(qkv), jnp.stack(out)

    sample_qkv_grad, sample_out_grad = attention_grads(0)
    feature_qkv_grad, feature_out_grad = attention_grads(1)
    ups, downs = [], []
    for layer_at in range(L):
        value = done[layer_at, 2]
        if not sz.fast:
            columns = PIECES * width // n
            start = lax.axis_index("tensor") * columns
            value = value.reshape(2, -1, PIECES * width)
            value = lax.dynamic_slice_in_dim(value, start, columns, 2)
        ups.append(value[0])
        downs.append(value[1].T)
    return (
        output.reshape(shape),
        tokens_grad.reshape(shape),
        gain_total,
        shift_total,
        sample_qkv_grad,
        sample_out_grad,
        feature_qkv_grad,
        feature_out_grad,
        bias_total,
        jnp.stack(ups),
        up_bias_total,
        jnp.stack(downs),
    )


def solution(mesh):
    placed = (
        P("dp", "tensor", None, None),
        P("dp", "tensor", None, None),
        P("dp"),
        P("dp"),
        P("dp"),
        P(),
        P(),
        P(None, None, None, "tensor"),
        P(None, "tensor", None),
        P(None, None, None, "tensor"),
        P(None, "tensor", None),
        P(),
        P(None, None, "tensor"),
        P(),
        P(None, "tensor", None),
    )
    return jax.shard_map(
        body,
        mesh=mesh,
        in_specs=placed,
        out_specs=(
            P("dp", "tensor", None, None),
            P("dp", "tensor", None, None),
            P(),
            P(),
            P(None, "dp", None, "tensor"),
            P(None, "tensor", "dp"),
            P(None, "dp", None, "tensor"),
            P(None, "tensor", "dp"),
            P(),
            P(None, "dp", "tensor"),
            P(),
            P(None, "tensor", "dp"),
        ),
        check_vma=False,
    )
```

```python
import functools

import jax
import jax.numpy as jnp
from jax import lax
from jax.experimental import pallas as pl
from jax.experimental.pallas import tpu as pltpu
from jax.sharding import PartitionSpec as P

HD = 64
L = 2
PIECES = 4
PAIR = 2 * HD
QKV = 3 * PAIR
TILE = 128

epsilon = 1e-05
masked_score = -1e30
SCALE = HD ** (-0.5)
F32 = jnp.float32
BF = jnp.bfloat16
NT = (((1,), (1,)), ((), ()))
TN = (((0,), (0,)), ((), ()))
TANH_A = 0.7978845608028654
TANH_B = 0.044715
VMEM_GRANT = 66977792
SMALL = ((0, 0, 7), (7, 8, 4), (11, 16, 2))
VMEM = pl.BlockSpec(memory_space=pltpu.VMEM)
SMEM = pl.BlockSpec(memory_space=pltpu.SMEM)
ANY = pl.BlockSpec(memory_space=pl.ANY)


class Sizes:
    def __init__(self, shape, tensor, dp):
        self.blocks, self.samples, self.feats, self.width = shape
        self.tensor, self.dp = tensor, dp
        self.rows = self.blocks * self.samples * self.feats
        self.own_feats = self.feats // tensor
        self.run = self.blocks * self.samples
        self.chunk = self.own_feats * self.run
        self.group = tensor * self.run
        self.block_rows = self.samples * self.feats
        self.fast = tensor == 4 and dp == 8


def places(z):
    tensor_at = lax.axis_index("tensor")
    dp_at = lax.axis_index("dp")
    return tensor_at, lax.rem(dp_at, 2), lax.div(dp_at, 2)


def dot(a, b):
    return jnp.dot(a, b, preferred_element_type=F32)


def dot_nt(a, b):
    return lax.dot_general(a, b, NT, preferred_element_type=F32)


def dot_tn(a, b):
    return lax.dot_general(a, b, TN, preferred_element_type=F32)


def normal_rows(x):
    centre = x - jnp.mean(x, axis=-1, keepdims=True)
    spread = jnp.mean(centre * centre, axis=-1, keepdims=True)
    rate = lax.rsqrt(spread + epsilon)
    return centre * rate, rate


def over_rows(rows, fn, carry=0, step=64):
    for at in range(rows // step):
        carry = fn(slice(at * step, (at + 1) * step), carry)
    return carry


def fold(x):
    return jnp.sum(x.reshape(-1, 8, x.shape[-1]), axis=0)


def total(x):
    return jnp.sum(x, axis=0, keepdims=True)


def put_strips(strips, rows, value):
    for lane in range(value.shape[1] // TILE):
        strips[lane, rows, :] = value[:, lane * TILE : (lane + 1) * TILE]


def get_strips(strips, rows):
    return jnp.concatenate([strips[lane, rows, :] for lane in range(strips.shape[0])], axis=1)


def feature_slot(sz, tensor_at, at, slot):
    return (tensor_at ^ at) * sz.own_feats + slot


def spread_out(sz, tensor_at, wide, chunks):
    for at in range(sz.tensor):
        for slot in range(sz.own_feats):
            first = feature_slot(sz, tensor_at, at, slot)
            for lane in range(sz.width // TILE):
                rows = wide[lane, pl.ds(first, sz.run, stride=sz.feats), :]
                chunks[at][
                    slot * sz.run : (slot + 1) * sz.run, lane * TILE : (lane + 1) * TILE
                ] = rows.astype(BF)


def bring_back(sz, tensor_at, chunks, wide):
    for at in range(sz.tensor):
        for slot in range(sz.own_feats):
            first = feature_slot(sz, tensor_at, at, slot)
            for lane in range(sz.width // TILE):
                rows = chunks[at][
                    slot * sz.run : (slot + 1) * sz.run, lane * TILE : (lane + 1) * TILE
                ]
                wide[lane, pl.ds(first, sz.run, stride=sz.feats), :] = rows.astype(F32)


def by_feature(sz, chunks, x):
    for at in range(sz.tensor):
        for slot in range(sz.own_feats):
            first = slot * sz.group + at * sz.run
            x[first : first + sz.run, :] = chunks[at][slot * sz.run : (slot + 1) * sz.run, :]


def to_chunks(sz, value, chunks):
    for at in range(sz.tensor):
        for slot in range(sz.own_feats):
            first = slot * sz.group + at * sz.run
            chunks[at][slot * sz.run : (slot + 1) * sz.run, :] = value[
                first : first + sz.run
            ].astype(BF)


def where_halves(core):
    other = 1 - core
    return (
        (1 + core, core),
        (2 - core, core),
        (3, core),
        (1 + other, other),
        (2 - other, other),
        (3, other),
    )


def load_unit(sz, layer_at, member, parts, w, w_out, sems, core):
    pairs = []
    if not sz.fast:
        pairs += [(parts[0], w), (parts[1], w_out)]
    else:
        qkv, out = parts[:2]
        for at in range(3):
            pairs.append((qkv.at[layer_at, at], w.at[:, pl.ds(at * PAIR, PAIR)]))
        pairs.append((out.at[layer_at], w_out.at[pl.ds(0, PAIR), :]))
        half_rows = sz.width // 2
        for source, (piece, half) in zip(parts[2:], where_halves(core)):
            if member is not None:
                source = source.at[member]
            start = pl.multiple_of(half * half_rows, half_rows)
            first = pl.multiple_of(piece * QKV, TILE)
            pairs.append(
                (source.at[:, pl.ds(0, QKV)], w.at[pl.ds(start, half_rows), pl.ds(first, QKV)])
            )
            first = pl.multiple_of(piece * PAIR, TILE)
            for block in range(half_rows // TILE):
                lanes = pl.ds(pl.multiple_of(start + block * TILE, TILE), TILE)
                pairs.append(
                    (
                        source.at[pl.ds(block * TILE, TILE), pl.ds(QKV, PAIR)],
                        w_out.at[pl.ds(first, PAIR), lanes],
                    )
                )
    return begin(pairs, sems)


def begin(pairs, sems):
    copies = []
    for source, target in pairs:
        copies.append(pltpu.make_async_copy(source, target, sems.at[len(copies)]))
        copies[-1].start()
    return copies


def finish(copies):
    for copy in copies:
        copy.wait()


def load_mlp(sz, layer_at, parts, up, down, sems, core):
    pairs = []
    if not sz.fast:
        pairs += [(parts[0], up), (parts[1], down)]
    else:
        width = sz.width
        pairs.append((parts[0].at[layer_at], up.at[:, pl.ds(0, width)]))
        pairs.append((parts[1].at[layer_at], down.at[pl.ds(0, width), :]))
        half_rows = width // 2
        for source, (piece, half) in zip(parts[2:], where_halves(core)):
            start = pl.multiple_of(half * half_rows, half_rows)
            first = pl.multiple_of(piece * width, width)
            pairs.append(
                (source.at[0], up.at[pl.ds(start, half_rows), pl.ds(first, width)])
            )
            rows = pl.ds(pl.multiple_of(first + start, half_rows), half_rows)
            pairs.append((source.at[1], down.at[rows, :]))
    return begin(pairs, sems)


def put_grad(sz, grads, outs, piece, member, core, z, direct=False):
    if not sz.fast:
        outs[0][piece, member] = grads[...]
        return
    mine, theirs = outs
    if direct or piece in (0, 3):
        at_mine = at_theirs = piece
    elif piece == 1:
        at_mine, at_theirs = 1 + core, 2 - core
    else:
        at_mine, at_theirs = 2 - core, 1 + core
    for place, near in enumerate((0, 1, 2, 3) if direct else (0, 2, 1, 3)):
        first = (z ^ near) * 128
        rows_mine = pl.ds(pl.multiple_of(first + core * 64, 64), 64)
        rows_theirs = pl.ds(pl.multiple_of(first + (1 - core) * 64, 64), 64)
        mine[at_mine, place, member] = grads[rows_mine, :]
        theirs[at_theirs, place, member] = grads[rows_theirs, :]
    flush(mine, at_mine, slice(None), member)
    flush(theirs, at_theirs, slice(None), member)


def head_masks():
    lane = lax.broadcasted_iota(jnp.int32, (1, PAIR), 1)
    return lane < HD, lane >= HD


def sample_bias(sz, tensor_at, tasks, lengths, bias):
    def of(index):
        run_at = index // sz.run
        block = (index // sz.samples) % sz.blocks
        sample = (run_at ^ tensor_at) * sz.samples + index % sz.samples
        task = jnp.zeros_like(index)
        length = jnp.zeros_like(index)
        for at in range(sz.blocks):
            task = jnp.where(block == at, tasks[at], task)
            length = jnp.where(block == at, lengths[at], length)
        return task, sample < length

    row_task, unused = of(lax.broadcasted_iota(jnp.int32, (sz.group, 1), 0))
    key_task, key_live = of(lax.broadcasted_iota(jnp.int32, (1, sz.group), 1))
    key_task = jnp.where(key_live, key_task, -1)
    bias[...] = jnp.where(row_task == key_task, 0.0, masked_score)


def feature_bias(sz, length):
    row = lax.broadcasted_iota(jnp.int32, (TILE, TILE), 0)
    key = lax.broadcasted_iota(jnp.int32, (TILE, TILE), 1)
    same = (row // sz.feats) == (key // sz.feats)
    return jnp.where(same & (key % sz.feats < length), 0.0, masked_score)


def attend(proj, piece, jobs, probs, mixed):
    masks = head_masks()
    first = piece * QKV
    scores = []
    for rows, bias, place in jobs:
        query = proj[rows, first : first + PAIR]
        key = proj[rows, first + PAIR : first + 2 * PAIR]
        for mask in masks:
            scores.append(dot_nt(jnp.where(mask, query, 0) * SCALE, key) + bias)
    tops = [jnp.max(part, axis=-1, keepdims=True) for part in scores]
    weights = [jnp.exp(part - top) for part, top in zip(scores, tops)]
    shares = [1.0 / jnp.sum(part, axis=-1, keepdims=True) for part in weights]
    weights = [(part * share).astype(BF) for part, share in zip(weights, shares)]
    for at, (rows, bias, place) in enumerate(jobs):
        value = proj[rows, first + 2 * PAIR : first + QKV]
        pair = weights[2 * at : 2 * at + 2]
        for head in range(2):
            probs[piece, place, head] = pair[head]
        mixed[rows, piece * PAIR : (piece + 1) * PAIR] = jnp.where(
            masks[0], dot(pair[0], value), dot(pair[1], value)
        ).astype(BF)
    flush(probs, piece)
    flush(mixed, slice(None), pl.ds(piece * PAIR, PAIR))


def attend_back(proj, piece, jobs, probs, mixed_grad, proj_grad):
    masks = head_masks()
    first = piece * QKV
    head_grads, weights, weight_grads = [], [], []
    for rows, place in jobs:
        grad = mixed_grad[rows, piece * PAIR : (piece + 1) * PAIR]
        value = proj[rows, first + 2 * PAIR : first + QKV]
        for head, mask in enumerate(masks):
            head_grads.append(jnp.where(mask, grad, 0))
            weights.append(probs[piece, place, head])
            weight_grads.append(dot_nt(head_grads[-1], value))
    score_grads = []
    for low, grad in zip(weights, weight_grads):
        wide = low.astype(F32)
        product = wide * grad
        score_grads.append((product - wide * jnp.sum(product, axis=-1, keepdims=True)).astype(BF))
    for at, (rows, place) in enumerate(jobs):
        query = proj[rows, first : first + PAIR]
        key = proj[rows, first + PAIR : first + 2 * PAIR]
        one, two = score_grads[2 * at : 2 * at + 2]
        queries = jnp.where(masks[0], dot(one, key), dot(two, key)) * SCALE
        keys = dot_tn(one, jnp.where(masks[0], query, 0))
        keys = (keys + dot_tn(two, jnp.where(masks[1], query, 0))) * SCALE
        values = dot_tn(weights[2 * at], head_grads[2 * at])
        values = values + dot_tn(weights[2 * at + 1], head_grads[2 * at + 1])
        proj_grad[rows, first : first + PAIR] = queries.astype(BF)
        proj_grad[rows, first + PAIR : first + 2 * PAIR] = keys.astype(BF)
        proj_grad[rows, first + 2 * PAIR : first + QKV] = values.astype(BF)
    flush(proj_grad, slice(None), pl.ds(first, QKV))


def norm_back_rows(state, incoming, gain):
    xhat, rate = normal_rows(state)
    inner = incoming * gain
    back = rate * (
        inner
        - jnp.mean(inner, axis=-1, keepdims=True)
        - xhat * jnp.mean(inner * xhat, axis=-1, keepdims=True)
    )
    return xhat, back


def pack_copies(sz, layer_at, qkv, out, sent, core):
    half = sz.width // 2
    rows = pl.ds(pl.multiple_of(core * half, half), half)
    pairs = []
    for at in range(3):
        pairs.append((qkv.at[layer_at, at, rows, :], sent.at[:, pl.ds(at * PAIR, PAIR)]))
    for block in range(half // TILE):
        lanes = pl.ds(pl.multiple_of(core * half + block * TILE, TILE), TILE)
        pairs.append(
            (out.at[layer_at, :, lanes], sent.at[pl.ds(block * TILE, TILE), pl.ds(QKV, PAIR)])
        )
    return pairs


def start_kernel(sz, tokens, gains, shifts, qkv, out, *rest):
    chunks, rest = rest[: sz.tensor], rest[sz.tensor :]
    tensor_at, core, z = places(sz)
    copies = []
    if sz.fast:
        sent, strips, sems = rest
        copies = begin(pack_copies(sz, 0, qkv, out, sent, core), sems)
    else:
        (strips,) = rest

    def rows_of(rows, kept):
        xhat, unused = normal_rows(tokens[rows, :].astype(F32))
        put_strips(strips, rows, xhat * gains[0, 0:1, :] + shifts[0, 0:1, :])
        return kept

    over_rows(sz.rows, rows_of)
    spread_out(sz, tensor_at, strips, chunks)
    finish(copies)


def pack_mlp_kernel(sz, layer_at, up, down, sent, sems):
    tensor_at, core, z = places(sz)
    finish(begin(mlp_pairs(sz, layer_at, up, down, sent, core), sems))


def mlp_pairs(sz, layer_at, up, down, sent, core):
    half = sz.width // 2
    rows = pl.ds(pl.multiple_of(core * half, half), half)
    return [(w.at[layer_at, rows, :], sent.at[at]) for at, w in enumerate((up, down))]


def pack_early_kernel(sz, sample_qkv, sample_out, feature_qkv, feature_out, up, down, *rest):
    first, mlp, units, sems = rest
    tensor_at, core, z = places(sz)
    pairs = pack_copies(sz, 0, feature_qkv, feature_out, first, core)
    pairs += mlp_pairs(sz, 0, up, down, mlp, core)
    pairs += pack_copies(sz, 1, sample_qkv, sample_out, units.at[0], core)
    pairs += pack_copies(sz, 1, feature_qkv, feature_out, units.at[1], core)
    finish(begin(pairs, sems))


def nothing_kernel(sz, *rest):
    pass


def send_near_kernel(sz, mine, other, rows, rows_other, *outs):
    kept = outs[-1]
    kept[...] = jnp.zeros_like(kept)
    for layer_at in range(L):
        for at, first, count in SMALL:
            here = slice(24 * layer_at + first, 24 * layer_at + first + count)
            there = slice(16 * layer_at + at, 16 * layer_at + at + count)
            kept[there, :] = rows[here, :] + rows_other[here, :]
    small = kept[...].astype(BF)
    kept[...] = small.astype(F32)
    for piece in range(1, PIECES):
        out = outs[piece - 1]
        for near in range(4):
            value = mine[piece, near, 0].astype(F32) + other[piece, near, 0].astype(F32)
            out[near * 64 : near * 64 + 64, :] = value.astype(BF)
        out[256:, :] = small


def pairwise(one, two, three, four):
    return (one + two) + (three + four)


def send_far_kernel(sz, *refs):
    first, last, small, outs = refs[:5], refs[5:10], refs[10], refs[11:16]
    kept, rows, sends = outs[0], outs[1], outs[2:]
    *held, sems = refs[16:]
    sources = (first[0], first[1], last[0], last[1])
    copies = begin([(ref.at[0], target) for ref, target in zip(sources, held)], sems)
    first, last = (*held[:2], *first[2:]), (*held[2:], *last[2:])
    finish(copies)

    def value(unit, at, near):
        mine, other, *got = unit
        out = mine[near, 0].astype(F32) + other[near, 0].astype(F32)
        for one in got:
            got_here = one[0, near, 0] if at == 0 else one[near * 64 : near * 64 + 64, :]
            out = out + got_here.astype(F32)
        return out

    x, y, d = (one[256:, :].astype(F32) for one in last[2:])
    low = pairwise(small[...], x, y, d).astype(BF)
    rows[...] = low.astype(F32)
    for at, unit in enumerate((first, last)):
        kept[at] = value(unit, at, 0)
        for near in range(1, 4):
            sends[near - 1][at * 64 : at * 64 + 64, :] = value(unit, at, near).astype(BF)
    for near in range(1, 4):
        sends[near - 1][128:, :] = low


def last_sums_kernel(sz, *refs):
    kept, rows, one, two, three, mlp, mlp_got, upper_mlp, upper_mlp_got = refs[:9]
    upper, upper_got = refs[9:11]
    s_qkv, s_out, f_qkv, f_out, up, down, gain, shift, bias, up_bias = refs[11:]
    small = pairwise(rows[...], *(got[128:, :].astype(F32) for got in (one, two, three)))

    def attention(layer_at, value, qkv, out):
        for at in range(3):
            qkv[layer_at, at] = value[:, at * PAIR : (at + 1) * PAIR]
        out[layer_at] = value[:, QKV:]

    for at, (qkv, out) in enumerate(((f_qkv, f_out), (s_qkv, s_out))):
        value = kept[at]
        for got in (one, two, three):
            value = value + got[at * 64 : at * 64 + 64, :].astype(F32)
        attention(0, value, qkv, out)
        attention(1, upper[0, 0, at] + upper_got[0, 0, at].astype(F32), qkv, out)
    for at, w in enumerate((up, down)):
        w[0] = mlp[0, 0, at] + mlp_got[0, 0, at].astype(F32)
        w[1] = upper_mlp[0, 0, at] + upper_mlp_got[0, 0, at].astype(F32)
    for layer_at in range(L):
        m, f, s = (16 * layer_at + at for at, first, count in SMALL)
        for out, places_in in ((gain, (s, f, m)), (shift, (s + 1, f + 1, m + 1)),
                               (bias, (f + 3, f + 2, m + 2))):
            for at, row in enumerate(places_in):
                out[at, layer_at : layer_at + 1, :] = small[row : row + 1]
        for piece in range(PIECES):
            lanes = slice(piece * sz.width, (piece + 1) * sz.width)
            row = m + 3 + piece
            up_bias[layer_at : layer_at + 1, lanes] = small[row : row + 1]


def unit_parts(sz):
    return 8 if sz.fast else 2


def sample_kernel(sz, layer_at, member, tasks, lengths, *rest):
    n, parts = sz.tensor, unit_parts(sz)
    chunks, weights = rest[:n], rest[n : n + parts]
    outs = rest[n + parts :]
    back, proj, mixed, probs = outs[:n], outs[n], outs[n + 1], outs[n + 2]
    x, bias, w, w_out, sems = outs[n + 3 :]
    tensor_at, core, z = places(sz)
    copies = load_unit(sz, layer_at, member, weights, w, w_out, sems, core)
    by_feature(sz, chunks, x)
    sample_bias(sz, tensor_at, tasks, lengths, bias)
    finish(copies)
    proj[...] = dot(x[...], w[...]).astype(BF)
    flush(proj)
    jobs = [
        (slice(slot * sz.group, (slot + 1) * sz.group), bias[...], slot)
        for slot in range(sz.own_feats)
    ]
    for piece in range(PIECES):
        attend(proj, piece, jobs, probs, mixed)
    to_chunks(sz, dot(mixed[...], w_out[...]), back)


def feature_kernel(sz, layer_at, member, lengths, state, gains, shifts, out_bias, *rest):
    n, parts = sz.tensor, unit_parts(sz)
    chunks, weights = rest[:n], rest[n : n + parts]
    state_1, state_2, normed_m, proj, mixed, probs = rest[n + parts : n + parts + 6]
    strips, wide, normed, w, w_out, sems = rest[n + parts + 6 :]
    tensor_at, core, z = places(sz)
    copies = load_unit(sz, layer_at, member, weights, w, w_out, sems, core)
    bring_back(sz, tensor_at, chunks, strips)
    at = slice(layer_at, layer_at + 1)

    def before(rows, kept):
        value = state[rows, :].astype(F32) + get_strips(strips, rows) + out_bias[0, at, :]
        state_1[rows, :] = value
        xhat, unused = normal_rows(value)
        normed[rows, :] = (xhat * gains[1, at, :] + shifts[1, at, :]).astype(BF)
        return kept

    over_rows(sz.rows, before)
    biases = [feature_bias(sz, lengths[block]) for block in range(sz.blocks)]
    jobs = [
        (slice(tile * TILE, (tile + 1) * TILE), biases[tile * TILE // sz.block_rows], tile)
        for tile in range(sz.rows // TILE)
    ]
    finish(copies)
    flush(state_1)
    proj[...] = dot(normed[...], w[...]).astype(BF)
    flush(proj)
    for piece in range(PIECES):
        attend(proj, piece, jobs, probs, mixed)
    wide[...] = dot(mixed[...], w_out[...])

    def after(rows, kept):
        value = state_1[rows, :] + wide[rows, :] + out_bias[1, at, :]
        state_2[rows, :] = value
        xhat, unused = normal_rows(value)
        normed_m[rows, :] = (xhat * gains[2, at, :] + shifts[2, at, :]).astype(BF)
        return kept

    over_rows(sz.rows, after)


def up_bias_rows(sz, tensor_at, piece):
    return (tensor_at ^ piece) if sz.fast else piece


def mlp_kernel(sz, layer_at, state_2, normed_m, up_bias, gains, shifts, out_bias, *rest):
    n = sz.tensor
    parts = 8 if sz.fast else 2
    weights, (state_3, *chunks) = rest[:parts], rest[parts : parts + 1 + n]
    strips, wide, hidden, up, down, sems = rest[parts + 1 + n :]
    tensor_at, core, z = places(sz)
    finish(load_mlp(sz, layer_at, weights, up, down, sems, core))
    width = sz.width
    for piece in range(PIECES):
        lanes = slice(piece * width, (piece + 1) * width)
        wide[...] = dot(normed_m[...], up[:, lanes])
        shift = up_bias[layer_at, pl.ds(up_bias_rows(sz, tensor_at, piece), 1), :]
        value = wide[...] + shift
        half = 0.5 + 0.5 * jnp.tanh(value * (TANH_A + TANH_A * TANH_B * (value * value)))
        hidden[:, lanes] = (value * half).astype(BF)
    wide[...] = dot(hidden[...], down[...])
    at = slice(layer_at, layer_at + 1)
    later = slice(layer_at + 1, layer_at + 2)

    def after(rows, kept):
        value = state_2[rows, :] + wide[rows, :] + out_bias[2, at, :]
        state_3[rows, :] = value
        xhat, unused = normal_rows(value)
        put_strips(strips, rows, xhat * gains[0, later, :] + shifts[0, later, :])
        return kept

    over_rows(sz.rows, after)
    spread_out(sz, tensor_at, strips, chunks)


def mlp_back(
    sz, layer_at, grad, state_2, normed_m, up_bias, gains, up, down, low, wide, other, hidden,
    up_grad, grads, grad_out, outs, small,
):
    tensor_at, core, z = places(sz)
    at = slice(layer_at, layer_at + 1)
    width = sz.width
    nothing = jnp.zeros((8, width), F32)

    def lower(rows, kept):
        part = grad[rows, :].astype(BF)
        low[rows, :] = part
        return kept + fold(part.astype(F32))

    small[...] = jnp.zeros_like(small)
    small[2:3, :] = total(over_rows(sz.rows, lower, nothing))
    for piece in range(PIECES):
        lanes = slice(piece * width, (piece + 1) * width)
        name = up_bias_rows(sz, tensor_at, piece)
        wide[...] = dot(normed_m[...], up[:, lanes])
        other[...] = dot_nt(low[...], down[lanes, :])
        shift = up_bias[layer_at, pl.ds(name, 1), :]
        value = wide[...] + shift
        square = value * value
        half = 0.5 + 0.5 * jnp.tanh(value * (TANH_A + TANH_A * TANH_B * square))
        full = value * half
        hidden[:, lanes] = full.astype(BF)
        slope = half + full * (1.0 - half) * (2.0 * TANH_A + 6.0 * TANH_A * TANH_B * square)
        part = (other[...] * slope).astype(BF)
        up_grad[:, lanes] = part
        small[pl.ds(3 + name, 1), :] = total(fold(part.astype(F32)))
        grads[...] = dot_tn(normed_m[...], up_grad[:, lanes]).astype(BF)
        put_grad(sz, grads, outs, piece, 0, core, z)
        grads[...] = dot_tn(low[...], hidden[:, lanes]).astype(BF)
        put_grad(sz, grads, outs, piece, 1, core, z)
    wide[...] = dot_nt(up_grad[...], up[...])

    def back(rows, kept):
        incoming = wide[rows, :]
        xhat, change = norm_back_rows(state_2[rows, :], incoming, gains[2, at, :])
        grad_out[rows, :] = grad[rows, :] + change
        return kept[0] + fold(incoming * xhat), kept[1] + fold(incoming)

    gain_sum, shift_sum = over_rows(sz.rows, back, (nothing, nothing))
    small[0:1, :] = total(gain_sum)
    small[1:2, :] = total(shift_sum)


def last_mlp_kernel(
    sz, layer_at, sample_lens, feature_lens, cotangent, state_2, normed_m, up_bias, gains, out_bias,
    *rest,
):
    parts, halves = unit_parts(sz), 2 if sz.fast else 1
    weights, rest = rest[:parts], rest[parts:]
    output, grad_out, small = rest[:3]
    outs = rest[3 : 3 + halves]
    grad, wide, other, low, hidden, up_grad, grads, up, down, sems = rest[3 + halves :]
    tensor_at, core, z = places(sz)
    copies = load_mlp(sz, layer_at, weights, up, down, sems, core)
    step = 64

    def live_rows(rows, kept):
        index = rows.start + lax.broadcasted_iota(jnp.int32, (step, 1), 0)
        block = index // sz.block_rows
        sample = tensor_at * sz.samples + (index // sz.feats) % sz.samples
        sample_len = jnp.zeros_like(index)
        feature_len = jnp.zeros_like(index)
        for at in range(sz.blocks):
            sample_len = jnp.where(block == at, sample_lens[at], sample_len)
            feature_len = jnp.where(block == at, feature_lens[at], feature_len)
        live = (sample < sample_len) & (index % sz.feats < feature_len)
        grad[rows, :] = jnp.where(live, cotangent[rows, :].astype(F32), 0.0)
        return kept

    over_rows(sz.rows, live_rows, 0, step)
    finish(copies)
    mlp_back(
        sz, layer_at, grad, state_2, normed_m, up_bias, gains, up, down, low, wide, other, hidden,
        up_grad, grads, grad_out, outs, small,
    )
    at = slice(layer_at, layer_at + 1)
    other[...] = dot(hidden[...], down[...])

    def after(rows, kept):
        value = state_2[rows, :] + other[rows, :] + out_bias[2, at, :]
        output[rows, :] = value.astype(BF)
        return kept

    over_rows(sz.rows, after)


def mlp_back_kernel(
    sz, layer_at, grad_in, state_3, state_2, normed_m, up_bias, gains, *rest
):
    n = sz.tensor
    parts, halves = unit_parts(sz), 2 if sz.fast else 1
    chunks, weights, rest = rest[:n], rest[n : n + parts], rest[n + parts :]
    grad_out, small = rest[:2]
    outs = rest[2 : 2 + halves]
    grad, strips, wide, other, low, hidden, up_grad, grads, up, down, sems = rest[2 + halves :]
    tensor_at, core, z = places(sz)
    copies = load_mlp(sz, layer_at, weights, up, down, sems, core)
    sample_norm_back(sz, layer_at + 1, tensor_at, grad_in, state_3, chunks, gains, strips, grad)
    finish(copies)
    mlp_back(
        sz, layer_at, grad, state_2, normed_m, up_bias, gains, up, down, low, wide, other, hidden,
        up_grad, grads, grad_out, outs, small,
    )


def sample_norm_back(sz, layer_at, tensor_at, grad_in, state, chunks, gains, strips, grad):
    bring_back(sz, tensor_at, chunks, strips)
    at = slice(layer_at, layer_at + 1)

    def back(rows, kept):
        incoming = get_strips(strips, rows)
        xhat, change = norm_back_rows(state[rows, :].astype(F32), incoming, gains[0, at, :])
        grad[rows, :] = grad_in[rows, :] + change
        return kept

    over_rows(sz.rows, back)


def last_norm_kernel(sz, grad_in, state, gains, *rest):
    chunks, (grad, strips) = rest[: sz.tensor], rest[sz.tensor :]
    tensor_at, core, z = places(sz)
    sample_norm_back(sz, 0, tensor_at, grad_in, state, chunks, gains, strips, grad)


def feature_back_kernel(sz, layer_at, member, grad, state_1, proj, probs, gains, shifts, *rest):
    n, parts = sz.tensor, unit_parts(sz)
    weights, rest = rest[:parts], rest[parts:]
    grad_out, low, proj_grad, normed, small = rest[:5]
    chunks = rest[5 : 5 + n]
    mixed_grad, strips, wide, w, w_out, sems = rest[5 + n :]
    tensor_at, core, z = places(sz)
    copies = load_unit(sz, layer_at, member, weights, w, w_out, sems, core)
    at = slice(layer_at, layer_at + 1)
    nothing = jnp.zeros((8, sz.width), F32)

    def lower(rows, kept):
        part = grad[rows, :].astype(BF)
        low[rows, :] = part
        return kept + fold(part.astype(F32))

    small[...] = jnp.zeros_like(small)
    small[2:3, :] = total(over_rows(sz.rows, lower, nothing))
    flush(low)
    finish(copies)
    mixed_grad[...] = dot_nt(low[...], w_out[...]).astype(BF)
    jobs = [(slice(tile * TILE, (tile + 1) * TILE), tile) for tile in range(sz.rows // TILE)]
    for piece in range(PIECES):
        attend_back(proj, piece, jobs, probs, mixed_grad, proj_grad)
    wide[...] = dot_nt(proj_grad[...], w[...])

    def back(rows, kept):
        incoming = wide[rows, :]
        gain = gains[1, at, :]
        xhat, change = norm_back_rows(state_1[rows, :], incoming, gain)
        value = grad[rows, :] + change
        grad_out[rows, :] = value
        put_strips(strips, rows, value)
        normed[rows, :] = (xhat * gain + shifts[1, at, :]).astype(BF)
        rounded = value.astype(BF).astype(F32)
        return (
            kept[0] + fold(incoming * xhat),
            kept[1] + fold(incoming),
            kept[2] + fold(rounded),
        )

    sums = over_rows(sz.rows, back, (nothing, nothing, nothing))
    small[0:1, :] = total(sums[0])
    small[1:2, :] = total(sums[1])
    small[3:4, :] = total(sums[2])
    spread_out(sz, tensor_at, strips, chunks)


def sample_back_kernel(sz, layer_at, member, extra, proj, probs, gains, shifts, *rest):
    n, parts = sz.tensor, unit_parts(sz)
    others, rest = rest[:extra], rest[extra:]
    chunks, rows_in, rest = rest[:n], rest[n : 2 * n], rest[2 * n :]
    weights, rest = rest[:parts], rest[parts:]
    back, low, proj_grad, small = rest[:n], rest[n], rest[n + 1], rest[n + 2]
    mixed_grad, normed, w, w_out, sems = rest[n + 3 :]
    tensor_at, core, z = places(sz)
    copies = load_unit(sz, layer_at, member, weights, w, w_out, sems, core)
    by_feature(sz, chunks, low)
    by_feature(sz, rows_in, normed)
    flush(low)
    finish(copies)
    mixed_grad[...] = dot_nt(low[...], w_out[...]).astype(BF)
    jobs = [
        (slice(slot * sz.group, (slot + 1) * sz.group), slot) for slot in range(sz.own_feats)
    ]
    for piece in range(PIECES):
        attend_back(proj, piece, jobs, probs, mixed_grad, proj_grad)
    normed_grad = dot_nt(proj_grad[...], w[...])
    to_chunks(sz, normed_grad, back)
    at = slice(layer_at, layer_at + 1)
    shift_sum = total(fold(normed_grad))
    gain_sum = total(fold(normed_grad * normed[...].astype(F32)))
    small[...] = jnp.zeros_like(small)
    first = 16 if extra else 0
    small[first : first + 1, :] = (gain_sum - shifts[0, at, :] * shift_sum) / gains[0, at, :]
    small[first + 1 : first + 2, :] = shift_sum
    for at, other in enumerate(others):
        place = at if at < 2 else at + 1
        small[8 * place : 8 * place + 8, :] = other[...]


def matrix_grad_kernel(sz, count, direct, proj_grad, low, mixed, *rest):
    halves = 2 if sz.fast else 1
    rows, outs, rest = rest[:count], rest[count : count + halves], rest[count + halves :]
    tensor_at, core, z = places(sz)
    if count == 1:
        (grads,) = rest
        (normed,) = rows
    else:
        grads, normed = rest
        by_feature(sz, rows, normed)
    qkv_grads = dot_tn(normed[...], proj_grad[...])
    out_grads = dot_tn(low[...], mixed[...])
    for piece in range(PIECES):
        lanes = slice(piece * QKV, (piece + 1) * QKV)
        grads[piece, :, :QKV] = qkv_grads[:, lanes].astype(BF)
        lanes = slice(piece * PAIR, (piece + 1) * PAIR)
        grads[piece, :, QKV:] = out_grads[:, lanes].astype(BF)
        put_grad(sz, grads.at[piece], outs, piece, 0, core, z, direct)


def shaped(shape, dtype):
    return jax.ShapeDtypeStruct(shape, dtype)


class Early:
    def __init__(self, target, held, sems):
        self.target, self.held, self.sems, self.copies = target, held, sems, []
        self.shape, self.dtype = held.shape, held.dtype

    def __getitem__(self, index):
        return self.held[index]

    def __setitem__(self, index, value):
        self.held[index] = value

    def flush(self, *index):
        source, target = self.held, self.target
        if index:
            source, target = source.at[index], target.at[index]
        copy = pltpu.make_async_copy(source, target, self.sems.at[len(self.copies)])
        copy.start()
        self.copies.append(copy)


def flush(ref, *index):
    if isinstance(ref, Early):
        ref.flush(*index)


class Job:
    def __init__(self, groups, outs, split, then):
        self.groups, self.outs, self.split, self.then = groups, outs, split, then
        self.terms = [term for group in groups for term in group]

    def scratch(self):
        shapes = [
            (count, array.shape[1], members, *array.shape[3:])
            for array, first, count, member, members in self.terms
        ]
        return [
            pltpu.VMEM(shape, term[0].dtype) for shape, term in zip(shapes, self.terms)
        ] + [pltpu.SemaphoreType.DMA((len(self.terms),))]

    def start(self, refs, scratch):
        pairs = []
        for ref, term, target in zip(refs, self.terms, scratch):
            array, first, count, member, members = term
            pairs.append((ref.at[pl.ds(first, count), :, pl.ds(member, members)], target))
        return begin(pairs, scratch[-1])

    def finish(self, copies, outs, scratch):
        finish(copies)
        at = place = 0
        for group in self.groups:
            refs = scratch[at : at + len(group)]
            at += len(group)
            lead, near, members = refs[0].shape[:3]
            for one in range(lead):
                for two in range(near):
                    for member in range(members):
                        value = refs[0][one, two, member].astype(F32)
                        for ref in refs[1:]:
                            value = value + ref[one, two, member].astype(F32)
                        out, index, lead_at = outs[0], two, one
                        if self.split == 1:
                            out, lead_at = outs[one], 0
                        elif self.split and two >= near // 2:
                            out, index = outs[1], two - near // 2
                        out[lead_at, index, place + member] = value.astype(out.dtype)
            place += members


def launch(
    kernel, name, operands, specs, outs, scratch, micros, after=(), jobs=(), early=None, through=(),
    defer=False,
):
    after, outs = list(after), list(outs)
    sums = [term[0] for job in jobs for term in job.terms]
    job_outs = [out for job in jobs for out in job.outs]
    job_scratch = [job.scratch() for job in jobs]
    count, plain = len(operands), len(scratch)
    before = count + len(sums) + len(after)
    skip = before + len(through)
    early = early or {}
    held = []
    for at, parts in early.items():
        held += [pltpu.VMEM(outs[at].shape, outs[at].dtype), pltpu.SemaphoreType.DMA((parts,))]

    def whole(*refs):
        given, results = refs[count : count + len(sums)], refs[skip : skip + len(outs)]
        extra = refs[skip + len(outs) : skip + len(outs) + len(job_outs)]
        rest = refs[skip + len(outs) + len(job_outs) + len(through) :]
        own, rest = rest[:plain], rest[plain:]
        results = list(results)
        for at in early:
            results[at] = Early(results[at], *rest[:2])
            rest = rest[2:]
        started = []
        for job, buffers in zip(jobs, job_scratch):
            mine, rest = rest[: len(buffers)], rest[len(buffers) :]
            started.append((job, mine, job.start(given[: len(job.terms)], mine)))
            given = given[len(job.terms) :]
        kernel(*refs[:count], *results, *own)
        for job, mine, copies in started:
            job.finish(copies, extra[: len(job.outs)], mine)
            extra = extra[len(job.outs) :]
        for at in early:
            finish(results[at].copies)

    results = pl.pallas_call(
        whole,
        out_shape=outs + job_outs + [shaped(v.shape, v.dtype) for v in through],
        input_output_aliases={
            before + at: len(outs) + len(job_outs) + at for at in range(len(through))
        },
        in_specs=list(specs) + [ANY] * (len(sums) + len(after) + len(through)),
        out_specs=[ANY if at in early else VMEM for at in range(len(outs))]
        + [VMEM] * len(job_outs)
        + [ANY] * len(through),
        scratch_shapes=list(scratch) + held + [buffer for buffers in job_scratch for buffer in buffers],
        name=name,
        cost_estimate=pl.CostEstimate(
            flops=int(micros * 8e9), bytes_accessed=1_000_000, transcendentals=0
        ),
        compiler_params=pltpu.CompilerParams(vmem_limit_bytes=VMEM_GRANT),
    )(*operands, *sums, *after, *through)
    results, extra = results[: len(outs)], results[len(outs) :]
    through = extra[len(job_outs) :]
    if defer:
        return list(results), list(extra[: len(job_outs)])
    for job in jobs:
        job.then(*extra[: len(job.outs)])
        extra = extra[len(job.outs) :]
    return list(results) + list(through)


def grad_shapes(sz, members):
    if sz.fast:
        return [shaped((PIECES, 4, members, 64, sz.width), BF)] * 2
    return [shaped((PIECES, members, sz.width, sz.width), BF)]


def swap_cores(sz, v):
    return lax.ppermute(v, "dp", [(at, at ^ 1) for at in range(sz.dp)])


def swap_near(sz, v, distance):
    return lax.ppermute(v, "tensor", [(at, at ^ distance) for at in range(sz.tensor)])


def swap_far(sz, v, distance):
    return lax.ppermute(v, "dp", [(at, at ^ (2 * distance)) for at in range(sz.dp)])


def swap_turn(sz, v, turn):
    pairs = []
    for dp_at in range(sz.dp):
        distance = 1 + ((dp_at + turn) % 2)
        for at in range(sz.tensor):
            base = dp_at * sz.tensor
            pairs.append((base + at, base + (at ^ distance)))
    return lax.ppermute(v, ("dp", "tensor"), pairs)


def exchange(sz, chunks):
    return [chunks[0]] + [swap_near(sz, chunks[at], at) for at in range(1, sz.tensor)]


def gather_unit(sz, half):
    first = swap_turn(sz, half, 0)
    second = swap_turn(sz, half, 1)
    third = swap_turn(sz, first, 1)
    got = [first, second, third]
    return got + [swap_cores(sz, v) for v in got]


class Reduction:
    def __init__(self, sz, *units):
        self.sz = sz
        self.units = [(mine, swap_cores(sz, theirs), mine.shape[2]) for mine, theirs in units]
        self.members = sum(unit[2] for unit in self.units)
        self.tail = units[0][0].shape[3:]

    def groups(self, first, count, extra):
        groups, place = [], 0
        for mine, other, members in self.units:
            group = [(mine, first, count, 0, members), (other, first, count, 0, members)]
            group += [(array, at, count, place, members) for array, at in extra]
            groups.append(group)
            place += members
        return groups

    def shape(self, lead, near, dtype=BF):
        return shaped((lead, near, self.members, *self.tail), dtype)

    def job(self, step):
        return getattr(self, f"step_{step}")()

    def step_1(self):
        def then(out):
            self.sent, self.far = out, swap_turn(self.sz, out, 1)

        return Job(self.groups(2, 2, []), [self.shape(2, 4)], 0, then)

    def step_2(self):
        def then(out):
            self.sent, self.near = out, swap_turn(self.sz, out, 0)

        return Job(self.groups(1, 1, [(self.far, 1)]), [self.shape(1, 4)], 0, then)

    def step_3(self):
        def then(kept, out):
            self.kept, self.got = kept, swap_far(self.sz, out, 1)

        groups = self.groups(0, 1, [(self.far, 0), (self.near, 0)])
        return Job(groups, [self.shape(1, 2)] * 2, 2, then)

    def step_4(self):
        def then(kept, out):
            self.kept, self.got = kept, swap_far(self.sz, out, 2)

        groups = [[(array, 0, 1, 0, self.members) for array in (self.kept, self.got)]]
        return Job(groups, [self.shape(1, 1, F32), self.shape(1, 1)], 2, then)

    def result(self):
        return (self.kept + self.got.astype(F32)).reshape(self.members, *self.tail)


class Direct:
    def __init__(self, sz, mine, theirs):
        self.sz, self.mine, self.theirs = sz, mine, theirs

    def job(self, step):
        def then(*sent):
            self.sent = sent

        group = [(array, 1, 3, 0, 1) for array in (self.mine, self.other)]
        shape = shaped((1, *self.mine.shape[1:]), BF)
        return Job([group], [shape] * 3, 1, then)


def join(sz, *parts):
    one = object.__new__(Reduction)
    one.sz, one.tail = sz, (64, sz.width)
    plain = [not isinstance(part, Reduction) for part in parts]
    one.members = sum(p.shape[2] if alone else p.members for p, alone in zip(parts, plain))

    def step_3():
        def then(kept, out):
            one.kept, one.sent = kept, out

        groups = []
        for part, alone in zip(parts, plain):
            if alone:
                groups.append([(part, 0, 1, 0, part.shape[2])])
            else:
                groups += part.groups(0, 1, [(part.far, 0), (part.near, 0)])
        return Job(groups, [one.shape(1, 2)] * 2, 2, then)

    one.step_3 = step_3
    return one


def region(flag, fn, *args):
    def nothing(*unused):
        return jax.tree.map(lambda v: jnp.zeros(v.shape, v.dtype), jax.eval_shape(fn, *args))

    return lax.cond(flag, fn, nothing, *args)


def reduce_whole(sz, full):
    members, width = full.shape[1], full.shape[2]
    full = full.transpose(1, 2, 0, 3)
    part = lax.psum_scatter(full, "dp", scatter_dimension=1, tiled=True)
    return lax.psum(part, "tensor").astype(F32)


def gathered_unit(qkv, out):
    qkv = lax.all_gather(qkv, "tensor", axis=2, tiled=True)
    out = lax.all_gather(out, "tensor", axis=0, tiled=True)
    width = qkv.shape[1]
    qkv = qkv.reshape(3, width, PIECES, PAIR).transpose(1, 2, 0, 3)
    return [qkv.reshape(width, PIECES * QKV), out]


def body(
    tokens,
    cotangent,
    block_task,
    sample_len,
    feature_len,
    norm_gain,
    norm_shift,
    sample_qkv,
    sample_out,
    feature_qkv,
    feature_out,
    out_bias,
    up_weight,
    up_bias,
    down_weight,
):
    shape = tokens.shape
    sz = Sizes(shape, lax.axis_size("tensor"), lax.axis_size("dp"))
    rows, width, n = sz.rows, sz.width, sz.tensor
    tokens = tokens.reshape(rows, width)
    cotangent = cotangent.reshape(rows, width)
    gains, shifts, biases = (
        jnp.transpose(v, (1, 0, 2)) for v in (norm_gain, norm_shift, out_bias)
    )
    up_rows = up_bias.reshape(L, PIECES, -1)
    qkvs = [jnp.transpose(v, (0, 2, 1, 3)) for v in (sample_qkv, feature_qkv)]
    outs = [sample_out, feature_out]
    part = functools.partial
    wide = pltpu.VMEM((rows, width), F32)
    strips = pltpu.VMEM((width // TILE, rows + sz.feats, TILE), F32)
    slim = pltpu.VMEM((rows, width), BF)
    dma = pltpu.SemaphoreType.DMA
    row_f32 = shaped((rows, width), F32)
    row_bf = shaped((rows, width), BF)
    chunk_shapes = [shaped((sz.chunk, width), BF)] * n
    proj_shape = shaped((rows, PIECES * QKV), BF)
    small_shape = shaped((8, width), F32)
    half_unit = (width // 2, width)
    sends = [shaped(half_unit, BF)] if sz.fast else []

    *chunks, sent = launch(
        part(start_kernel, sz), "start", (tokens, gains, shifts, qkvs[0], outs[0]),
        [VMEM] * 3 + [ANY] * 2, chunk_shapes + sends, [strips] + [dma((5,))] * len(sends), 3,
    ) if sz.fast else [*launch(
        part(start_kernel, sz), "start", (tokens, gains, shifts, qkvs[0], outs[0]),
        [VMEM] * 3 + [ANY] * 2, chunk_shapes, [strips], 3,
    ), None]

    units = [[None, None] for _ in range(L)]
    members = [[None, None]] + [[0, 1]] * (L - 1)
    mlps = [None] * L
    if sz.fast:

        def pack_mlp(layer_at, after):
            return launch(
                part(pack_mlp_kernel, sz, layer_at), f"pack_mlp_{layer_at}",
                [up_weight, down_weight], [ANY] * 2, [shaped((2, *half_unit), BF)], [dma((2,))],
                2, after,
            )[0]

        got = gather_unit(sz, sent)
        units[0][0] = [qkvs[0], outs[0]] + got
    else:
        for layer_at in range(L):
            for kind in range(2):
                units[layer_at][kind] = gathered_unit(qkvs[kind][layer_at], outs[kind][layer_at])
            up = lax.all_gather(up_weight[layer_at], "tensor", axis=1, tiled=True)
            down = lax.all_gather(down_weight[layer_at], "tensor", axis=0, tiled=True)
            mlps[layer_at] = [up, down]

    def gather_units(layer_at, kinds, sent):
        got = gather_unit(sz, sent)
        for kind in kinds:
            units[layer_at][kind] = [qkvs[kind], outs[kind]] + got

    def gather_mlp(layer_at, sent):
        mlps[layer_at] = [up_weight, down_weight] + gather_unit(sz, sent)

    def arrived(parts, count):
        return parts[2 : 2 + count] if sz.fast else []

    unit_specs = [ANY] * unit_parts(sz)
    mlp_specs = [ANY] * unit_parts(sz)
    unit_scratch = [
        pltpu.VMEM((width, PIECES * QKV), BF),
        pltpu.VMEM((width, width), BF),
        dma((22 if sz.fast else 2,)),
    ]
    mlp_scratch = [
        pltpu.VMEM((width, PIECES * width), BF),
        pltpu.VMEM((PIECES * width, width), BF),
        dma((14 if sz.fast else 2,)),
    ]
    hidden = pltpu.VMEM((rows, PIECES * width), BF)
    square = pltpu.VMEM((width, width), BF)

    state = tokens
    kept = []
    for layer_at in range(L):
        entry = state
        got = exchange(sz, chunks)
        slots = sz.own_feats
        began = []
        if sz.fast and layer_at == 0:
            half_mlp, half_units = shaped((2, *half_unit), BF), shaped((2, *half_unit), BF)
            sent, sent_mlp, *waiting = launch(
                part(pack_early_kernel, sz), "pack_early",
                (qkvs[0], outs[0], qkvs[1], outs[1], up_weight, down_weight), [ANY] * 6,
                [shaped(half_unit, BF), half_mlp, half_units], [dma((17,))], 2,
                got[1:] + arrived(units[0][0], 2),
            )
            gather_units(0, (1,), sent)
            gather_mlp(0, sent_mlp)
            began = [sent, sent_mlp]
        elif sz.fast:
            sent = pack_mlp(layer_at, got[1:] + arrived(units[layer_at][0], 2))
            gather_mlp(layer_at, sent)
            began = [sent]
        *back, proj_s, mixed_s, probs_s = launch(
            part(sample_kernel, sz, layer_at, members[layer_at][0]), f"sample_{layer_at}",
            (block_task, sample_len, *got, *units[layer_at][0]),
            [SMEM] * 2 + [VMEM] * n + unit_specs,
            chunk_shapes
            + [proj_shape, row_bf, shaped((PIECES, slots, 2, sz.group, sz.group), BF)],
            [slim, pltpu.VMEM((sz.group, sz.group), F32), *unit_scratch],
            8, began, early={n: 1, n + 1: PIECES, n + 2: PIECES},
        )
        back = exchange(sz, back)
        tiles = rows // TILE
        passed = waiting if sz.fast and layer_at < L - 1 else []
        state_1, state_2, normed_m, proj_f, mixed_f, probs_f, *passed = launch(
            part(feature_kernel, sz, layer_at, members[layer_at][1]), f"feature_{layer_at}",
            (feature_len, state, gains, shifts, biases, *back, *units[layer_at][1]),
            [SMEM] + [VMEM] * (4 + n) + unit_specs,
            [row_f32, row_f32, row_bf, proj_shape, row_bf,
             shaped((PIECES, tiles, 2, TILE, TILE), BF)],
            [strips, wide, slim, *unit_scratch],
            9, through=passed,
        )
        if layer_at < L - 1:
            if sz.fast:
                gather_units(layer_at + 1, (0, 1), passed[0])
            state, *chunks = launch(
                part(mlp_kernel, sz, layer_at), f"mlp_{layer_at}",
                (state_2, normed_m, up_rows, gains, shifts, biases, *mlps[layer_at]),
                [VMEM] * 6 + mlp_specs,
                [row_f32] + chunk_shapes,
                [strips, wide, hidden, *mlp_scratch],
                9,
            )
        kept.append((entry, got, proj_s, mixed_s, probs_s, state_1, state_2, normed_m,
                     proj_f, mixed_f, probs_f))

    reductions, whole, done = {}, {}, {}

    def reduction(layer_at, kind, parts):
        if sz.fast and layer_at == 0 and kind < 2:
            reductions[layer_at, kind] = Direct(sz, *parts)
        elif sz.fast:
            reductions[layer_at, kind] = Reduction(sz, parts)
        else:
            (whole[layer_at, kind],) = parts

    def jobs(*steps):
        return [reductions[at[:2]].job(at[2]) for at in steps if at[:2] in reductions]

    def add_up(name, after, *steps, through=()):
        todo = jobs(*steps)
        if not todo:
            return []
        return launch(
            part(nothing_kernel, sz), name, [], [], [], [], 0.05, after, todo, through=through
        )

    smalls = [None] * L

    def small_rows():
        return jnp.concatenate([one for layer in smalls for one in layer], axis=0)

    for layer_at in reversed(range(L)):
        (entry, got, proj_s, mixed_s, probs_s, state_1, state_2, normed_m,
         proj_f, mixed_f, probs_f) = kept[layer_at]
        above = layer_at + 1
        if layer_at == L - 1:
            output, grad, small_m, *parts = launch(
                part(last_mlp_kernel, sz, layer_at), f"last_mlp_{layer_at}",
                (sample_len, feature_len, cotangent, state_2, normed_m, up_rows, gains, biases,
                 *mlps[layer_at]),
                [SMEM] * 2 + [VMEM] * 6 + mlp_specs,
                [row_bf, row_f32, small_shape] + grad_shapes(sz, 2),
                [wide, wide, wide, slim, hidden, hidden, square, *mlp_scratch],
                15,
            )
        else:
            grad, small_m, *parts = launch(
                part(mlp_back_kernel, sz, layer_at), f"mlp_back_{layer_at}",
                (grad, kept[above][0], state_2, normed_m, up_rows, gains, *back,
                 *mlps[layer_at]),
                [VMEM] * (6 + n) + mlp_specs,
                [row_f32, small_shape] + grad_shapes(sz, 2),
                [wide, strips, wide, wide, slim, hidden, hidden, square, *mlp_scratch],
                15, parts[:1], early={2: 2 * PIECES, 3: 2 * PIECES} if sz.fast else None,
            )
        reduction(layer_at, 2, parts)
        began = []
        if layer_at < L - 1 and sz.fast:
            add_up(f"sums_{layer_at}", [grad], (above, 2, 3), (above, 1, 2), (above, 0, 1))
            began = [reductions[above, 1].sent, reductions[above, 0].sent]
        grad, low, proj_grad, normed, small_f, *chunks = launch(
            part(feature_back_kernel, sz, layer_at, members[layer_at][1]),
            f"feature_back_{layer_at}",
            (grad, state_1, proj_f, probs_f, gains, shifts, *units[layer_at][1]),
            [VMEM] * 6 + unit_specs,
            [row_f32, row_bf, proj_shape, row_bf, small_shape] + chunk_shapes,
            [slim, strips, wide, *unit_scratch],
            9, began,
        )
        smalls[layer_at] = [small_m, small_f]
        chunks = exchange(sz, chunks)
        parts = launch(
            part(matrix_grad_kernel, sz, 1, layer_at == 0), f"feature_matrix_{layer_at}",
            (proj_grad, low, mixed_f, normed), [VMEM] * 4, grad_shapes(sz, 1),
            [pltpu.VMEM((PIECES, width, width), BF)], 0.7,
            jobs=jobs((layer_at, 2, 1), (above, 0, 2), (above, 2, 4)),
        )
        reduction(layer_at, 1, parts)
        others = []
        if layer_at == 0 and sz.fast:
            others = [one for layer in smalls for one in layer]
        *back, low, proj_grad, small_s = launch(
            part(sample_back_kernel, sz, layer_at, members[layer_at][0], len(others)),
            f"sample_back_{layer_at}",
            (proj_s, probs_s, gains, shifts, *others, *chunks, *got, *units[layer_at][0]),
            [VMEM] * (4 + len(others) + 2 * n) + unit_specs,
            chunk_shapes + [row_bf, proj_shape, shaped((24 * L, width), F32) if others else small_shape],
            [slim, slim, *unit_scratch],
            9, parts[:1],
        )
        smalls[layer_at].append(small_s)
        began = []
        if not sz.fast or layer_at > 0:
            back = exchange(sz, back)
        if sz.fast and layer_at == 0:
            reductions[1, 3] = upper = join(sz, reductions[1, 1], reductions[1, 0])
            began = [reductions[1, 2].got, reductions[1, 1].near, reductions[1, 0].near]
            rows_small = small_s
            reductions[0, 1].other = swap_cores(sz, reductions[0, 1].theirs)
        parts = launch(
            part(matrix_grad_kernel, sz, n, layer_at == 0), f"sample_matrix_{layer_at}",
            (proj_grad, low, mixed_s, *got), [VMEM] * (3 + n), grad_shapes(sz, 1),
            [pltpu.VMEM((PIECES, width, width), BF), slim], 0.7, began,
            jobs((layer_at, 1, 1), *(((layer_at, 2, 2),) if layer_at else ((1, 3, 3),))),
        )
        reduction(layer_at, 0, parts)
    def last_norm(back):
        (tokens_grad,) = launch(
            part(last_norm_kernel, sz), "last_norm", (grad, tokens, gains, *back),
            [VMEM] * (3 + n), [row_f32], [strips], 5,
        )
        return tokens_grad

    if sz.fast:
        first, last = reductions[0, 1], reductions[0, 0]
        block = shaped((16 * L, width), F32)
        mlp = reductions[0, 2]

        def near_region(pieces, mine, theirs, rows_own):
            got = [swap_near(sz, v, at + 1) for at, v in enumerate(pieces)]
            other, rows_other = swap_cores(sz, theirs), swap_cores(sz, rows_own)
            results, (mlp_sent,) = launch(
                part(send_near_kernel, sz), "send_near", (mine, other, rows_own, rows_other),
                [VMEM] * 4, [shaped((256 + 16 * L, width), BF)] * 3 + [block], [], 5, [],
                [mlp.job(2)], defer=True,
            )
            return got, other, results, mlp_sent

        upper.got = swap_far(sz, upper.sent, 1)
        first.got, last.other, (*sent, rows_kept), mlp_sent = region(
            sample_len[0] > 0, near_region, first.sent, last.mine, last.theirs, rows_small
        )
        mlp.near = swap_turn(sz, mlp_sent, 0)
        last.got = [swap_near(sz, v, at + 1) for at, v in enumerate(sent)]
        add_up("sums_upper", [rows_kept], (1, 3, 4))
        back = add_up("sums_mlp", [rows_kept, upper.kept], (0, 2, 3), through=back)
        attention_kept, rows_kept, *sent = launch(
            part(send_far_kernel, sz), "send_far",
            (first.mine, first.other, *first.got, last.mine, last.other, *last.got, rows_kept),
            [ANY] * 2 + [VMEM] * 3 + [ANY] * 2 + [VMEM] * 4,
            [shaped((2, 64, width), F32), block] + [shaped((128 + 16 * L, width), BF)] * 3,
            [pltpu.VMEM((4, 1, 64, width), BF)] * 4 + [dma((4,))], 0.05, [mlp.kept, upper.got],
        )
        add_up("sums_late", [rows_kept], (0, 2, 4))
        got = [swap_far(sz, v, at + 1) for at, v in enumerate(sent)]
        tokens_grad = last_norm(exchange(sz, back))
        upper_mlp = reductions[1, 2]
        qkv_shape, out_shape = shaped((L, 3, 64, PAIR), F32), shaped((L, 64, PAIR), F32)
        wide_shape, row_shape = shaped((L, 64, width), F32), shaped((3, L, width), F32)
        (s_qkv, s_out, f_qkv, f_out, up, down, gain_total, shift_total, bias_total,
         up_bias_total) = launch(
            part(last_sums_kernel, sz), "last_sums",
            (attention_kept, rows_kept, *got, mlp.kept, mlp.got, upper_mlp.kept, upper_mlp.got,
             upper.kept, upper.got), [VMEM] * 11,
            [qkv_shape, out_shape, qkv_shape, out_shape, wide_shape, wide_shape,
             row_shape, row_shape, row_shape, shaped((L, PIECES * width), F32)], [], 0.05,
        )

        def turned(v):
            return jnp.transpose(v, (0, 2, 1))

        gain_total, shift_total, bias_total = (
            jnp.transpose(v, (1, 0, 2)) for v in (gain_total, shift_total, bias_total)
        )
        return (
            output.reshape(shape), tokens_grad.reshape(shape), gain_total, shift_total,
            jnp.transpose(s_qkv, (0, 2, 1, 3)), turned(s_out),
            jnp.transpose(f_qkv, (0, 2, 1, 3)), turned(f_out),
            bias_total, up, up_bias_total, turned(down),
        )
    tokens_grad = last_norm(back)
    early = lax.psum(small_rows(), ("dp", "tensor"))
    early = early.reshape(-1, 8, width)
    by_layer = []
    at = 0
    for layer_at in range(L):
        count = len(smalls[layer_at])
        sums = [early[at + member] for member in range(count)]
        at += count
        by_layer.append(sums)
    gain_total, shift_total = (
        jnp.stack([jnp.stack([s[row], f[row], m[row]]) for m, f, s in by_layer])
        for row in range(2)
    )
    bias_total = jnp.stack([jnp.stack([f[3], f[2], m[2]]) for m, f, s in by_layer])
    up_bias_total = jnp.stack([m[3 : 3 + PIECES].reshape(-1) for m, f, s in by_layer])

    if not sz.fast:
        for key, full in whole.items():
            done[key] = reduce_whole(sz, full)

    def attention_grads(kind):
        qkv, out = [], []
        for layer_at in range(L):
            if sz.fast:
                value = done[layer_at, kind][0]
                qkv.append(value[:, :QKV].reshape(-1, 3, PAIR))
                out.append(value[:, QKV:].T)
            else:
                value = done[layer_at, kind][0]
                columns = width // n
                start = lax.axis_index("tensor") * columns
                whole = value[:, :, :QKV].reshape(-1, PIECES, 3, PAIR).transpose(0, 2, 1, 3)
                whole = whole.reshape(-1, 3, width)
                qkv.append(lax.dynamic_slice_in_dim(whole, start, columns, 2))
                whole = value[:, :, QKV:].reshape(-1, width)
                out.append(lax.dynamic_slice_in_dim(whole, start, columns, 1).T)
        return jnp.stack(qkv), jnp.stack(out)

    sample_qkv_grad, sample_out_grad = attention_grads(0)
    feature_qkv_grad, feature_out_grad = attention_grads(1)
    ups, downs = [], []
    for layer_at in range(L):
        value = done[layer_at, 2]
        if not sz.fast:
            columns = PIECES * width // n
            start = lax.axis_index("tensor") * columns
            value = value.reshape(2, -1, PIECES * width)
            value = lax.dynamic_slice_in_dim(value, start, columns, 2)
        ups.append(value[0])
        downs.append(value[1].T)
    return (
        output.reshape(shape),
        tokens_grad.reshape(shape),
        gain_total,
        shift_total,
        sample_qkv_grad,
        sample_out_grad,
        feature_qkv_grad,
        feature_out_grad,
        bias_total,
        jnp.stack(ups),
        up_bias_total,
        jnp.stack(downs),
    )


def solution(mesh):
    placed = (
        P("dp", "tensor", None, None),
        P("dp", "tensor", None, None),
        P("dp"),
        P("dp"),
        P("dp"),
        P(),
        P(),
        P(None, None, None, "tensor"),
        P(None, "tensor", None),
        P(None, None, None, "tensor"),
        P(None, "tensor", None),
        P(),
        P(None, None, "tensor"),
        P(),
        P(None, "tensor", None),
    )
    return jax.shard_map(
        body,
        mesh=mesh,
        in_specs=placed,
        out_specs=(
            P("dp", "tensor", None, None),
            P("dp", "tensor", None, None),
            P(),
            P(),
            P(None, "dp", None, "tensor"),
            P(None, "tensor", "dp"),
            P(None, "dp", None, "tensor"),
            P(None, "tensor", "dp"),
            P(),
            P(None, "dp", "tensor"),
            P(),
            P(None, "tensor", "dp"),
        ),
        check_vma=False,
    )
```

```python
import functools

import jax
import jax.numpy as jnp
from jax import lax
from jax.experimental import pallas as pl
from jax.experimental.pallas import tpu as pltpu
from jax.sharding import PartitionSpec as P

HD = 64
L = 2
PIECES = 4
PAIR = 2 * HD
QKV = 3 * PAIR
TILE = 128

epsilon = 1e-05
masked_score = -1e30
SCALE = HD ** (-0.5)
F32 = jnp.float32
BF = jnp.bfloat16
NT = (((1,), (1,)), ((), ()))
TN = (((0,), (0,)), ((), ()))
TANH_A = 0.7978845608028654
TANH_B = 0.044715
VMEM_GRANT = 66977792
SMALL = ((0, 0, 7), (7, 8, 4), (11, 16, 2))
VMEM = pl.BlockSpec(memory_space=pltpu.VMEM)
SMEM = pl.BlockSpec(memory_space=pltpu.SMEM)
ANY = pl.BlockSpec(memory_space=pl.ANY)


class Sizes:
    def __init__(self, shape, tensor, dp):
        self.blocks, self.samples, self.feats, self.width = shape
        self.tensor, self.dp = tensor, dp
        self.rows = self.blocks * self.samples * self.feats
        self.own_feats = self.feats // tensor
        self.run = self.blocks * self.samples
        self.chunk = self.own_feats * self.run
        self.group = tensor * self.run
        self.block_rows = self.samples * self.feats
        self.fast = tensor == 4 and dp == 8


def places(z):
    tensor_at = lax.axis_index("tensor")
    dp_at = lax.axis_index("dp")
    return tensor_at, lax.rem(dp_at, 2), lax.div(dp_at, 2)


def dot(a, b):
    return jnp.dot(a, b, preferred_element_type=F32)


def dot_nt(a, b):
    return lax.dot_general(a, b, NT, preferred_element_type=F32)


def dot_tn(a, b):
    return lax.dot_general(a, b, TN, preferred_element_type=F32)


def normal_rows(x):
    centre = x - jnp.mean(x, axis=-1, keepdims=True)
    spread = jnp.mean(centre * centre, axis=-1, keepdims=True)
    rate = lax.rsqrt(spread + epsilon)
    return centre * rate, rate


def over_rows(rows, fn, carry=0, step=64):
    for at in range(rows // step):
        carry = fn(slice(at * step, (at + 1) * step), carry)
    return carry


def fold(x):
    return jnp.sum(x.reshape(-1, 8, x.shape[-1]), axis=0)


def total(x):
    return jnp.sum(x, axis=0, keepdims=True)


def put_strips(strips, rows, value):
    for lane in range(value.shape[1] // TILE):
        strips[lane, rows, :] = value[:, lane * TILE : (lane + 1) * TILE]


def get_strips(strips, rows):
    return jnp.concatenate([strips[lane, rows, :] for lane in range(strips.shape[0])], axis=1)


def feature_slot(sz, tensor_at, at, slot):
    return (tensor_at ^ at) * sz.own_feats + slot


def spread_out(sz, tensor_at, wide, chunks):
    for at in range(sz.tensor):
        for slot in range(sz.own_feats):
            first = feature_slot(sz, tensor_at, at, slot)
            for lane in range(sz.width // TILE):
                rows = wide[lane, pl.ds(first, sz.run, stride=sz.feats), :]
                chunks[at][
                    slot * sz.run : (slot + 1) * sz.run, lane * TILE : (lane + 1) * TILE
                ] = rows.astype(BF)


def bring_back(sz, tensor_at, chunks, wide):
    for at in range(sz.tensor):
        for slot in range(sz.own_feats):
            first = feature_slot(sz, tensor_at, at, slot)
            for lane in range(sz.width // TILE):
                rows = chunks[at][
                    slot * sz.run : (slot + 1) * sz.run, lane * TILE : (lane + 1) * TILE
                ]
                wide[lane, pl.ds(first, sz.run, stride=sz.feats), :] = rows.astype(F32)


def by_feature(sz, chunks, x):
    for at in range(sz.tensor):
        for slot in range(sz.own_feats):
            first = slot * sz.group + at * sz.run
            x[first : first + sz.run, :] = chunks[at][slot * sz.run : (slot + 1) * sz.run, :]


def to_chunks(sz, value, chunks):
    for at in range(sz.tensor):
        for slot in range(sz.own_feats):
            first = slot * sz.group + at * sz.run
            chunks[at][slot * sz.run : (slot + 1) * sz.run, :] = value[
                first : first + sz.run
            ].astype(BF)


def where_halves(core):
    other = 1 - core
    return (
        (1 + core, core),
        (2 - core, core),
        (3, core),
        (1 + other, other),
        (2 - other, other),
        (3, other),
    )


def load_unit(sz, layer_at, member, parts, w, w_out, sems, core):
    pairs = []
    if not sz.fast:
        pairs += [(parts[0], w), (parts[1], w_out)]
    else:
        qkv, out = parts[:2]
        for at in range(3):
            pairs.append((qkv.at[layer_at, at], w.at[:, pl.ds(at * PAIR, PAIR)]))
        pairs.append((out.at[layer_at], w_out.at[pl.ds(0, PAIR), :]))
        half_rows = sz.width // 2
        for source, (piece, half) in zip(parts[2:], where_halves(core)):
            if member is not None:
                source = source.at[member]
            start = pl.multiple_of(half * half_rows, half_rows)
            first = pl.multiple_of(piece * QKV, TILE)
            pairs.append(
                (source.at[:, pl.ds(0, QKV)], w.at[pl.ds(start, half_rows), pl.ds(first, QKV)])
            )
            first = pl.multiple_of(piece * PAIR, TILE)
            for block in range(half_rows // TILE):
                lanes = pl.ds(pl.multiple_of(start + block * TILE, TILE), TILE)
                pairs.append(
                    (
                        source.at[pl.ds(block * TILE, TILE), pl.ds(QKV, PAIR)],
                        w_out.at[pl.ds(first, PAIR), lanes],
                    )
                )
    return begin(pairs, sems)


def begin(pairs, sems):
    copies = []
    for source, target in pairs:
        copies.append(pltpu.make_async_copy(source, target, sems.at[len(copies)]))
        copies[-1].start()
    return copies


def finish(copies):
    for copy in copies:
        copy.wait()


def load_mlp(sz, layer_at, parts, up, down, sems, core):
    pairs = []
    if not sz.fast:
        pairs += [(parts[0], up), (parts[1], down)]
    else:
        width = sz.width
        pairs.append((parts[0].at[layer_at], up.at[:, pl.ds(0, width)]))
        pairs.append((parts[1].at[layer_at], down.at[pl.ds(0, width), :]))
        half_rows = width // 2
        for source, (piece, half) in zip(parts[2:], where_halves(core)):
            start = pl.multiple_of(half * half_rows, half_rows)
            first = pl.multiple_of(piece * width, width)
            pairs.append(
                (source.at[0], up.at[pl.ds(start, half_rows), pl.ds(first, width)])
            )
            rows = pl.ds(pl.multiple_of(first + start, half_rows), half_rows)
            pairs.append((source.at[1], down.at[rows, :]))
    return begin(pairs, sems)


def put_grad(sz, grads, outs, piece, member, core, z, direct=False):
    if not sz.fast:
        outs[0][piece, member] = grads[...]
        return
    mine, theirs = outs
    if direct or piece in (0, 3):
        at_mine = at_theirs = piece
    elif piece == 1:
        at_mine, at_theirs = 1 + core, 2 - core
    else:
        at_mine, at_theirs = 2 - core, 1 + core
    for place, near in enumerate((0, 1, 2, 3) if direct else (0, 2, 1, 3)):
        first = (z ^ near) * 128
        rows_mine = pl.ds(pl.multiple_of(first + core * 64, 64), 64)
        rows_theirs = pl.ds(pl.multiple_of(first + (1 - core) * 64, 64), 64)
        mine[at_mine, place, member] = grads[rows_mine, :]
        theirs[at_theirs, place, member] = grads[rows_theirs, :]
    flush(mine, at_mine, slice(None), member)
    flush(theirs, at_theirs, slice(None), member)


def head_masks():
    lane = lax.broadcasted_iota(jnp.int32, (1, PAIR), 1)
    return lane < HD, lane >= HD


def sample_bias(sz, tensor_at, tasks, lengths, bias):
    def of(index):
        run_at = index // sz.run
        block = (index // sz.samples) % sz.blocks
        sample = (run_at ^ tensor_at) * sz.samples + index % sz.samples
        task = jnp.zeros_like(index)
        length = jnp.zeros_like(index)
        for at in range(sz.blocks):
            task = jnp.where(block == at, tasks[at], task)
            length = jnp.where(block == at, lengths[at], length)
        return task, sample < length

    row_task, unused = of(lax.broadcasted_iota(jnp.int32, (sz.group, 1), 0))
    key_task, key_live = of(lax.broadcasted_iota(jnp.int32, (1, sz.group), 1))
    key_task = jnp.where(key_live, key_task, -1)
    bias[...] = jnp.where(row_task == key_task, 0.0, masked_score)


def feature_bias(sz, length):
    row = lax.broadcasted_iota(jnp.int32, (TILE, TILE), 0)
    key = lax.broadcasted_iota(jnp.int32, (TILE, TILE), 1)
    same = (row // sz.feats) == (key // sz.feats)
    return jnp.where(same & (key % sz.feats < length), 0.0, masked_score)


def attend(proj, piece, jobs, probs, mixed):
    masks = head_masks()
    first = piece * QKV
    scores = []
    for rows, bias, place in jobs:
        query = proj[rows, first : first + PAIR]
        key = proj[rows, first + PAIR : first + 2 * PAIR]
        for mask in masks:
            scores.append(dot_nt(jnp.where(mask, query, 0) * SCALE, key) + bias)
    tops = [jnp.max(part, axis=-1, keepdims=True) for part in scores]
    weights = [jnp.exp(part - top) for part, top in zip(scores, tops)]
    shares = [1.0 / jnp.sum(part, axis=-1, keepdims=True) for part in weights]
    weights = [(part * share).astype(BF) for part, share in zip(weights, shares)]
    for at, (rows, bias, place) in enumerate(jobs):
        value = proj[rows, first + 2 * PAIR : first + QKV]
        pair = weights[2 * at : 2 * at + 2]
        for head in range(2):
            probs[piece, place, head] = pair[head]
        mixed[rows, piece * PAIR : (piece + 1) * PAIR] = jnp.where(
            masks[0], dot(pair[0], value), dot(pair[1], value)
        ).astype(BF)
    flush(probs, piece)
    flush(mixed, slice(None), pl.ds(piece * PAIR, PAIR))


def attend_back(proj, piece, jobs, probs, mixed_grad, proj_grad):
    masks = head_masks()
    first = piece * QKV
    head_grads, weights, weight_grads = [], [], []
    for rows, place in jobs:
        grad = mixed_grad[rows, piece * PAIR : (piece + 1) * PAIR]
        value = proj[rows, first + 2 * PAIR : first + QKV]
        for head, mask in enumerate(masks):
            head_grads.append(jnp.where(mask, grad, 0))
            weights.append(probs[piece, place, head])
            weight_grads.append(dot_nt(head_grads[-1], value))
    score_grads = []
    for low, grad in zip(weights, weight_grads):
        wide = low.astype(F32)
        product = wide * grad
        score_grads.append((product - wide * jnp.sum(product, axis=-1, keepdims=True)).astype(BF))
    for at, (rows, place) in enumerate(jobs):
        query = proj[rows, first : first + PAIR]
        key = proj[rows, first + PAIR : first + 2 * PAIR]
        one, two = score_grads[2 * at : 2 * at + 2]
        queries = jnp.where(masks[0], dot(one, key), dot(two, key)) * SCALE
        keys = dot_tn(one, jnp.where(masks[0], query, 0))
        keys = (keys + dot_tn(two, jnp.where(masks[1], query, 0))) * SCALE
        values = dot_tn(weights[2 * at], head_grads[2 * at])
        values = values + dot_tn(weights[2 * at + 1], head_grads[2 * at + 1])
        proj_grad[rows, first : first + PAIR] = queries.astype(BF)
        proj_grad[rows, first + PAIR : first + 2 * PAIR] = keys.astype(BF)
        proj_grad[rows, first + 2 * PAIR : first + QKV] = values.astype(BF)
    flush(proj_grad, slice(None), pl.ds(first, QKV))


def norm_back_rows(state, incoming, gain):
    xhat, rate = normal_rows(state)
    inner = incoming * gain
    back = rate * (
        inner
        - jnp.mean(inner, axis=-1, keepdims=True)
        - xhat * jnp.mean(inner * xhat, axis=-1, keepdims=True)
    )
    return xhat, back


def pack_copies(sz, layer_at, qkv, out, sent, core):
    half = sz.width // 2
    rows = pl.ds(pl.multiple_of(core * half, half), half)
    pairs = []
    for at in range(3):
        pairs.append((qkv.at[layer_at, at, rows, :], sent.at[:, pl.ds(at * PAIR, PAIR)]))
    for block in range(half // TILE):
        lanes = pl.ds(pl.multiple_of(core * half + block * TILE, TILE), TILE)
        pairs.append(
            (out.at[layer_at, :, lanes], sent.at[pl.ds(block * TILE, TILE), pl.ds(QKV, PAIR)])
        )
    return pairs


def start_kernel(sz, tokens, gains, shifts, *rest):
    chunks, (strips,) = rest[: sz.tensor], rest[sz.tensor :]
    tensor_at, core, z = places(sz)

    def rows_of(rows, kept):
        xhat, unused = normal_rows(tokens[rows, :].astype(F32))
        put_strips(strips, rows, xhat * gains[0, 0:1, :] + shifts[0, 0:1, :])
        return kept

    over_rows(sz.rows, rows_of)
    spread_out(sz, tensor_at, strips, chunks)


def pack_first_kernel(sz, qkv, out, sent, sems):
    tensor_at, core, z = places(sz)
    finish(begin(pack_copies(sz, 0, qkv, out, sent, core), sems))


def pack_mlp_kernel(sz, layer_at, up, down, sent, sems):
    tensor_at, core, z = places(sz)
    finish(begin(mlp_pairs(sz, layer_at, up, down, sent, core), sems))


def mlp_pairs(sz, layer_at, up, down, sent, core):
    half = sz.width // 2
    rows = pl.ds(pl.multiple_of(core * half, half), half)
    return [(w.at[layer_at, rows, :], sent.at[at]) for at, w in enumerate((up, down))]


def pack_early_kernel(sz, sample_qkv, sample_out, feature_qkv, feature_out, up, down, *rest):
    first, mlp, units, sems = rest
    tensor_at, core, z = places(sz)
    pairs = pack_copies(sz, 0, feature_qkv, feature_out, first, core)
    pairs += mlp_pairs(sz, 0, up, down, mlp, core)
    pairs += pack_copies(sz, 1, sample_qkv, sample_out, units.at[0], core)
    pairs += pack_copies(sz, 1, feature_qkv, feature_out, units.at[1], core)
    finish(begin(pairs, sems))


def nothing_kernel(sz, *rest):
    pass


def send_near_kernel(sz, mine, other, rows, rows_other, *outs):
    kept = outs[-1]
    kept[...] = jnp.zeros_like(kept)
    for layer_at in range(L):
        for at, first, count in SMALL:
            here = slice(24 * layer_at + first, 24 * layer_at + first + count)
            there = slice(16 * layer_at + at, 16 * layer_at + at + count)
            kept[there, :] = rows[here, :] + rows_other[here, :]
    small = kept[...].astype(BF)
    kept[...] = small.astype(F32)
    for piece in range(1, PIECES):
        out = outs[piece - 1]
        for near in range(4):
            value = mine[piece, near, 0].astype(F32) + other[piece, near, 0].astype(F32)
            out[near * 64 : near * 64 + 64, :] = value.astype(BF)
        out[256:, :] = small


def pairwise(one, two, three, four):
    return (one + two) + (three + four)


def send_far_kernel(sz, *refs):
    first, last, small, outs = refs[:5], refs[5:10], refs[10], refs[11:16]
    kept, rows, sends = outs[0], outs[1], outs[2:]
    *held, sems = refs[16:]
    sources = (first[0], first[1], last[0], last[1])
    copies = begin([(ref.at[0], target) for ref, target in zip(sources, held)], sems)
    first, last = (*held[:2], *first[2:]), (*held[2:], *last[2:])
    finish(copies)

    def value(unit, at, near):
        mine, other, *got = unit
        out = mine[near, 0].astype(F32) + other[near, 0].astype(F32)
        for one in got:
            got_here = one[0, near, 0] if at == 0 else one[near * 64 : near * 64 + 64, :]
            out = out + got_here.astype(F32)
        return out

    x, y, d = (one[256:, :].astype(F32) for one in last[2:])
    low = pairwise(small[...], x, y, d).astype(BF)
    rows[...] = low.astype(F32)
    for at, unit in enumerate((first, last)):
        kept[at] = value(unit, at, 0)
        for near in range(1, 4):
            sends[near - 1][at * 64 : at * 64 + 64, :] = value(unit, at, near).astype(BF)
    for near in range(1, 4):
        sends[near - 1][128:, :] = low


def last_sums_kernel(sz, *refs):
    kept, rows, one, two, three, mlp, mlp_got, upper_mlp, upper_mlp_got = refs[:9]
    upper, upper_got = refs[9:11]
    s_qkv, s_out, f_qkv, f_out, up, down, gain, shift, bias, up_bias = refs[11:]
    small = pairwise(rows[...], *(got[128:, :].astype(F32) for got in (one, two, three)))

    def attention(layer_at, value, qkv, out):
        for at in range(3):
            qkv[layer_at, at] = value[:, at * PAIR : (at + 1) * PAIR]
        out[layer_at] = value[:, QKV:]

    for at, (qkv, out) in enumerate(((f_qkv, f_out), (s_qkv, s_out))):
        value = kept[at]
        for got in (one, two, three):
            value = value + got[at * 64 : at * 64 + 64, :].astype(F32)
        attention(0, value, qkv, out)
        attention(1, upper[0, 0, at] + upper_got[0, 0, at].astype(F32), qkv, out)
    for at, w in enumerate((up, down)):
        w[0] = mlp[0, 0, at] + mlp_got[0, 0, at].astype(F32)
        w[1] = upper_mlp[0, 0, at] + upper_mlp_got[0, 0, at].astype(F32)
    for layer_at in range(L):
        m, f, s = (16 * layer_at + at for at, first, count in SMALL)
        for out, places_in in ((gain, (s, f, m)), (shift, (s + 1, f + 1, m + 1)),
                               (bias, (f + 3, f + 2, m + 2))):
            for at, row in enumerate(places_in):
                out[at, layer_at : layer_at + 1, :] = small[row : row + 1]
        for piece in range(PIECES):
            lanes = slice(piece * sz.width, (piece + 1) * sz.width)
            row = m + 3 + piece
            up_bias[layer_at : layer_at + 1, lanes] = small[row : row + 1]


def unit_parts(sz):
    return 8 if sz.fast else 2


def sample_kernel(sz, layer_at, member, tasks, lengths, *rest):
    n, parts = sz.tensor, unit_parts(sz)
    chunks, weights = rest[:n], rest[n : n + parts]
    outs = rest[n + parts :]
    back, proj, mixed, probs = outs[:n], outs[n], outs[n + 1], outs[n + 2]
    x, bias, w, w_out, sems = outs[n + 3 :]
    tensor_at, core, z = places(sz)
    copies = load_unit(sz, layer_at, member, weights, w, w_out, sems, core)
    by_feature(sz, chunks, x)
    sample_bias(sz, tensor_at, tasks, lengths, bias)
    finish(copies)
    proj[...] = dot(x[...], w[...]).astype(BF)
    flush(proj)
    jobs = [
        (slice(slot * sz.group, (slot + 1) * sz.group), bias[...], slot)
        for slot in range(sz.own_feats)
    ]
    for piece in range(PIECES):
        attend(proj, piece, jobs, probs, mixed)
    to_chunks(sz, dot(mixed[...], w_out[...]), back)


def feature_kernel(sz, layer_at, member, lengths, state, gains, shifts, out_bias, *rest):
    n, parts = sz.tensor, unit_parts(sz)
    chunks, weights = rest[:n], rest[n : n + parts]
    state_1, state_2, normed_m, proj, mixed, probs = rest[n + parts : n + parts + 6]
    strips, wide, normed, w, w_out, sems = rest[n + parts + 6 :]
    tensor_at, core, z = places(sz)
    copies = load_unit(sz, layer_at, member, weights, w, w_out, sems, core)
    bring_back(sz, tensor_at, chunks, strips)
    at = slice(layer_at, layer_at + 1)

    def before(rows, kept):
        value = state[rows, :].astype(F32) + get_strips(strips, rows) + out_bias[0, at, :]
        state_1[rows, :] = value
        xhat, unused = normal_rows(value)
        normed[rows, :] = (xhat * gains[1, at, :] + shifts[1, at, :]).astype(BF)
        return kept

    over_rows(sz.rows, before)
    biases = [feature_bias(sz, lengths[block]) for block in range(sz.blocks)]
    jobs = [
        (slice(tile * TILE, (tile + 1) * TILE), biases[tile * TILE // sz.block_rows], tile)
        for tile in range(sz.rows // TILE)
    ]
    finish(copies)
    flush(state_1)
    proj[...] = dot(normed[...], w[...]).astype(BF)
    flush(proj)
    for piece in range(PIECES):
        attend(proj, piece, jobs, probs, mixed)
    wide[...] = dot(mixed[...], w_out[...])

    def after(rows, kept):
        value = state_1[rows, :] + wide[rows, :] + out_bias[1, at, :]
        state_2[rows, :] = value
        xhat, unused = normal_rows(value)
        normed_m[rows, :] = (xhat * gains[2, at, :] + shifts[2, at, :]).astype(BF)
        return kept

    over_rows(sz.rows, after)


def up_bias_rows(sz, tensor_at, piece):
    return (tensor_at ^ piece) if sz.fast else piece


def mlp_kernel(sz, layer_at, state_2, normed_m, up_bias, gains, shifts, out_bias, *rest):
    n = sz.tensor
    parts = 8 if sz.fast else 2
    weights, (state_3, *chunks) = rest[:parts], rest[parts : parts + 1 + n]
    strips, wide, hidden, up, down, sems = rest[parts + 1 + n :]
    tensor_at, core, z = places(sz)
    finish(load_mlp(sz, layer_at, weights, up, down, sems, core))
    width = sz.width
    for piece in range(PIECES):
        lanes = slice(piece * width, (piece + 1) * width)
        wide[...] = dot(normed_m[...], up[:, lanes])
        shift = up_bias[layer_at, pl.ds(up_bias_rows(sz, tensor_at, piece), 1), :]
        value = wide[...] + shift
        half = 0.5 + 0.5 * jnp.tanh(value * (TANH_A + TANH_A * TANH_B * (value * value)))
        hidden[:, lanes] = (value * half).astype(BF)
    wide[...] = dot(hidden[...], down[...])
    at = slice(layer_at, layer_at + 1)
    later = slice(layer_at + 1, layer_at + 2)

    def after(rows, kept):
        value = state_2[rows, :] + wide[rows, :] + out_bias[2, at, :]
        state_3[rows, :] = value
        xhat, unused = normal_rows(value)
        put_strips(strips, rows, xhat * gains[0, later, :] + shifts[0, later, :])
        return kept

    over_rows(sz.rows, after)
    spread_out(sz, tensor_at, strips, chunks)


def mlp_back(
    sz, layer_at, grad, state_2, normed_m, up_bias, gains, up, down, low, wide, other, hidden,
    up_grad, grads, grad_out, outs, small,
):
    tensor_at, core, z = places(sz)
    at = slice(layer_at, layer_at + 1)
    width = sz.width
    nothing = jnp.zeros((8, width), F32)

    def lower(rows, kept):
        part = grad[rows, :].astype(BF)
        low[rows, :] = part
        return kept + fold(part.astype(F32))

    small[...] = jnp.zeros_like(small)
    small[2:3, :] = total(over_rows(sz.rows, lower, nothing))
    for piece in range(PIECES):
        lanes = slice(piece * width, (piece + 1) * width)
        name = up_bias_rows(sz, tensor_at, piece)
        wide[...] = dot(normed_m[...], up[:, lanes])
        other[...] = dot_nt(low[...], down[lanes, :])
        shift = up_bias[layer_at, pl.ds(name, 1), :]
        value = wide[...] + shift
        square = value * value
        half = 0.5 + 0.5 * jnp.tanh(value * (TANH_A + TANH_A * TANH_B * square))
        full = value * half
        hidden[:, lanes] = full.astype(BF)
        slope = half + full * (1.0 - half) * (2.0 * TANH_A + 6.0 * TANH_A * TANH_B * square)
        part = (other[...] * slope).astype(BF)
        up_grad[:, lanes] = part
        small[pl.ds(3 + name, 1), :] = total(fold(part.astype(F32)))
        grads[...] = dot_tn(normed_m[...], up_grad[:, lanes]).astype(BF)
        put_grad(sz, grads, outs, piece, 0, core, z)
        grads[...] = dot_tn(low[...], hidden[:, lanes]).astype(BF)
        put_grad(sz, grads, outs, piece, 1, core, z)
    wide[...] = dot_nt(up_grad[...], up[...])

    def back(rows, kept):
        incoming = wide[rows, :]
        xhat, change = norm_back_rows(state_2[rows, :], incoming, gains[2, at, :])
        grad_out[rows, :] = grad[rows, :] + change
        return kept[0] + fold(incoming * xhat), kept[1] + fold(incoming)

    gain_sum, shift_sum = over_rows(sz.rows, back, (nothing, nothing))
    small[0:1, :] = total(gain_sum)
    small[1:2, :] = total(shift_sum)


def last_mlp_kernel(
    sz, layer_at, sample_lens, feature_lens, cotangent, state_2, normed_m, up_bias, gains, out_bias,
    *rest,
):
    parts, halves = unit_parts(sz), 2 if sz.fast else 1
    weights, rest = rest[:parts], rest[parts:]
    output, grad_out, small = rest[:3]
    outs = rest[3 : 3 + halves]
    grad, wide, other, low, hidden, up_grad, grads, up, down, sems = rest[3 + halves :]
    tensor_at, core, z = places(sz)
    copies = load_mlp(sz, layer_at, weights, up, down, sems, core)
    step = 64

    def live_rows(rows, kept):
        index = rows.start + lax.broadcasted_iota(jnp.int32, (step, 1), 0)
        block = index // sz.block_rows
        sample = tensor_at * sz.samples + (index // sz.feats) % sz.samples
        sample_len = jnp.zeros_like(index)
        feature_len = jnp.zeros_like(index)
        for at in range(sz.blocks):
            sample_len = jnp.where(block == at, sample_lens[at], sample_len)
            feature_len = jnp.where(block == at, feature_lens[at], feature_len)
        live = (sample < sample_len) & (index % sz.feats < feature_len)
        grad[rows, :] = jnp.where(live, cotangent[rows, :].astype(F32), 0.0)
        return kept

    over_rows(sz.rows, live_rows, 0, step)
    finish(copies)
    mlp_back(
        sz, layer_at, grad, state_2, normed_m, up_bias, gains, up, down, low, wide, other, hidden,
        up_grad, grads, grad_out, outs, small,
    )
    at = slice(layer_at, layer_at + 1)
    other[...] = dot(hidden[...], down[...])

    def after(rows, kept):
        value = state_2[rows, :] + other[rows, :] + out_bias[2, at, :]
        output[rows, :] = value.astype(BF)
        return kept

    over_rows(sz.rows, after)


def mlp_back_kernel(
    sz, layer_at, grad_in, state_3, state_2, normed_m, up_bias, gains, *rest
):
    n = sz.tensor
    parts, halves = unit_parts(sz), 2 if sz.fast else 1
    chunks, weights, rest = rest[:n], rest[n : n + parts], rest[n + parts :]
    grad_out, small = rest[:2]
    outs = rest[2 : 2 + halves]
    grad, strips, wide, other, low, hidden, up_grad, grads, up, down, sems = rest[2 + halves :]
    tensor_at, core, z = places(sz)
    copies = load_mlp(sz, layer_at, weights, up, down, sems, core)
    sample_norm_back(sz, layer_at + 1, tensor_at, grad_in, state_3, chunks, gains, strips, grad)
    finish(copies)
    mlp_back(
        sz, layer_at, grad, state_2, normed_m, up_bias, gains, up, down, low, wide, other, hidden,
        up_grad, grads, grad_out, outs, small,
    )


def sample_norm_back(sz, layer_at, tensor_at, grad_in, state, chunks, gains, strips, grad):
    bring_back(sz, tensor_at, chunks, strips)
    at = slice(layer_at, layer_at + 1)

    def back(rows, kept):
        incoming = get_strips(strips, rows)
        xhat, change = norm_back_rows(state[rows, :].astype(F32), incoming, gains[0, at, :])
        grad[rows, :] = grad_in[rows, :] + change
        return kept

    over_rows(sz.rows, back)


def last_norm_kernel(sz, grad_in, state, gains, *rest):
    chunks, (grad, strips) = rest[: sz.tensor], rest[sz.tensor :]
    tensor_at, core, z = places(sz)
    sample_norm_back(sz, 0, tensor_at, grad_in, state, chunks, gains, strips, grad)


def feature_back_kernel(sz, layer_at, member, grad, state_1, proj, probs, gains, shifts, *rest):
    n, parts = sz.tensor, unit_parts(sz)
    weights, rest = rest[:parts], rest[parts:]
    grad_out, low, proj_grad, normed, small = rest[:5]
    chunks = rest[5 : 5 + n]
    mixed_grad, strips, wide, w, w_out, sems = rest[5 + n :]
    tensor_at, core, z = places(sz)
    copies = load_unit(sz, layer_at, member, weights, w, w_out, sems, core)
    at = slice(layer_at, layer_at + 1)
    nothing = jnp.zeros((8, sz.width), F32)

    def lower(rows, kept):
        part = grad[rows, :].astype(BF)
        low[rows, :] = part
        return kept + fold(part.astype(F32))

    small[...] = jnp.zeros_like(small)
    small[2:3, :] = total(over_rows(sz.rows, lower, nothing))
    flush(low)
    finish(copies)
    mixed_grad[...] = dot_nt(low[...], w_out[...]).astype(BF)
    jobs = [(slice(tile * TILE, (tile + 1) * TILE), tile) for tile in range(sz.rows // TILE)]
    for piece in range(PIECES):
        attend_back(proj, piece, jobs, probs, mixed_grad, proj_grad)
    wide[...] = dot_nt(proj_grad[...], w[...])

    def back(rows, kept):
        incoming = wide[rows, :]
        gain = gains[1, at, :]
        xhat, change = norm_back_rows(state_1[rows, :], incoming, gain)
        value = grad[rows, :] + change
        grad_out[rows, :] = value
        put_strips(strips, rows, value)
        normed[rows, :] = (xhat * gain + shifts[1, at, :]).astype(BF)
        rounded = value.astype(BF).astype(F32)
        return (
            kept[0] + fold(incoming * xhat),
            kept[1] + fold(incoming),
            kept[2] + fold(rounded),
        )

    sums = over_rows(sz.rows, back, (nothing, nothing, nothing))
    small[0:1, :] = total(sums[0])
    small[1:2, :] = total(sums[1])
    small[3:4, :] = total(sums[2])
    spread_out(sz, tensor_at, strips, chunks)


def sample_back_kernel(sz, layer_at, member, extra, proj, probs, gains, shifts, *rest):
    n, parts = sz.tensor, unit_parts(sz)
    others, rest = rest[:extra], rest[extra:]
    chunks, rows_in, rest = rest[:n], rest[n : 2 * n], rest[2 * n :]
    weights, rest = rest[:parts], rest[parts:]
    back, low, proj_grad, small = rest[:n], rest[n], rest[n + 1], rest[n + 2]
    mixed_grad, normed, w, w_out, sems = rest[n + 3 :]
    tensor_at, core, z = places(sz)
    copies = load_unit(sz, layer_at, member, weights, w, w_out, sems, core)
    by_feature(sz, chunks, low)
    by_feature(sz, rows_in, normed)
    flush(low)
    finish(copies)
    mixed_grad[...] = dot_nt(low[...], w_out[...]).astype(BF)
    jobs = [
        (slice(slot * sz.group, (slot + 1) * sz.group), slot) for slot in range(sz.own_feats)
    ]
    for piece in range(PIECES):
        attend_back(proj, piece, jobs, probs, mixed_grad, proj_grad)
    normed_grad = dot_nt(proj_grad[...], w[...])
    to_chunks(sz, normed_grad, back)
    at = slice(layer_at, layer_at + 1)
    shift_sum = total(fold(normed_grad))
    gain_sum = total(fold(normed_grad * normed[...].astype(F32)))
    small[...] = jnp.zeros_like(small)
    first = 16 if extra else 0
    small[first : first + 1, :] = (gain_sum - shifts[0, at, :] * shift_sum) / gains[0, at, :]
    small[first + 1 : first + 2, :] = shift_sum
    for at, other in enumerate(others):
        place = at if at < 2 else at + 1
        small[8 * place : 8 * place + 8, :] = other[...]


def matrix_grad_kernel(sz, count, direct, proj_grad, low, mixed, *rest):
    halves = 2 if sz.fast else 1
    rows, outs, rest = rest[:count], rest[count : count + halves], rest[count + halves :]
    tensor_at, core, z = places(sz)
    if count == 1:
        (grads,) = rest
        (normed,) = rows
    else:
        grads, normed = rest
        by_feature(sz, rows, normed)
    qkv_grads = dot_tn(normed[...], proj_grad[...])
    out_grads = dot_tn(low[...], mixed[...])
    for piece in range(PIECES):
        lanes = slice(piece * QKV, (piece + 1) * QKV)
        grads[piece, :, :QKV] = qkv_grads[:, lanes].astype(BF)
        lanes = slice(piece * PAIR, (piece + 1) * PAIR)
        grads[piece, :, QKV:] = out_grads[:, lanes].astype(BF)
        put_grad(sz, grads.at[piece], outs, piece, 0, core, z, direct)


def shaped(shape, dtype):
    return jax.ShapeDtypeStruct(shape, dtype)


class Early:
    def __init__(self, target, held, sems):
        self.target, self.held, self.sems, self.copies = target, held, sems, []
        self.shape, self.dtype = held.shape, held.dtype

    def __getitem__(self, index):
        return self.held[index]

    def __setitem__(self, index, value):
        self.held[index] = value

    def flush(self, *index):
        source, target = self.held, self.target
        if index:
            source, target = source.at[index], target.at[index]
        copy = pltpu.make_async_copy(source, target, self.sems.at[len(self.copies)])
        copy.start()
        self.copies.append(copy)


def flush(ref, *index):
    if isinstance(ref, Early):
        ref.flush(*index)


class Job:
    def __init__(self, groups, outs, split, then):
        self.groups, self.outs, self.split, self.then = groups, outs, split, then
        self.terms = [term for group in groups for term in group]

    def scratch(self):
        shapes = [
            (count, array.shape[1], members, *array.shape[3:])
            for array, first, count, member, members in self.terms
        ]
        return [
            pltpu.VMEM(shape, term[0].dtype) for shape, term in zip(shapes, self.terms)
        ] + [pltpu.SemaphoreType.DMA((len(self.terms),))]

    def start(self, refs, scratch):
        pairs = []
        for ref, term, target in zip(refs, self.terms, scratch):
            array, first, count, member, members = term
            pairs.append((ref.at[pl.ds(first, count), :, pl.ds(member, members)], target))
        return begin(pairs, scratch[-1])

    def finish(self, copies, outs, scratch):
        finish(copies)
        at = place = 0
        for group in self.groups:
            refs = scratch[at : at + len(group)]
            at += len(group)
            lead, near, members = refs[0].shape[:3]
            for one in range(lead):
                for two in range(near):
                    for member in range(members):
                        value = refs[0][one, two, member].astype(F32)
                        for ref in refs[1:]:
                            value = value + ref[one, two, member].astype(F32)
                        out, index, lead_at = outs[0], two, one
                        if self.split == 1:
                            out, lead_at = outs[one], 0
                        elif self.split and two >= near // 2:
                            out, index = outs[1], two - near // 2
                        out[lead_at, index, place + member] = value.astype(out.dtype)
            place += members


def launch(
    kernel, name, operands, specs, outs, scratch, micros, after=(), jobs=(), early=None, through=(),
    defer=False,
):
    after, outs = list(after), list(outs)
    sums = [term[0] for job in jobs for term in job.terms]
    job_outs = [out for job in jobs for out in job.outs]
    job_scratch = [job.scratch() for job in jobs]
    count, plain = len(operands), len(scratch)
    before = count + len(sums) + len(after)
    skip = before + len(through)
    early = early or {}
    held = []
    for at, parts in early.items():
        held += [pltpu.VMEM(outs[at].shape, outs[at].dtype), pltpu.SemaphoreType.DMA((parts,))]

    def whole(*refs):
        given, results = refs[count : count + len(sums)], refs[skip : skip + len(outs)]
        extra = refs[skip + len(outs) : skip + len(outs) + len(job_outs)]
        rest = refs[skip + len(outs) + len(job_outs) + len(through) :]
        own, rest = rest[:plain], rest[plain:]
        results = list(results)
        for at in early:
            results[at] = Early(results[at], *rest[:2])
            rest = rest[2:]
        started = []
        for job, buffers in zip(jobs, job_scratch):
            mine, rest = rest[: len(buffers)], rest[len(buffers) :]
            started.append((job, mine, job.start(given[: len(job.terms)], mine)))
            given = given[len(job.terms) :]
        kernel(*refs[:count], *results, *own)
        for job, mine, copies in started:
            job.finish(copies, extra[: len(job.outs)], mine)
            extra = extra[len(job.outs) :]
        for at in early:
            finish(results[at].copies)

    results = pl.pallas_call(
        whole,
        out_shape=outs + job_outs + [shaped(v.shape, v.dtype) for v in through],
        input_output_aliases={
            before + at: len(outs) + len(job_outs) + at for at in range(len(through))
        },
        in_specs=list(specs) + [ANY] * (len(sums) + len(after) + len(through)),
        out_specs=[ANY if at in early else VMEM for at in range(len(outs))]
        + [VMEM] * len(job_outs)
        + [ANY] * len(through),
        scratch_shapes=list(scratch) + held + [buffer for buffers in job_scratch for buffer in buffers],
        name=name,
        cost_estimate=pl.CostEstimate(
            flops=int(micros * 8e9), bytes_accessed=1_000_000, transcendentals=0
        ),
        compiler_params=pltpu.CompilerParams(vmem_limit_bytes=VMEM_GRANT),
    )(*operands, *sums, *after, *through)
    results, extra = results[: len(outs)], results[len(outs) :]
    through = extra[len(job_outs) :]
    if defer:
        return list(results), list(extra[: len(job_outs)])
    for job in jobs:
        job.then(*extra[: len(job.outs)])
        extra = extra[len(job.outs) :]
    return list(results) + list(through)


def grad_shapes(sz, members):
    if sz.fast:
        return [shaped((PIECES, 4, members, 64, sz.width), BF)] * 2
    return [shaped((PIECES, members, sz.width, sz.width), BF)]


def swap_cores(sz, v):
    return lax.ppermute(v, "dp", [(at, at ^ 1) for at in range(sz.dp)])


def swap_near(sz, v, distance):
    return lax.ppermute(v, "tensor", [(at, at ^ distance) for at in range(sz.tensor)])


def swap_far(sz, v, distance):
    return lax.ppermute(v, "dp", [(at, at ^ (2 * distance)) for at in range(sz.dp)])


def swap_turn(sz, v, turn):
    pairs = []
    for dp_at in range(sz.dp):
        distance = 1 + ((dp_at + turn) % 2)
        for at in range(sz.tensor):
            base = dp_at * sz.tensor
            pairs.append((base + at, base + (at ^ distance)))
    return lax.ppermute(v, ("dp", "tensor"), pairs)


def exchange(sz, chunks):
    return [chunks[0]] + [swap_near(sz, chunks[at], at) for at in range(1, sz.tensor)]


def gather_unit(sz, half):
    first = swap_turn(sz, half, 0)
    second = swap_turn(sz, half, 1)
    third = swap_turn(sz, first, 1)
    got = [first, second, third]
    return got + [swap_cores(sz, v) for v in got]


class Reduction:
    def __init__(self, sz, *units):
        self.sz = sz
        self.units = [(mine, swap_cores(sz, theirs), mine.shape[2]) for mine, theirs in units]
        self.members = sum(unit[2] for unit in self.units)
        self.tail = units[0][0].shape[3:]

    def groups(self, first, count, extra):
        groups, place = [], 0
        for mine, other, members in self.units:
            group = [(mine, first, count, 0, members), (other, first, count, 0, members)]
            group += [(array, at, count, place, members) for array, at in extra]
            groups.append(group)
            place += members
        return groups

    def shape(self, lead, near, dtype=BF):
        return shaped((lead, near, self.members, *self.tail), dtype)

    def job(self, step):
        return getattr(self, f"step_{step}")()

    def step_1(self):
        def then(out):
            self.sent, self.far = out, swap_turn(self.sz, out, 1)

        return Job(self.groups(2, 2, []), [self.shape(2, 4)], 0, then)

    def step_2(self):
        def then(out):
            self.sent, self.near = out, swap_turn(self.sz, out, 0)

        return Job(self.groups(1, 1, [(self.far, 1)]), [self.shape(1, 4)], 0, then)

    def step_3(self):
        def then(kept, out):
            self.kept, self.got = kept, swap_far(self.sz, out, 1)

        groups = self.groups(0, 1, [(self.far, 0), (self.near, 0)])
        return Job(groups, [self.shape(1, 2)] * 2, 2, then)

    def step_4(self):
        def then(kept, out):
            self.kept, self.got = kept, swap_far(self.sz, out, 2)

        groups = [[(array, 0, 1, 0, self.members) for array in (self.kept, self.got)]]
        return Job(groups, [self.shape(1, 1, F32), self.shape(1, 1)], 2, then)

    def result(self):
        return (self.kept + self.got.astype(F32)).reshape(self.members, *self.tail)


class Direct:
    def __init__(self, sz, mine, theirs):
        self.sz, self.mine, self.theirs = sz, mine, theirs

    def job(self, step):
        def then(*sent):
            self.sent = sent

        group = [(array, 1, 3, 0, 1) for array in (self.mine, self.other)]
        shape = shaped((1, *self.mine.shape[1:]), BF)
        return Job([group], [shape] * 3, 1, then)


def join(sz, *parts):
    one = object.__new__(Reduction)
    one.sz, one.tail = sz, (64, sz.width)
    plain = [not isinstance(part, Reduction) for part in parts]
    one.members = sum(p.shape[2] if alone else p.members for p, alone in zip(parts, plain))

    def step_3():
        def then(kept, out):
            one.kept, one.sent = kept, out

        groups = []
        for part, alone in zip(parts, plain):
            if alone:
                groups.append([(part, 0, 1, 0, part.shape[2])])
            else:
                groups += part.groups(0, 1, [(part.far, 0), (part.near, 0)])
        return Job(groups, [one.shape(1, 2)] * 2, 2, then)

    one.step_3 = step_3
    return one


def region(flag, fn, *args):
    def nothing(*unused):
        return jax.tree.map(lambda v: jnp.zeros(v.shape, v.dtype), jax.eval_shape(fn, *args))

    return lax.cond(flag, fn, nothing, *args)


def reduce_whole(sz, full):
    members, width = full.shape[1], full.shape[2]
    full = full.transpose(1, 2, 0, 3)
    part = lax.psum_scatter(full, "dp", scatter_dimension=1, tiled=True)
    return lax.psum(part, "tensor").astype(F32)


def gathered_unit(qkv, out):
    qkv = lax.all_gather(qkv, "tensor", axis=2, tiled=True)
    out = lax.all_gather(out, "tensor", axis=0, tiled=True)
    width = qkv.shape[1]
    qkv = qkv.reshape(3, width, PIECES, PAIR).transpose(1, 2, 0, 3)
    return [qkv.reshape(width, PIECES * QKV), out]


def body(
    tokens,
    cotangent,
    block_task,
    sample_len,
    feature_len,
    norm_gain,
    norm_shift,
    sample_qkv,
    sample_out,
    feature_qkv,
    feature_out,
    out_bias,
    up_weight,
    up_bias,
    down_weight,
):
    shape = tokens.shape
    sz = Sizes(shape, lax.axis_size("tensor"), lax.axis_size("dp"))
    rows, width, n = sz.rows, sz.width, sz.tensor
    tokens = tokens.reshape(rows, width)
    cotangent = cotangent.reshape(rows, width)
    gains, shifts, biases = (
        jnp.transpose(v, (1, 0, 2)) for v in (norm_gain, norm_shift, out_bias)
    )
    up_rows = up_bias.reshape(L, PIECES, -1)
    qkvs = [jnp.transpose(v, (0, 2, 1, 3)) for v in (sample_qkv, feature_qkv)]
    outs = [sample_out, feature_out]
    part = functools.partial
    wide = pltpu.VMEM((rows, width), F32)
    strips = pltpu.VMEM((width // TILE, rows + sz.feats, TILE), F32)
    slim = pltpu.VMEM((rows, width), BF)
    dma = pltpu.SemaphoreType.DMA
    row_f32 = shaped((rows, width), F32)
    row_bf = shaped((rows, width), BF)
    chunk_shapes = [shaped((sz.chunk, width), BF)] * n
    proj_shape = shaped((rows, PIECES * QKV), BF)
    small_shape = shaped((8, width), F32)
    half_unit = (width // 2, width)
    sends = [shaped(half_unit, BF)] if sz.fast else []

    sent = []
    if sz.fast:
        sent = launch(
            part(pack_first_kernel, sz), "pack_first", (qkvs[0], outs[0]), [ANY] * 2, sends,
            [dma((5,))], 0.2,
        )
    chunks = launch(
        part(start_kernel, sz), "start", (tokens, gains, shifts), [VMEM] * 3, chunk_shapes,
        [strips], 3, sent,
    )
    sent = sent[0] if sz.fast else None

    units = [[None, None] for _ in range(L)]
    members = [[None, None]] + [[0, 1]] * (L - 1)
    mlps = [None] * L
    if sz.fast:

        def pack_mlp(layer_at, after):
            return launch(
                part(pack_mlp_kernel, sz, layer_at), f"pack_mlp_{layer_at}",
                [up_weight, down_weight], [ANY] * 2, [shaped((2, *half_unit), BF)], [dma((2,))],
                2, after,
            )[0]

        got = gather_unit(sz, sent)
        units[0][0] = [qkvs[0], outs[0]] + got
    else:
        for layer_at in range(L):
            for kind in range(2):
                units[layer_at][kind] = gathered_unit(qkvs[kind][layer_at], outs[kind][layer_at])
            up = lax.all_gather(up_weight[layer_at], "tensor", axis=1, tiled=True)
            down = lax.all_gather(down_weight[layer_at], "tensor", axis=0, tiled=True)
            mlps[layer_at] = [up, down]

    def gather_units(layer_at, kinds, sent):
        got = gather_unit(sz, sent)
        for kind in kinds:
            units[layer_at][kind] = [qkvs[kind], outs[kind]] + got

    def gather_mlp(layer_at, sent):
        mlps[layer_at] = [up_weight, down_weight] + gather_unit(sz, sent)

    def arrived(parts, count):
        return parts[2 : 2 + count] if sz.fast else []

    unit_specs = [ANY] * unit_parts(sz)
    mlp_specs = [ANY] * unit_parts(sz)
    unit_scratch = [
        pltpu.VMEM((width, PIECES * QKV), BF),
        pltpu.VMEM((width, width), BF),
        dma((22 if sz.fast else 2,)),
    ]
    mlp_scratch = [
        pltpu.VMEM((width, PIECES * width), BF),
        pltpu.VMEM((PIECES * width, width), BF),
        dma((14 if sz.fast else 2,)),
    ]
    hidden = pltpu.VMEM((rows, PIECES * width), BF)
    square = pltpu.VMEM((width, width), BF)

    state = tokens
    kept = []
    for layer_at in range(L):
        entry = state
        got = exchange(sz, chunks)
        slots = sz.own_feats
        began = []
        if sz.fast and layer_at == 0:
            half_mlp, half_units = shaped((2, *half_unit), BF), shaped((2, *half_unit), BF)
            sent, sent_mlp, *waiting = launch(
                part(pack_early_kernel, sz), "pack_early",
                (qkvs[0], outs[0], qkvs[1], outs[1], up_weight, down_weight), [ANY] * 6,
                [shaped(half_unit, BF), half_mlp, half_units], [dma((17,))], 2,
                got[1:] + arrived(units[0][0], 2),
            )
            gather_units(0, (1,), sent)
            gather_mlp(0, sent_mlp)
            began = [sent, sent_mlp]
        elif sz.fast:
            sent = pack_mlp(layer_at, got[1:] + arrived(units[layer_at][0], 2))
            gather_mlp(layer_at, sent)
            began = [sent]
        *back, proj_s, mixed_s, probs_s = launch(
            part(sample_kernel, sz, layer_at, members[layer_at][0]), f"sample_{layer_at}",
            (block_task, sample_len, *got, *units[layer_at][0]),
            [SMEM] * 2 + [VMEM] * n + unit_specs,
            chunk_shapes
            + [proj_shape, row_bf, shaped((PIECES, slots, 2, sz.group, sz.group), BF)],
            [slim, pltpu.VMEM((sz.group, sz.group), F32), *unit_scratch],
            8, began, early={n: 1, n + 1: PIECES, n + 2: PIECES},
        )
        back = exchange(sz, back)
        tiles = rows // TILE
        passed = waiting if sz.fast and layer_at < L - 1 else []
        state_1, state_2, normed_m, proj_f, mixed_f, probs_f, *passed = launch(
            part(feature_kernel, sz, layer_at, members[layer_at][1]), f"feature_{layer_at}",
            (feature_len, state, gains, shifts, biases, *back, *units[layer_at][1]),
            [SMEM] + [VMEM] * (4 + n) + unit_specs,
            [row_f32, row_f32, row_bf, proj_shape, row_bf,
             shaped((PIECES, tiles, 2, TILE, TILE), BF)],
            [strips, wide, slim, *unit_scratch],
            9, through=passed,
        )
        if layer_at < L - 1:
            if sz.fast:
                gather_units(layer_at + 1, (0, 1), passed[0])
            state, *chunks = launch(
                part(mlp_kernel, sz, layer_at), f"mlp_{layer_at}",
                (state_2, normed_m, up_rows, gains, shifts, biases, *mlps[layer_at]),
                [VMEM] * 6 + mlp_specs,
                [row_f32] + chunk_shapes,
                [strips, wide, hidden, *mlp_scratch],
                9,
            )
        kept.append((entry, got, proj_s, mixed_s, probs_s, state_1, state_2, normed_m,
                     proj_f, mixed_f, probs_f))

    reductions, whole, done = {}, {}, {}

    def reduction(layer_at, kind, parts):
        if sz.fast and layer_at == 0 and kind < 2:
            reductions[layer_at, kind] = Direct(sz, *parts)
        elif sz.fast:
            reductions[layer_at, kind] = Reduction(sz, parts)
        else:
            (whole[layer_at, kind],) = parts

    def jobs(*steps):
        return [reductions[at[:2]].job(at[2]) for at in steps if at[:2] in reductions]

    def add_up(name, after, *steps, through=()):
        todo = jobs(*steps)
        if not todo:
            return []
        return launch(
            part(nothing_kernel, sz), name, [], [], [], [], 0.05, after, todo, through=through
        )

    smalls = [None] * L

    def small_rows():
        return jnp.concatenate([one for layer in smalls for one in layer], axis=0)

    for layer_at in reversed(range(L)):
        (entry, got, proj_s, mixed_s, probs_s, state_1, state_2, normed_m,
         proj_f, mixed_f, probs_f) = kept[layer_at]
        above = layer_at + 1
        if layer_at == L - 1:
            output, grad, small_m, *parts = launch(
                part(last_mlp_kernel, sz, layer_at), f"last_mlp_{layer_at}",
                (sample_len, feature_len, cotangent, state_2, normed_m, up_rows, gains, biases,
                 *mlps[layer_at]),
                [SMEM] * 2 + [VMEM] * 6 + mlp_specs,
                [row_bf, row_f32, small_shape] + grad_shapes(sz, 2),
                [wide, wide, wide, slim, hidden, hidden, square, *mlp_scratch],
                15,
            )
        else:
            grad, small_m, *parts = launch(
                part(mlp_back_kernel, sz, layer_at), f"mlp_back_{layer_at}",
                (grad, kept[above][0], state_2, normed_m, up_rows, gains, *back,
                 *mlps[layer_at]),
                [VMEM] * (6 + n) + mlp_specs,
                [row_f32, small_shape] + grad_shapes(sz, 2),
                [wide, strips, wide, wide, slim, hidden, hidden, square, *mlp_scratch],
                15, parts[:1], early={2: 2 * PIECES, 3: 2 * PIECES} if sz.fast else None,
            )
        reduction(layer_at, 2, parts)
        began = []
        if layer_at < L - 1 and sz.fast:
            add_up(f"sums_{layer_at}", [grad], (above, 2, 3), (above, 1, 2), (above, 0, 1))
            began = [reductions[above, 1].sent, reductions[above, 0].sent]
        grad, low, proj_grad, normed, small_f, *chunks = launch(
            part(feature_back_kernel, sz, layer_at, members[layer_at][1]),
            f"feature_back_{layer_at}",
            (grad, state_1, proj_f, probs_f, gains, shifts, *units[layer_at][1]),
            [VMEM] * 6 + unit_specs,
            [row_f32, row_bf, proj_shape, row_bf, small_shape] + chunk_shapes,
            [slim, strips, wide, *unit_scratch],
            9, began,
        )
        smalls[layer_at] = [small_m, small_f]
        chunks = exchange(sz, chunks)
        parts = launch(
            part(matrix_grad_kernel, sz, 1, layer_at == 0), f"feature_matrix_{layer_at}",
            (proj_grad, low, mixed_f, normed), [VMEM] * 4, grad_shapes(sz, 1),
            [pltpu.VMEM((PIECES, width, width), BF)], 0.7,
            jobs=jobs((layer_at, 2, 1), (above, 0, 2), (above, 2, 4)),
        )
        reduction(layer_at, 1, parts)
        others = []
        if layer_at == 0 and sz.fast:
            others = [one for layer in smalls for one in layer]
        *back, low, proj_grad, small_s = launch(
            part(sample_back_kernel, sz, layer_at, members[layer_at][0], len(others)),
            f"sample_back_{layer_at}",
            (proj_s, probs_s, gains, shifts, *others, *chunks, *got, *units[layer_at][0]),
            [VMEM] * (4 + len(others) + 2 * n) + unit_specs,
            chunk_shapes + [row_bf, proj_shape, shaped((24 * L, width), F32) if others else small_shape],
            [slim, slim, *unit_scratch],
            9, parts[:1],
        )
        smalls[layer_at].append(small_s)
        began = []
        if not sz.fast or layer_at > 0:
            back = exchange(sz, back)
        if sz.fast and layer_at == 0:
            reductions[1, 3] = upper = join(sz, reductions[1, 1], reductions[1, 0])
            began = [reductions[1, 2].got, reductions[1, 1].near, reductions[1, 0].near]
            rows_small = small_s
            reductions[0, 1].other = swap_cores(sz, reductions[0, 1].theirs)
        parts = launch(
            part(matrix_grad_kernel, sz, n, layer_at == 0), f"sample_matrix_{layer_at}",
            (proj_grad, low, mixed_s, *got), [VMEM] * (3 + n), grad_shapes(sz, 1),
            [pltpu.VMEM((PIECES, width, width), BF), slim], 0.7, began,
            jobs((layer_at, 1, 1), *(((layer_at, 2, 2),) if layer_at else ((1, 3, 3),))),
        )
        reduction(layer_at, 0, parts)
    def last_norm(back):
        (tokens_grad,) = launch(
            part(last_norm_kernel, sz), "last_norm", (grad, tokens, gains, *back),
            [VMEM] * (3 + n), [row_f32], [strips], 5,
        )
        return tokens_grad

    if sz.fast:
        first, last = reductions[0, 1], reductions[0, 0]
        block = shaped((16 * L, width), F32)
        mlp = reductions[0, 2]

        def near_region(pieces, mine, theirs, rows_own):
            got = [swap_near(sz, v, at + 1) for at, v in enumerate(pieces)]
            other, rows_other = swap_cores(sz, theirs), swap_cores(sz, rows_own)
            results, (mlp_sent,) = launch(
                part(send_near_kernel, sz), "send_near", (mine, other, rows_own, rows_other),
                [VMEM] * 4, [shaped((256 + 16 * L, width), BF)] * 3 + [block], [], 5, [],
                [mlp.job(2)], defer=True,
            )
            return got, other, results, mlp_sent

        upper.got = swap_far(sz, upper.sent, 1)
        first.got, last.other, (*sent, rows_kept), mlp_sent = region(
            sample_len[0] > 0, near_region, first.sent, last.mine, last.theirs, rows_small
        )
        mlp.near = swap_turn(sz, mlp_sent, 0)
        last.got = [swap_near(sz, v, at + 1) for at, v in enumerate(sent)]
        add_up("sums_upper", [rows_kept], (1, 3, 4))
        back = add_up("sums_mlp", [rows_kept, upper.kept], (0, 2, 3), through=back)
        attention_kept, rows_kept, *sent = launch(
            part(send_far_kernel, sz), "send_far",
            (first.mine, first.other, *first.got, last.mine, last.other, *last.got, rows_kept),
            [ANY] * 2 + [VMEM] * 3 + [ANY] * 2 + [VMEM] * 4,
            [shaped((2, 64, width), F32), block] + [shaped((128 + 16 * L, width), BF)] * 3,
            [pltpu.VMEM((4, 1, 64, width), BF)] * 4 + [dma((4,))], 0.05, [mlp.kept, upper.got],
        )
        add_up("sums_late", [rows_kept], (0, 2, 4))
        got = [swap_far(sz, v, at + 1) for at, v in enumerate(sent)]
        tokens_grad = last_norm(exchange(sz, back))
        upper_mlp = reductions[1, 2]
        qkv_shape, out_shape = shaped((L, 3, 64, PAIR), F32), shaped((L, 64, PAIR), F32)
        wide_shape, row_shape = shaped((L, 64, width), F32), shaped((3, L, width), F32)
        (s_qkv, s_out, f_qkv, f_out, up, down, gain_total, shift_total, bias_total,
         up_bias_total) = launch(
            part(last_sums_kernel, sz), "last_sums",
            (attention_kept, rows_kept, *got, mlp.kept, mlp.got, upper_mlp.kept, upper_mlp.got,
             upper.kept, upper.got), [VMEM] * 11,
            [qkv_shape, out_shape, qkv_shape, out_shape, wide_shape, wide_shape,
             row_shape, row_shape, row_shape, shaped((L, PIECES * width), F32)], [], 0.05,
        )

        def turned(v):
            return jnp.transpose(v, (0, 2, 1))

        gain_total, shift_total, bias_total = (
            jnp.transpose(v, (1, 0, 2)) for v in (gain_total, shift_total, bias_total)
        )
        return (
            output.reshape(shape), tokens_grad.reshape(shape), gain_total, shift_total,
            jnp.transpose(s_qkv, (0, 2, 1, 3)), turned(s_out),
            jnp.transpose(f_qkv, (0, 2, 1, 3)), turned(f_out),
            bias_total, up, up_bias_total, turned(down),
        )
    tokens_grad = last_norm(back)
    early = lax.psum(small_rows(), ("dp", "tensor"))
    early = early.reshape(-1, 8, width)
    by_layer = []
    at = 0
    for layer_at in range(L):
        count = len(smalls[layer_at])
        sums = [early[at + member] for member in range(count)]
        at += count
        by_layer.append(sums)
    gain_total, shift_total = (
        jnp.stack([jnp.stack([s[row], f[row], m[row]]) for m, f, s in by_layer])
        for row in range(2)
    )
    bias_total = jnp.stack([jnp.stack([f[3], f[2], m[2]]) for m, f, s in by_layer])
    up_bias_total = jnp.stack([m[3 : 3 + PIECES].reshape(-1) for m, f, s in by_layer])

    if not sz.fast:
        for key, full in whole.items():
            done[key] = reduce_whole(sz, full)

    def attention_grads(kind):
        qkv, out = [], []
        for layer_at in range(L):
            if sz.fast:
                value = done[layer_at, kind][0]
                qkv.append(value[:, :QKV].reshape(-1, 3, PAIR))
                out.append(value[:, QKV:].T)
            else:
                value = done[layer_at, kind][0]
                columns = width // n
                start = lax.axis_index("tensor") * columns
                whole = value[:, :, :QKV].reshape(-1, PIECES, 3, PAIR).transpose(0, 2, 1, 3)
                whole = whole.reshape(-1, 3, width)
                qkv.append(lax.dynamic_slice_in_dim(whole, start, columns, 2))
                whole = value[:, :, QKV:].reshape(-1, width)
                out.append(lax.dynamic_slice_in_dim(whole, start, columns, 1).T)
        return jnp.stack(qkv), jnp.stack(out)

    sample_qkv_grad, sample_out_grad = attention_grads(0)
    feature_qkv_grad, feature_out_grad = attention_grads(1)
    ups, downs = [], []
    for layer_at in range(L):
        value = done[layer_at, 2]
        if not sz.fast:
            columns = PIECES * width // n
            start = lax.axis_index("tensor") * columns
            value = value.reshape(2, -1, PIECES * width)
            value = lax.dynamic_slice_in_dim(value, start, columns, 2)
        ups.append(value[0])
        downs.append(value[1].T)
    return (
        output.reshape(shape),
        tokens_grad.reshape(shape),
        gain_total,
        shift_total,
        sample_qkv_grad,
        sample_out_grad,
        feature_qkv_grad,
        feature_out_grad,
        bias_total,
        jnp.stack(ups),
        up_bias_total,
        jnp.stack(downs),
    )


def solution(mesh):
    placed = (
        P("dp", "tensor", None, None),
        P("dp", "tensor", None, None),
        P("dp"),
        P("dp"),
        P("dp"),
        P(),
        P(),
        P(None, None, None, "tensor"),
        P(None, "tensor", None),
        P(None, None, None, "tensor"),
        P(None, "tensor", None),
        P(),
        P(None, None, "tensor"),
        P(),
        P(None, "tensor", None),
    )
    return jax.shard_map(
        body,
        mesh=mesh,
        in_specs=placed,
        out_specs=(
            P("dp", "tensor", None, None),
            P("dp", "tensor", None, None),
            P(),
            P(),
            P(None, "dp", None, "tensor"),
            P(None, "tensor", "dp"),
            P(None, "dp", None, "tensor"),
            P(None, "tensor", "dp"),
            P(),
            P(None, "dp", "tensor"),
            P(),
            P(None, "tensor", "dp"),
        ),
        check_vma=False,
    )
```
